32 devices in a mesh: dp: 8 (over z, x), tensor: 4 (over y, core).
Axes of the slice: x: 2, y: 2, z: 4, core: 2. Of those that a mesh axis runs over, the one named last changes fastest.
Arguments:
- tokens: bfloat16 [32768, 1536], P(('dp', 'tensor')), may hold values from -6 to 6
- lengths: int32 [8, 4], P('dp'), may hold values from 0 to 4096, as said below
- norm_gain: float32 [1536], replicated, may hold values from 0.1 to 1.9
- w_gate: bfloat16 [1536, 3072], P(None, 'tensor'), may hold values from -0.15625 to 0.15625
- w_value: bfloat16 [1536, 3072], P(None, 'tensor'), may hold values from -0.15625 to 0.15625
- w_shared: bfloat16 [1536, 256], replicated, may hold values from -0.15625 to 0.15625
- w_rate: bfloat16 [1536, 48], P(None, 'tensor'), may hold values from -0.15625 to 0.15625
- conv_value: float32 [3072, 4], P('tensor'), may hold values from -0.5 to 0.5
- value_bias: float32 [3072], P('tensor'), may hold values from -0.5 to 0.5
- conv_shared: float32 [256, 4], replicated, may hold values from -0.5 to 0.5
- shared_bias: float32 [256], replicated, may hold values from -0.5 to 0.5
- rate_bias: float32 [48], P('tensor'), may hold values from -6.9 to -2.3
- decay_log: float32 [48], P('tensor'), may hold values from 0 to 2.77
- skip_gain: float32 [48], P('tensor'), may hold values from 0.25 to 3.75, as said below
- mix_gain: float32 [3072], P('tensor'), may hold values from 0.1 to 1.9
- w_out: bfloat16 [3072, 1536], P('tensor'), may hold values from -0.109375 to 0.109375
- cotangent: bfloat16 [32768, 1536], P(('dp', 'tensor')), may hold values from -6 to 6
Outputs:
- block_out: bfloat16 [32768, 1536], P(('dp', 'tensor'))
- tokens_grad: float32 [32768, 1536], P(('dp', 'tensor'))
- norm_gain_grad: float32 [1536], replicated
- w_gate_grad: float32 [1536, 3072], P('dp', 'tensor')
- w_value_grad: float32 [1536, 3072], P('dp', 'tensor')
- w_shared_grad: float32 [1536, 256], replicated
- w_rate_grad: float32 [1536, 48], P('dp', 'tensor')
- conv_value_grad: float32 [3072, 4], P('tensor')
- value_bias_grad: float32 [3072], P('tensor')
- conv_shared_grad: float32 [256, 4], replicated
- shared_bias_grad: float32 [256], replicated
- rate_bias_grad: float32 [48], P('tensor')
- decay_log_grad: float32 [48], P('tensor')
- skip_gain_grad: float32 [48], P('tensor')
- mix_gain_grad: float32 [3072], P('tensor')
- w_out_grad: float32 [3072, 1536], P('tensor', 'dp')
The draws below stay inside these ranges and needn't reach their ends.
Inputs may be any that keep to these rules, and one draw needn't show every extreme that they name: Each row lists its sequences' lengths from the first slot; each used entry is 1024 or more and the unused entries are 0 at the end; a row's lengths sum to more than half of 4096 and to 4096 at most; some row holds one sequence of exactly 4096. `skip_gain`: Positive.
All inputs are finite; a program needn't handle non-finite values.
Results may differ from the reference program's by a relative error of at most 0.0079.
Values may be sent and summed in bfloat16 or wider, within the bound.
No kernel may reach another device: no remote copies, remote signals or barrier semaphores. Data moves between devices by JAX's collectives and lax.ppermute only.
A program may use at most 320 MiB of HBM per device.

```python
from functools import partial
import jax
import jax.numpy as jnp
from jax import lax

D = 1536
HEADS = 48
STATE = 128
CONV = 4
GROUP = 256
SLOTS = 4096
MIN_LEN = 1024
INNER = 3072
MAX_SEQS = 4
TOKENS = 32768


def draw_lengths(key, part):
    key = jax.random.fold_in(key, 11)
    row_count = TOKENS // SLOTS
    key_count, key_total, key_cuts, key_pick = jax.random.split(key, 4)
    counts = jax.random.randint(key_count, (row_count,), 1, MAX_SEQS + 1)
    lowest = jnp.maximum(SLOTS // 2 + 1, MIN_LEN * counts)
    span_total = SLOTS - lowest + 1
    totals = lowest + jax.random.randint(key_total, (row_count,), 0, 1 << 20) % span_total
    forced = jax.random.randint(key_pick, (), 0, row_count)
    is_forced = jnp.arange(row_count) == forced
    counts = jnp.where(is_forced, 1, counts)
    totals = jnp.where(is_forced, SLOTS, totals)
    extra = totals - MIN_LEN * counts
    cuts = jax.random.randint(key_cuts, (row_count, MAX_SEQS - 1), 0, 1 << 20) % (extra[:, None] + 1)
    cuts = jnp.sort(cuts, axis=1)
    index = jnp.arange(MAX_SEQS - 1)
    cuts = jnp.where(index[None, :] < counts[:, None] - 1, cuts, extra[:, None])
    bounds = jnp.concatenate([jnp.zeros((row_count, 1), jnp.int32), cuts.astype(jnp.int32), extra[:, None].astype(jnp.int32)], axis=1)
    pieces = bounds[:, 1:] - bounds[:, :-1]
    places = jnp.arange(MAX_SEQS)
    return jnp.where(places[None, :] < counts[:, None], MIN_LEN + pieces, 0).astype(jnp.int32)


def draw_skip_gain(key, part):
    key = jax.random.fold_in(key, 23)
    heads_index = jnp.arange(HEADS).astype(jnp.float32)
    base = jax.random.uniform(key, (HEADS,), jnp.float32, 0.5, 1.5)
    return base * (0.5 + 2.0 * heads_index / HEADS)


def levels(own_key, extent, cuts, least, largest):
    level, own = 1.0, jax.random.fold_in(own_key, 6)
    for dim, parts in cuts:
        steps = jnp.exp(jax.random.uniform(jax.random.fold_in(own, dim), (parts,), jnp.float32, least / len(cuts), largest / len(cuts)))
        level = level * jnp.repeat(steps, extent[dim] // parts).reshape([-1 if axis == dim else 1 for axis in range(len(extent))])
    return level


def scatter_about(rng, shape, scale, limit, cuts=(), kind=jnp.bfloat16):
    values = jax.random.normal(rng, shape, jnp.float32) * scale
    if len(cuts) > 0:
        values = levels(rng, shape, cuts, -0.22, 0.18) * values
    return jnp.clip(values, min=-limit, max=limit).astype(kind)


def setup_inputs(seed: int = 0) -> dict:
    streams_of = jax.random.split(jax.random.key(seed), 18)
    tokens = scatter_about(streams_of[0], (TOKENS, D), 1.0, 6.0, ((0, 32),))
    lengths = draw_lengths(jax.random.fold_in(streams_of[17], 71), 0)
    norm_gain = jnp.clip(1.0 + 0.18 * jax.random.normal(streams_of[2], (D,), jnp.float32), 0.1, 1.9)
    w_gate = scatter_about(streams_of[3], (D, INNER), D ** -0.5, 0.15625, ((1, 4),))
    w_value = scatter_about(streams_of[4], (D, INNER), D ** -0.5, 0.15625, ((1, 4),))
    w_shared = scatter_about(streams_of[5], (D, 2 * STATE), D ** -0.5, 0.15625)
    w_rate = scatter_about(streams_of[6], (D, HEADS), D ** -0.5, 0.15625, ((1, 4),))
    conv_value = jnp.clip(jax.random.uniform(streams_of[7], (INNER, CONV), jnp.float32, -0.5, 0.5) * levels(streams_of[7], (INNER, CONV), ((0, 4),), -0.4, 0.0), -0.5, 0.5)
    value_bias = jnp.clip(jax.random.uniform(streams_of[8], (INNER,), jnp.float32, -0.5, 0.5) * levels(streams_of[8], (INNER,), ((0, 4),), -0.4, 0.0), -0.5, 0.5)
    conv_shared = jnp.clip(jax.random.uniform(streams_of[9], (2 * STATE, CONV), jnp.float32, -0.5, 0.5), -0.5, 0.5)
    shared_bias = jnp.clip(jax.random.uniform(streams_of[10], (2 * STATE,), jnp.float32, -0.5, 0.5), -0.5, 0.5)
    rate_bias = jnp.clip(-6.9 + 4.6000001430511475 * jax.random.uniform(streams_of[11], (HEADS,), jnp.float32) ** levels(streams_of[11], (HEADS,), ((0, 4),), -0.2, 0.2), -6.9, -2.3)
    decay_log = jnp.clip(2.77 * jax.random.uniform(streams_of[12], (HEADS,), jnp.float32) ** levels(streams_of[12], (HEADS,), ((0, 4),), -0.2, 0.2), 0.0, 2.77)
    skip_gain = draw_skip_gain(jax.random.fold_in(streams_of[17], 71), 0)
    mix_gain = jnp.clip(1.0 + 0.18 * jax.random.normal(streams_of[14], (INNER,), jnp.float32), 0.1, 1.9)
    w_out = scatter_about(streams_of[15], (INNER, D), INNER ** -0.5, 0.109375, ((0, 4),))
    cotangent = scatter_about(streams_of[16], (TOKENS, D), 1.0, 6.0, ((0, 32),))
    return dict(tokens=tokens, lengths=lengths, norm_gain=norm_gain, w_gate=w_gate, w_value=w_value, w_shared=w_shared, w_rate=w_rate, conv_value=conv_value, value_bias=value_bias, conv_shared=conv_shared, shared_bias=shared_bias, rate_bias=rate_bias, decay_log=decay_log, skip_gain=skip_gain, mix_gain=mix_gain, w_out=w_out, cotangent=cotangent)


EPS = 1e-05
HIGH = lax.Precision.HIGHEST

@jax.custom_vjp
def low(v):
    return lax.optimization_barrier(v.astype(jnp.bfloat16)).astype(jnp.float32)

@jax.custom_vjp
def low_back(v):
    return v

def low_keep(v):
    return (low(v), None)

def low_pass(kept, grad):
    return (grad,)

def back_keep(v):
    return (v, None)

def back_low(kept, grad):
    return (low(grad),)
low.defvjp(low_keep, low_pass)
low_back.defvjp(back_keep, back_low)

def segments_of(lengths_row, position_count):
    ends = jnp.cumsum(lengths_row).astype(jnp.int32)
    position = jnp.arange(position_count, dtype=jnp.int32)
    segment = lax.optimization_barrier(jnp.sum((position[:, None] >= ends[None, :]).astype(jnp.int32), axis=1)).astype(jnp.int32)
    validity = (position < ends[-1]).astype(jnp.float32)
    return (segment, validity)

def causal_conv(values, weight, offset_bias, segment):
    position_count = values.shape[0]
    taps = weight.shape[1]
    running = values * weight[:, taps - 1] + offset_bias
    for offset in range(1, taps):
        earlier = jnp.pad(values, ((offset, 0), (0, 0)))[:position_count]
        before = jnp.pad(segment, (offset, 0), constant_values=-1)[:position_count]
        running = running + jnp.where((before == segment)[:, None], earlier, 0.0) * weight[:, taps - 1 - offset]
    return running

def group_step(carried, block, decay_rate):
    state, last_segment = carried
    inputs, steps, b_block, c_block, segment = block
    length = steps.shape[0]
    logs = steps * decay_rate[None, :]
    cumulative = jnp.cumsum(logs, axis=0)
    order = jnp.arange(length)
    allowed = (segment[:, None] == segment[None, :]) & (order[:, None] >= order[None, :])
    spread = cumulative[:, None, :] - cumulative[None, :, :]
    decays = jnp.where(allowed[:, :, None], jnp.exp(jnp.where(allowed[:, :, None], spread, 0.0)), 0.0)
    scores = jnp.dot(c_block, b_block.T, precision=HIGH)
    weights = decays * scores[:, :, None] * steps[None, :, :]
    inside = jnp.einsum('tsh,shp->thp', weights, inputs, precision=HIGH)
    carries = (segment == last_segment).astype(jnp.float32)
    from_state = jnp.einsum('tn,hpn->thp', c_block, state, precision=HIGH)
    outside = from_state * (jnp.exp(cumulative) * carries[:, None])[:, :, None]
    end_segment = segment[length - 1]
    tails = jnp.exp(cumulative[length - 1][None, :] - cumulative) * (segment == end_segment).astype(jnp.float32)[:, None] * steps
    fresh = jnp.einsum('shp,sn->hpn', inputs * tails[:, :, None], b_block, precision=HIGH)
    kept_share = (end_segment == last_segment).astype(jnp.float32)
    state = state * (jnp.exp(cumulative[length - 1]) * kept_share)[:, None, None] + fresh
    return ((state, end_segment), inside + outside)

def state_space(inputs, steps, decay_rate, b_rows, c_rows, segment):
    position_count, head_count, head_size = inputs.shape
    group_count = position_count // GROUP
    blocks = (inputs.reshape(group_count, GROUP, head_count, head_size), steps.reshape(group_count, GROUP, head_count), b_rows.reshape(group_count, GROUP, b_rows.shape[1]), c_rows.reshape(group_count, GROUP, c_rows.shape[1]), segment.reshape(group_count, GROUP))
    initial = (jnp.zeros((head_count, head_size, b_rows.shape[1]), jnp.float32), jnp.array(-1, jnp.int32))
    stepper = jax.checkpoint(partial(group_step, decay_rate=decay_rate))
    finished, outputs = lax.scan(stepper, initial, blocks)
    return outputs.reshape(position_count, head_count, head_size)

def row_mixer(gate, value, shared, rate, segment, conv_value, value_bias, conv_shared, shared_bias, rate_bias, decay_log, skip_gain):
    head_count = rate.shape[1]
    position_count = value.shape[0]
    head_size = value.shape[1] // head_count
    value_act = jax.nn.silu(causal_conv(value, conv_value, value_bias, segment))
    shared_act = jax.nn.silu(causal_conv(shared, conv_shared, shared_bias, segment))
    state_size = shared.shape[1] // 2
    steps = jax.nn.softplus(rate + rate_bias)
    inputs = value_act.reshape(position_count, head_count, head_size)
    mixed_heads = state_space(inputs, steps, -jnp.exp(decay_log), shared_act[:, :state_size], shared_act[:, state_size:], segment)
    mixed_heads = mixed_heads + skip_gain[None, :, None] * inputs
    return mixed_heads.reshape(position_count, head_count * head_size) * jax.nn.silu(gate)

def row_forward(x_row, params, segment, validity):
    norm_gain, w_gate, w_value, w_shared, w_rate, conv_value, value_bias, conv_shared, shared_bias, rate_bias, decay_log, skip_gain, mix_gain, w_out = params
    inverse_in = lax.rsqrt(lax.optimization_barrier(jnp.mean(x_row * x_row, axis=1, keepdims=True)) + EPS)
    normed = low(x_row * inverse_in * norm_gain)
    gate = low_back(jnp.dot(normed, w_gate, precision=HIGH))
    value = low_back(jnp.dot(normed, w_value, precision=HIGH))
    shared = low_back(jnp.dot(normed, w_shared, precision=HIGH))
    rate = low_back(jnp.dot(normed, w_rate, precision=HIGH))
    gated = row_mixer(gate, value, shared, rate, segment, conv_value, value_bias, conv_shared, shared_bias, rate_bias, decay_log, skip_gain)
    inverse_mix = lax.rsqrt(lax.optimization_barrier(jnp.mean(gated * gated, axis=1, keepdims=True)) + EPS)
    mixed = low(gated * inverse_mix * mix_gain * validity[:, None])
    return x_row + jnp.dot(mixed, w_out, precision=HIGH)

def reference(tokens, lengths, norm_gain, w_gate, w_value, w_shared, w_rate, conv_value, value_bias, conv_shared, shared_bias, rate_bias, decay_log, skip_gain, mix_gain, w_out, cotangent):
    params = (norm_gain.astype(jnp.float32), w_gate.astype(jnp.float32), w_value.astype(jnp.float32), w_shared.astype(jnp.float32), w_rate.astype(jnp.float32), conv_value.astype(jnp.float32), value_bias.astype(jnp.float32), conv_shared.astype(jnp.float32), shared_bias.astype(jnp.float32), rate_bias.astype(jnp.float32), decay_log.astype(jnp.float32), skip_gain.astype(jnp.float32), mix_gain.astype(jnp.float32), w_out.astype(jnp.float32))
    row_count = lengths.shape[0]
    x_rows = tokens.astype(jnp.float32).reshape(row_count, SLOTS, D)
    back_rows = cotangent.astype(jnp.float32).reshape(row_count, SLOTS, D)
    zeroed = jax.tree.map(jnp.zeros_like, params)

    def one_row(totals, member):
        x_row, back_row, lengths_row = member
        segment, validity = segments_of(lengths_row, SLOTS)
        result, pull = jax.vjp(lambda xr, pr: row_forward(xr, pr, segment, validity), x_row, params)
        grad_x, grad_params = pull(back_row)
        return (jax.tree.map(jnp.add, totals, grad_params), (result.astype(jnp.bfloat16), grad_x))
    totals, (outputs, grads_x) = lax.scan(one_row, zeroed, (x_rows, back_rows, lengths))
    return (outputs.reshape(TOKENS, D), grads_x.reshape(TOKENS, D), totals[0], totals[1], totals[2], totals[3], totals[4], totals[5], totals[6], totals[7], totals[8], totals[9], totals[10], totals[11], totals[12], totals[13])
```

```python
from functools import partial

import jax
import jax.numpy as jnp
import numpy as np
from jax import lax
from jax.experimental import pallas as pl
from jax.experimental.pallas import tpu as pltpu
from jax.sharding import PartitionSpec as P

Q = 128
STATE = 128
HEAD = 64
EPS = 1e-05
LOG2E = 1.4426950408889634
NEVER = -1e30
F32 = jnp.float32
BF16 = jnp.bfloat16
HIGH = lax.Precision.HIGHEST
VMEM_LIMIT = 56 * 1024 * 1024

NN = (((1,), (0,)), ((), ()))
NT = (((1,), (1,)), ((), ()))
TN = (((0,), (0,)), ((), ()))


def dot(a, b, dims=NN, precision=None):
    return lax.dot_general(a, b, dims, precision=precision, preferred_element_type=F32)


def segment_of(scal, position):
    end = scal[0]
    count = (position >= end).astype(jnp.int32)
    for k in range(1, 4):
        end = end + scal[k]
        count = count + (position >= end).astype(jnp.int32)
    return count


def rows_of(scal, group):
    return scal[4] + group * Q + lax.broadcasted_iota(jnp.int32, (Q, 1), 0)


def same_segment(scal, position, other):
    return (segment_of(scal, position) == segment_of(scal, other)).astype(F32)


def masks(scal, group):
    column = rows_of(scal, group)
    first = scal[4] + group * Q
    before = segment_of(scal, first - 1)
    last = segment_of(scal, first + Q - 1)
    segment = segment_of(scal, column)
    carries = (segment == before).astype(F32)
    ending = (segment == last).astype(F32)
    kept = (before == last).astype(F32)
    return carries, ending, kept


def reaches(scal, group):
    first = scal[4] + group * Q
    return (segment_of(scal, first - 1) == segment_of(scal, scal[4] - 1)).astype(F32)


def triangle(scal, group, flipped):
    first = scal[4] + group * Q
    rows = first + lax.broadcasted_iota(jnp.int32, (Q, Q), 0)
    cols = first + lax.broadcasted_iota(jnp.int32, (Q, Q), 1)
    ordered = (rows <= cols) if flipped else (rows >= cols)
    allowed = ordered & (segment_of(scal, rows) == segment_of(scal, cols))
    return jnp.where(allowed, 0.0, NEVER)


def in_first(rows):
    return lax.broadcasted_iota(jnp.int32, (rows, 2 * HEAD), 1) < HEAD


def pair_of(columns, head):
    rows = columns.shape[0]
    first = jnp.broadcast_to(columns[:, head : head + 1], (rows, 2 * HEAD))
    second = jnp.broadcast_to(columns[:, head + 1 : head + 2], (rows, 2 * HEAD))
    return jnp.where(in_first(rows), first, second)


def spread_heads(columns, head, channels):
    return jnp.concatenate(
        [pair_of(columns, head + 2 * p) for p in range(channels // (2 * HEAD))], axis=1
    )


def stacked_heads(member):
    first = in_first(member.shape[0])
    none = jnp.zeros_like(member)
    return jnp.concatenate([jnp.where(first, member, none), jnp.where(first, none, member)], axis=0)


def head_sums(member, picks):
    high = member.astype(BF16)
    rest = (member - high.astype(F32)).astype(BF16)
    return dot(high, picks) + dot(rest, picks)


def sigmoid(v):
    return 1.0 / (1.0 + jnp.exp(-v))


def load_earlier(group, ext, halo, before, current):
    ext[0:8, :] = jnp.where(group == 0, halo[...], before[...])
    ext[8 : 8 + Q, :] = current


def conv_before_act(ext, taps, scal, group):
    column = rows_of(scal, group)
    total = ext[8 : 8 + Q, :] * taps[3:4, :] + taps[4:5, :]
    for j in range(1, 4):
        total = total + (ext[8 - j : 8 - j + Q, :] * same_segment(scal, column, column - j)) * taps[
            3 - j : 4 - j, :
        ]
    return total


def prepare_kernel(
    scal, cur, before, halo, taps, head_rows, bc, bct, steps, logs, logs_t, total, ext, running
):
    group = pl.program_id(0)
    width = bc.shape[1]

    @pl.when(group == 0)
    def _():
        running[...] = jnp.zeros_like(running)

    load_earlier(group, ext, halo, before, cur[:, :width])
    pre = conv_before_act(ext, taps, scal, group)
    act = pre * sigmoid(pre)
    bc[...] = act.astype(BF16)
    bct[...] = jnp.concatenate(
        [act[:, k * STATE : (k + 1) * STATE].T for k in range(width // STATE)], axis=0
    ).astype(BF16)
    raw = cur[:, width:] + head_rows[0:1, :]
    step = jnp.maximum(raw, 0.0) + jnp.log1p(jnp.exp(-jnp.abs(raw)))
    steps[...] = step
    scaled = step * (head_rows[1:2, :] * LOG2E)
    lower = (
        lax.broadcasted_iota(jnp.int32, (Q, Q), 0) >= lax.broadcasted_iota(jnp.int32, (Q, Q), 1)
    ).astype(F32)
    summed = dot(lower, scaled, precision=HIGH)
    logs[...] = summed
    logs_t[0] = summed.T[: logs_t.shape[1]]
    total[...] = running[...]
    running[...] = running[...] + summed[Q - 1 : Q, :]


def states_kernel(
    head, scal, cur, before, halo, taps, steps, logs, bct, total, act_out, slope_out, states, final,
    through, ext, state,
):
    group = pl.program_id(0)
    channels = cur.shape[1]

    @pl.when(group == 0)
    def _():
        state[...] = jnp.zeros_like(state)

    load_earlier(group, ext, halo, before, cur[...])
    pre = conv_before_act(ext, taps, scal, group)
    gate = sigmoid(pre)
    act = (pre * gate).astype(BF16)
    act_out[...] = act
    slope_out[...] = (gate * (1.0 + pre * (1.0 - gate))).astype(BF16)
    _, ending, kept = masks(scal, group)
    summed = spread_heads(logs[...], head, channels)
    last = summed[Q - 1 : Q, :]
    tails = jnp.exp2(last - summed) * ending
    scaled = (act.astype(F32) * spread_heads(steps[...], head, channels)).astype(BF16)
    fresh = dot(bct[:STATE, :], (scaled.astype(F32) * tails).astype(BF16))
    states[0] = state[...].astype(BF16)
    state[...] = state[...] * (jnp.exp2(last) * kept) + fresh

    @pl.when(group == pl.num_programs(0) - 1)
    def _():
        final[...] = state[...]
        ended = spread_heads(total[...] + logs[Q - 1 : Q, :], head, channels)
        through[...] = jnp.exp2(ended) * reaches(scal, group + 1)


def entering(scal, group, head, states, start, total, channels):
    share = jnp.exp2(spread_heads(total[...], head, channels))[0:1] * reaches(scal, group)
    return states[0].astype(F32) + share * start[...]


def scan_kernel(
    head, scal, act, bc, steps, logs, logs_t, total, gate, back, states, start, rows, scanned, stats
):
    group = pl.program_id(0)
    channels = act.shape[1]
    b_map, c_map = bc[:, :STATE], bc[:, STATE:]
    scores = dot(c_map, b_map, NT)
    allowed = triangle(scal, group, False)
    carries, _, _ = masks(scal, group)
    state = entering(scal, group, head, states, start, total, channels).astype(BF16)
    outside = dot(c_map, state)
    valid = (rows_of(scal, group) < scal[0] + scal[1] + scal[2] + scal[3]).astype(F32)
    squares = jnp.zeros((Q, 2 * HEAD), F32)
    inner = jnp.zeros((Q, 2 * HEAD), F32)
    for p in range(channels // (2 * HEAD)):
        part = slice(2 * HEAD * p, 2 * HEAD * (p + 1))
        weights = []
        columns = []
        for h in (head + 2 * p, head + 2 * p + 1):
            column = jnp.broadcast_to(logs[:, h : h + 1], (Q, Q))
            columns.append(column)
            decay = jnp.exp2(column + (allowed - logs_t[0, h : h + 1, :]))
            weights.append((decay * scores).astype(BF16))
        summed = jnp.where(in_first(Q), columns[0], columns[1])
        member = act[:, part].astype(F32)
        scaled = (member * pair_of(steps[...], head + 2 * p)).astype(BF16)
        result = dot(jnp.concatenate(weights, axis=1), stacked_heads(scaled))
        result = result + outside[:, part] * (jnp.exp2(summed) * carries)
        scanned[:, part] = result
        mixed_heads = result + rows[6:7, part] * member
        raw = gate[:, part]
        gated = mixed_heads * (raw * sigmoid(raw))
        squares = squares + gated * gated
        inner = inner + back[:, part] * rows[5:6, part] * gated
    squares = jnp.sum(squares, axis=1, keepdims=True)
    inner = jnp.sum(inner, axis=1, keepdims=True) * valid
    lane = lax.broadcasted_iota(jnp.int32, (Q, Q), 1)
    both = jnp.where(lane == 0, squares, jnp.where(lane == 1, inner, 0.0))
    stats[...] = both.T[:8]


def gate_back_kernel(
    head, inner_channels, scal, scanned, act, gate, back, stats, bct, logs, total, rows, mixed,
    low_gate, back_heads, reach, sums,
):
    group = pl.program_id(0)
    channels = act.shape[1]

    @pl.when(group == 0)
    def _():
        reach[...] = jnp.zeros_like(reach)
        sums[...] = jnp.zeros_like(sums)

    row = lax.broadcasted_iota(jnp.int32, (8, Q), 0)
    inverse_row = lax.rsqrt(stats[...] / inner_channels + EPS)
    both = jnp.concatenate(
        [jnp.where(row == 0, inverse_row, stats[...]), jnp.zeros((Q - 8, Q), F32)], axis=0
    ).T
    inverse, inner = both[:, 0:1], both[:, 1:2]
    valid = (rows_of(scal, group) < scal[0] + scal[1] + scal[2] + scal[3]).astype(F32)
    slope = inverse * inverse * inverse * inner * valid / inner_channels
    inverse_valid = inverse * valid
    carries, _, _ = masks(scal, group)
    gradients = []
    for p in range(channels // (2 * HEAD)):
        part = slice(2 * HEAD * p, 2 * HEAD * (p + 1))
        member = act[:, part].astype(F32)
        mixed_heads = scanned[:, part] + rows[6:7, part] * member
        raw = gate[:, part]
        share = sigmoid(raw)
        opened = raw * share
        gated = mixed_heads * opened
        back_part = back[:, part]
        gain = rows[5:6, part]
        normal = gated * inverse_valid
        mixed[:, part] = (normal * gain).astype(BF16)
        scaled_back = back_part * inverse_valid
        gradient = scaled_back * gain - gated * slope
        low_gate[:, part] = (
            gradient * mixed_heads * (share * (1.0 + raw * (1.0 - share)))
        ).astype(BF16)
        low = (gradient * opened).astype(BF16)
        back_heads[:, part] = low
        wide = low.astype(F32)
        sums[0:1, part] = sums[0:1, part] + jnp.sum(scaled_back * gated, axis=0, keepdims=True)
        sums[1:2, part] = sums[1:2, part] + jnp.sum(wide * member, axis=0, keepdims=True)
        entered = jnp.exp2(pair_of(logs[...], head + 2 * p)) * carries
        gradients.append((wide * entered).astype(BF16))
    share = jnp.exp2(spread_heads(total[...], head, channels))[0:1] * reaches(scal, group)
    reach[...] = reach[...] + share * dot(bct[STATE:, :], jnp.concatenate(gradients, axis=1))


def scan_back_kernel(
    head, scal, act, slope, back_heads, scanned, cur, before, halo, rows, picks, bc, bct, steps,
    logs, logs_t, total, raw_rate, head_rows, states, start, leaving, low_value, back_bc, low_rate,
    sums, head_out, first_rows, last_rows, ext, back_ext, back_state,
):
    turn = pl.program_id(0)
    turns = pl.num_programs(0)
    group = turns - 1 - turn
    channels = act.shape[1]

    @pl.when(turn == 0)
    def _():
        back_state[...] = leaving[...]
        back_ext[Q : Q + 8, :] = jnp.zeros_like(back_ext[Q : Q + 8, :])
        sums[...] = jnp.zeros_like(sums)
        head_out[...] = jnp.zeros_like(head_out)

    b_map, c_map = bc[:, :STATE], bc[:, STATE:]
    scores = dot(b_map, c_map, NT)
    allowed = triangle(scal, group, True)
    carries, ending, kept = masks(scal, group)
    state = entering(scal, group, head, states, start, total, channels)
    state_low = state.astype(BF16)
    leaving_low = back_state[...].astype(BF16)
    from_state = dot(b_map, leaving_low)
    back_scores = jnp.zeros((Q, Q), F32)
    into_state, out_of_state, differences, passed, products = [], [], [], [], []
    for p in range(channels // (2 * HEAD)):
        part = slice(2 * HEAD * p, 2 * HEAD * (p + 1))
        low = back_heads[:, part]
        wide = low.astype(F32)
        member = act[:, part].astype(F32)
        step = pair_of(steps[...], head + 2 * p)
        scaled = (member * step).astype(BF16)
        back_weights = dot(stacked_heads(scaled), low, NT)
        weights, columns = [], []
        for k, h in enumerate((head + 2 * p, head + 2 * p + 1)):
            column = jnp.broadcast_to(logs[:, h : h + 1], (Q, Q))
            columns.append(column)
            decay = jnp.exp2((logs_t[0, h : h + 1, :] + allowed) - column)
            weights.append((decay * scores).astype(BF16))
            back_scores = back_scores + decay * back_weights[k * Q : (k + 1) * Q]
        summed = jnp.where(in_first(Q), columns[0], columns[1])
        last = summed[Q - 1 : Q, :]
        tails = jnp.exp2(last - summed) * ending
        back_scaled = dot(jnp.concatenate(weights, axis=1), stacked_heads(low))
        scaled_wide = scaled.astype(F32)
        from_end = tails * from_state[:, part]
        differences.append(wide * scanned[:, part] - scaled_wide * back_scaled)
        passed.append((scaled_wide * from_end).astype(BF16))
        back_scaled = back_scaled + from_end
        into_state.append((scaled_wide * tails).astype(BF16))
        out_of_state.append((wide * (jnp.exp2(summed) * carries)).astype(BF16))
        products.append((back_scaled * member).astype(BF16))
        back_act = back_scaled * step + rows[6:7, part] * wide
        back_ext[0:Q, part] = back_act * slope[:, part].astype(F32)
    into_state = jnp.concatenate(into_state, axis=1)
    out_of_state = jnp.concatenate(out_of_state, axis=1)
    back_b = dot(back_scores.astype(BF16), c_map) + dot(into_state, leaving_low, NT)
    back_c = dot(back_scores.T.astype(BF16), b_map) + dot(out_of_state, state_low, NT)
    back_bc[:, :STATE] = back_b
    back_bc[:, STATE:] = back_c

    whole = spread_heads(logs[Q - 1 : Q, :], head, channels)
    kept_state = back_state[...] * (jnp.exp2(whole) * kept)
    back_state[...] = kept_state + dot(bct[STATE:, :], out_of_state)
    crossing = jnp.sum(kept_state * state, axis=0, keepdims=True)

    difference = head_sums(jnp.concatenate(differences, axis=1), picks[...])
    before_it = dot(jnp.concatenate(passed, axis=1), picks[...])
    product = dot(jnp.concatenate(products, axis=1), picks[...])
    crossing = head_sums(jnp.broadcast_to(crossing, (8, channels)), picks[...])
    rows_at = lax.broadcasted_iota(jnp.int32, (Q, Q), 0)
    cols_at = lax.broadcasted_iota(jnp.int32, (Q, Q), 1)
    back_logs = (
        dot((rows_at <= cols_at).astype(F32), difference, precision=HIGH)
        + dot((rows_at > cols_at).astype(F32), before_it, precision=HIGH)
        + crossing[0:1, :]
    )
    decays = back_logs * head_rows[1:2, :]
    back_rate = (product + decays) * sigmoid(raw_rate[...] + head_rows[0:1, :])
    low_rate[...] = back_rate.astype(BF16)
    head_out[0:1, :] = head_out[0:1, :] + jnp.sum(back_rate, axis=0, keepdims=True)
    head_out[1:2, :] = head_out[1:2, :] + jnp.sum(decays * steps[...], axis=0, keepdims=True)

    conv_back(group, turn, scal, ext, back_ext, cur[...], before, halo, rows, low_value, sums,
              first_rows, last_rows)


def conv_back(
    group, turn, scal, ext, back_ext, current, before, halo, taps, low, sums, first_rows, last_rows
):
    load_earlier(group, ext, halo, before, current)
    column = rows_of(scal, group)
    now = back_ext[0:Q, :]
    sums[3:4, :] = sums[3:4, :] + jnp.sum(now * ext[8 : 8 + Q, :], axis=0, keepdims=True)
    sums[4:5, :] = sums[4:5, :] + jnp.sum(now, axis=0, keepdims=True)
    total = now * taps[3:4, :]
    for j in range(1, 4):
        tap = slice(3 - j, 4 - j)
        earlier = ext[8 - j : 8 - j + Q, :] * same_segment(scal, column, column - j)
        sums[tap, :] = sums[tap, :] + jnp.sum(now * earlier, axis=0, keepdims=True)
        later = back_ext[j : j + Q, :] * same_segment(scal, column, column + j)
        total = total + later * taps[tap, :]
    low[...] = total.astype(BF16)

    @pl.when(turn == 0)
    def _():
        last_rows[...] = total[Q - 8 : Q, :]

    back_ext[Q : Q + 8, :] = back_ext[0:8, :]

    @pl.when(group == 0)
    def _():
        first_rows[...] = back_ext[0:8, :]


def shared_back_kernel(
    scal, back_bc, back_more, cur, before, halo, taps, low, sums, first_rows, last_rows, ext, back_ext
):
    turn = pl.program_id(0)
    group = pl.num_programs(0) - 1 - turn

    @pl.when(turn == 0)
    def _():
        back_ext[Q : Q + 8, :] = jnp.zeros_like(back_ext[Q : Q + 8, :])
        sums[...] = jnp.zeros_like(sums)

    load_earlier(group, ext, halo, before, cur[...])
    pre = conv_before_act(ext, taps, scal, group)
    gate = sigmoid(pre)
    back_ext[0:Q, :] = (back_bc[...] + back_more[...]) * (gate * (1.0 + pre * (1.0 - gate)))
    conv_back(
        group, turn, scal, ext, back_ext, cur[...], before, halo, taps, low, sums, first_rows, last_rows
    )


def many_dots_kernel(dims, scal, *refs):
    count = len(dims)
    out = refs[2 * count]
    total = dot(refs[0][...], refs[count][...], dims[0])
    for k in range(1, count):
        total = total + dot(refs[k][...], refs[count + k][...], dims[k])
    out[...] = total.astype(out.dtype)


def call(body, grid, in_specs, out_specs, out_shape, scratch, name, flops, args):
    moved = sum(a.size * a.dtype.itemsize for a in args) + sum(
        int(np.prod(o.shape)) * np.dtype(o.dtype).itemsize for o in out_shape
    )
    return pl.pallas_call(
        body,
        grid_spec=pltpu.PrefetchScalarGridSpec(
            num_scalar_prefetch=1,
            grid=(grid,),
            in_specs=in_specs,
            out_specs=out_specs,
            scratch_shapes=scratch,
        ),
        out_shape=out_shape,
        compiler_params=pltpu.CompilerParams(vmem_limit_bytes=VMEM_LIMIT),
        cost_estimate=pl.CostEstimate(flops=flops, bytes_accessed=moved, transcendentals=0),
        name=name,
    )(*args)


def whole(shape):
    return pl.BlockSpec(shape, lambda i, s: tuple(0 for _ in shape))


def shape_of(shape, dtype):
    return jax.ShapeDtypeStruct(shape, dtype)


def many_dots(offset_rows, lefts, rights, dims, rows, dtype, name):
    tile = min(256, rows)
    columns = rights[0].shape[0 if dims[0] == NT else 1]
    scal = (offset_rows // tile).reshape(1).astype(jnp.int32)
    flops = 2 * rows * columns * sum(a.shape[1] for a in lefts)
    return call(
        partial(many_dots_kernel, tuple(dims)),
        rows // tile,
        [pl.BlockSpec((tile, a.shape[1]), lambda i, s: (s[0] + i, 0)) for a in lefts]
        + [whole(b.shape) for b in rights],
        [pl.BlockSpec((tile, columns), lambda i, s: (i, 0))],
        [shape_of((rows, columns), dtype)],
        [],
        name,
        flops,
        (scal, *lefts, *rights),
    )[0]


def solution(mesh):
    tensor = mesh.shape["tensor"]
    copies = mesh.shape["dp"]
    ny = tensor // 2
    nx = ny if copies % ny == 0 else 1
    nz = copies // nx

    def from_y(member, shift):
        pairs = [((((y + shift) % ny) * 2 + c), y * 2 + c) for y in range(ny) for c in range(2)]
        return lax.ppermute(member, "tensor", pairs)

    def next_y(member, step):
        pairs = [
            ((y - step) * 2 + c, y * 2 + c)
            for y in range(ny)
            for c in range(2)
            if 0 <= y - step < ny
        ]
        return lax.ppermute(member, "tensor", pairs)

    def from_core(member):
        return lax.ppermute(member, "tensor", [(t ^ 1, t) for t in range(tensor)])

    def from_x(member, shift):
        pairs = [(z * nx + (x + shift) % nx, z * nx + x) for z in range(nz) for x in range(nx)]
        return lax.ppermute(member, "dp", pairs)

    def from_z(member, shift):
        pairs = [(((z + shift) % nz) * nx + x, z * nx + x) for z in range(nz) for x in range(nx)]
        return lax.ppermute(member, "dp", pairs)

    def sum_rows(member):
        bit = 1
        while bit < copies:
            member = member + lax.ppermute(member, "dp", [(d ^ bit, d) for d in range(copies)])
            bit *= 2
        return member

    def sum_all(member):
        bit = 1
        while bit < tensor:
            member = member + lax.ppermute(member, "tensor", [(t ^ bit, t) for t in range(tensor)])
            bit *= 2
        return sum_rows(member)

    def reduce_blocks(blocks, x, z):
        rows, columns = blocks[0].shape
        each = rows // copies
        half = each // 2
        views = [b.reshape(nz, nx, each, columns) for b in blocks]

        def along_y(parts):
            total = parts[0].astype(F32)
            for j in range(1, ny):
                total = total + from_y(parts[j], ny - j).astype(F32)
            return total

        def along_x(part):
            total = lax.dynamic_index_in_dim(part, x, 1, keepdims=False).astype(F32)
            for k in range(1, nx):
                sent = lax.dynamic_index_in_dim(part, (x + k) % nx, 1, keepdims=False)
                total = total + from_x(sent.astype(BF16), nx - k).astype(F32)
            return total

        first = along_x(along_y([v[:, :, :half] for v in views]).astype(BF16))
        second = along_y([along_x(v[:, :, half:]).astype(BF16) for v in views])
        both = jnp.concatenate([first, second], axis=1).astype(BF16)
        total = lax.dynamic_index_in_dim(both, z, 0, keepdims=False).astype(F32)
        for k in range(1, nz):
            sent = lax.dynamic_index_in_dim(both, (z + k) % nz, 0, keepdims=False)
            total = total + from_z(sent, nz - k).astype(F32)
        return total

    def shards(
        tokens, lengths, norm_gain, w_gate, w_value, w_shared, w_rate, conv_value, value_bias,
        conv_shared, shared_bias, rate_bias, decay_log, skip_gain, mix_gain, w_out, cotangent,
    ):
        index = lax.axis_index("tensor")
        y, core = index // 2, index % 2
        dp = lax.axis_index("dp")
        z, x = dp // nx, dp % nx
        own_rows, width = tokens.shape
        rows = 2 * own_rows
        groups = rows // Q
        channels = w_gate.shape[1]
        heads = w_rate.shape[1]
        inner = channels * tensor
        own_start = core * own_rows
        lanes = 128
        wide_heads = -(-(ny * heads) // 8) * 8
        maps = w_shared.shape[1]
        blocks = range(ny)

        values = [w_value] + [from_y(w_value, j) for j in range(1, ny)]
        gates = [w_gate] + [from_y(w_gate, j) for j in range(1, ny)]
        outs = [w_out] + [from_y(w_out, j) for j in range(1, ny)]
        packed = jnp.concatenate(
            [
                conv_value.T,
                value_bias[None],
                mix_gain[None],
                jnp.repeat(skip_gain, HEAD)[None],
                jnp.concatenate([rate_bias, decay_log, jnp.zeros((channels - 2 * heads,), F32)])[None],
            ],
            axis=0,
        )
        packs = [packed] + [from_y(packed, j) for j in range(1, ny)]
        rate_t = w_rate.T
        rates_t = [rate_t] + [from_y(rate_t, j) for j in range(1, ny)]
        all_rates = jnp.concatenate(
            rates_t + [jnp.zeros((lanes - ny * heads, width), BF16)], axis=0
        )
        w_small = jnp.concatenate([w_shared, all_rates.T], axis=1)
        fill = jnp.zeros((lanes - ny * heads,), F32)
        head_rows = jnp.concatenate(
            [
                jnp.concatenate([p[7, :heads] for p in packs] + [fill])[None],
                jnp.concatenate([-jnp.exp(p[7, heads : 2 * heads]) for p in packs] + [fill])[None],
                jnp.zeros((6, lanes), F32),
            ],
            axis=0,
        )
        shared_taps = jnp.concatenate(
            [conv_shared.T, shared_bias[None], jnp.zeros((3, maps), F32)], axis=0
        )
        scal = jnp.concatenate([lengths[0], (y * rows).reshape(1)]).astype(jnp.int32)

        residual = tokens.astype(F32)
        inverse_in = lax.rsqrt(jnp.mean(residual * residual, axis=1, keepdims=True) + EPS)
        normed_own = (residual * inverse_in * norm_gain).astype(BF16)

        def chip_rows(own):
            other = from_core(own)
            both = lax.dynamic_update_slice(jnp.zeros((rows, width), own.dtype), own, (own_start, 0))
            return lax.dynamic_update_slice(both, other, (own_rows - own_start, 0))

        normed = chip_rows(normed_own)
        back_rows = chip_rows(cotangent)
        halo = next_y(normed[rows - 16 :], 1)

        def group_rows(columns, at=0):
            return pl.BlockSpec((Q, columns), lambda i, s: (i, at))

        def rows_before(columns):
            return pl.BlockSpec((8, columns), lambda i, s: (jnp.maximum(i * (Q // 8) - 1, 0), 0))

        def turned(columns, at=0):
            return pl.BlockSpec((Q, columns), lambda i, s: (groups - 1 - i, at))

        def turned_before(columns):
            return pl.BlockSpec(
                (8, columns), lambda i, s: (jnp.maximum((groups - 1 - i) * (Q // 8) - 1, 0), 0)
            )

        small = dot(normed, w_small)
        small_halo = dot(halo, w_small)[8:]
        bc, bct, steps, logs, logs_t, total = call(
            prepare_kernel,
            groups,
            [
                group_rows(maps + lanes),
                rows_before(maps),
                whole((8, maps)),
                whole((8, maps)),
                whole((8, lanes)),
            ],
            [
                group_rows(maps),
                pl.BlockSpec((maps, Q), lambda i, s: (0, i)),
                group_rows(lanes),
                group_rows(lanes),
                pl.BlockSpec((1, wide_heads, Q), lambda i, s: (i, 0, 0)),
                pl.BlockSpec((8, lanes), lambda i, s: (i, 0)),
            ],
            [
                shape_of((rows, maps), BF16),
                shape_of((maps, rows), BF16),
                shape_of((rows, lanes), F32),
                shape_of((rows, lanes), F32),
                shape_of((groups, wide_heads, Q), F32),
                shape_of((groups * 8, lanes), F32),
            ],
            [pltpu.VMEM((Q + 8, maps), F32), pltpu.VMEM((8, lanes), F32)],
            "prepare",
            rows * 2000,
            (scal, small, small[:, :maps], small_halo[:, :maps], shared_taps, head_rows),
        )

        flops_scan = rows * channels * 2 * 600
        raw_values, value_halos, acts, slopes, states, finals, throughs = [], [], [], [], [], [], []
        for j in blocks:
            raw = dot(normed, values[j])
            raw_halo = dot(halo, values[j])[8:]
            act, slope, state, final, through = call(
                partial(states_kernel, j * heads),
                groups,
                [
                    group_rows(channels),
                    rows_before(channels),
                    whole((8, channels)),
                    whole((8, channels)),
                    group_rows(lanes),
                    group_rows(lanes),
                    pl.BlockSpec((maps, Q), lambda i, s: (0, i)),
                    pl.BlockSpec((8, lanes), lambda i, s: (i, 0)),
                ],
                [
                    group_rows(channels),
                    group_rows(channels),
                    pl.BlockSpec((1, STATE, channels), lambda i, s: (i, 0, 0)),
                    whole((STATE, channels)),
                    whole((8, channels)),
                ],
                [
                    shape_of((rows, channels), BF16),
                    shape_of((rows, channels), BF16),
                    shape_of((groups, STATE, channels), BF16),
                    shape_of((STATE, channels), F32),
                    shape_of((8, channels), F32),
                ],
                [pltpu.VMEM((Q + 8, channels), F32), pltpu.VMEM((STATE, channels), F32)],
                "states",
                flops_scan // 2,
                (scal, raw, raw, raw_halo, packs[j], steps, logs, bct, total),
            )
            raw_values.append(raw)
            value_halos.append(raw_halo)
            acts.append(act)
            slopes.append(slope)
            states.append(state)
            finals.append(final)
            throughs.append(through)

        before = [(j + 1) % ny for j in blocks]
        after = [(j - 1) % ny for j in blocks]
        starts = [next_y(finals[k], 1) for k in before]
        for _ in range(ny - 2):
            starts = [next_y(finals[k] + throughs[k][0:1] * starts[k], 1) for k in before]

        raw_gates, backs, scans, stats = [], [], [], []
        for j in blocks:
            raw_gate = dot(normed, gates[j])
            back = dot(back_rows, outs[j], NT)
            scanned, stat = call(
                partial(scan_kernel, j * heads),
                groups,
                [
                    group_rows(channels),
                    group_rows(maps),
                    group_rows(lanes),
                    group_rows(lanes),
                    pl.BlockSpec((1, wide_heads, Q), lambda i, s: (i, 0, 0)),
                    pl.BlockSpec((8, lanes), lambda i, s: (i, 0)),
                    group_rows(channels),
                    group_rows(channels),
                    pl.BlockSpec((1, STATE, channels), lambda i, s: (i, 0, 0)),
                    whole((STATE, channels)),
                    whole((8, channels)),
                ],
                [group_rows(channels), pl.BlockSpec((8, Q), lambda i, s: (0, i))],
                [shape_of((rows, channels), F32), shape_of((8, rows), F32)],
                [],
                "scan",
                flops_scan,
                (scal, acts[j], bc, steps, logs, logs_t, total, raw_gate, back, states[j], starts[j],
                 packs[j]),
            )
            raw_gates.append(raw_gate)
            backs.append(back)
            scans.append(scanned)
            stats.append(stat)

        stat = sum(stats[1:], stats[0])
        stat = stat + from_core(stat)

        mixeds, low_gates, back_heads, reaching, gate_sums = [], [], [], [], []
        for j in blocks:
            mixed, low_gate, back_head, reach, sums = call(
                partial(gate_back_kernel, j * heads, inner),
                groups,
                [
                    group_rows(channels),
                    group_rows(channels),
                    group_rows(channels),
                    group_rows(channels),
                    pl.BlockSpec((8, Q), lambda i, s: (0, i)),
                    pl.BlockSpec((maps, Q), lambda i, s: (0, i)),
                    group_rows(lanes),
                    pl.BlockSpec((8, lanes), lambda i, s: (i, 0)),
                    whole((8, channels)),
                ],
                [
                    group_rows(channels),
                    group_rows(channels),
                    group_rows(channels),
                    whole((STATE, channels)),
                    whole((8, channels)),
                ],
                [
                    shape_of((rows, channels), BF16),
                    shape_of((rows, channels), BF16),
                    shape_of((rows, channels), BF16),
                    shape_of((STATE, channels), F32),
                    shape_of((8, channels), F32),
                ],
                [],
                "gate_back",
                flops_scan // 2,
                (scal, scans[j], acts[j], raw_gates[j], backs[j], stat, bct, logs, total, packs[j]),
            )
            mixeds.append(mixed)
            low_gates.append(low_gate)
            back_heads.append(back_head)
            reaching.append(reach)
            gate_sums.append(sums)

        leavings = [next_y(reaching[k], -1) for k in after]
        for _ in range(ny - 2):
            leavings = [next_y(reaching[k] + throughs[k][0:1] * leavings[k], -1) for k in after]

        ahead = (1 - core) * own_rows
        sent = many_dots(ahead, mixeds, outs, [NN] * ny, own_rows, BF16, "out_other")
        kept = many_dots(own_start, mixeds, outs, [NN] * ny, own_rows, F32, "out_own")
        block_out = (residual + kept + from_core(sent).astype(F32)).astype(BF16)
        out_blocks = [dot(back_rows, m, TN).astype(BF16) for m in mixeds]
        grad_out = reduce_blocks(out_blocks, x, z).T
        gate_blocks = [dot(normed, low, TN).astype(BF16) for low in low_gates]
        grad_gate = reduce_blocks(gate_blocks, x, z)

        channel = np.arange(channels)
        low_values, back_bcs, low_rates, conv_sums, head_sums_ = [None] * ny, [], [], [None] * ny, []
        for j in reversed(blocks):
            picks = jnp.asarray(
                (np.arange(lanes)[None, :] == (j * heads + channel // HEAD)[:, None]), BF16
            )
            low, back_bc, low_rate, sums, head_out, first_rows, last_rows = call(
                partial(scan_back_kernel, j * heads),
                groups,
                [
                    turned(channels),
                    turned(channels),
                    turned(channels),
                    turned(channels),
                    turned(channels),
                    turned_before(channels),
                    whole((8, channels)),
                    whole((8, channels)),
                    whole((channels, lanes)),
                    turned(maps),
                    pl.BlockSpec((maps, Q), lambda i, s: (0, groups - 1 - i)),
                    turned(lanes),
                    turned(lanes),
                    pl.BlockSpec((1, wide_heads, Q), lambda i, s: (groups - 1 - i, 0, 0)),
                    pl.BlockSpec((8, lanes), lambda i, s: (groups - 1 - i, 0)),
                    turned(lanes, maps // lanes),
                    whole((8, lanes)),
                    pl.BlockSpec((1, STATE, channels), lambda i, s: (groups - 1 - i, 0, 0)),
                    whole((STATE, channels)),
                    whole((STATE, channels)),
                ],
                [
                    turned(channels),
                    turned(maps),
                    turned(lanes),
                    whole((8, channels)),
                    whole((8, lanes)),
                    whole((8, channels)),
                    whole((8, channels)),
                ],
                [
                    shape_of((rows, channels), BF16),
                    shape_of((rows, maps), F32),
                    shape_of((rows, lanes), BF16),
                    shape_of((8, channels), F32),
                    shape_of((8, lanes), F32),
                    shape_of((8, channels), F32),
                    shape_of((8, channels), F32),
                ],
                [
                    pltpu.VMEM((Q + 8, channels), F32),
                    pltpu.VMEM((Q + 8, channels), F32),
                    pltpu.VMEM((STATE, channels), F32),
                ],
                "scan_back",
                flops_scan * 3,
                (scal, acts[j], slopes[j], back_heads[j], scans[j], raw_values[j], raw_values[j],
                 value_halos[j], packs[j], picks, bc, bct, steps, logs, logs_t, total, small, head_rows,
                 states[j], starts[j], leavings[j]),
            )
            low_values[j] = (low, first_rows, last_rows)
            back_bcs.append(back_bc)
            low_rates.append(low_rate)
            conv_sums[j] = sums
            head_sums_.append(head_out)

        firsts = [member[1] for member in low_values]
        low_values = [
            joined(scal, low_values[j][0], firsts[after[j]], low_values[j][2], packs[j], next_y, rows)
            for j in blocks
        ]
        value_blocks = [dot(normed, low, TN).astype(BF16) for low in low_values]
        grad_value = reduce_blocks(value_blocks, x, z)

        back_bc = sum(back_bcs[1:], back_bcs[0])
        low_shared, shared_sums, first_rows, last_rows = call(
            shared_back_kernel,
            groups,
            [
                turned(maps),
                turned(maps),
                turned(maps),
                turned_before(maps),
                whole((8, maps)),
                whole((8, maps)),
            ],
            [turned(maps), whole((8, maps)), whole((8, maps)), whole((8, maps))],
            [
                shape_of((rows, maps), BF16),
                shape_of((8, maps), F32),
                shape_of((8, maps), F32),
                shape_of((8, maps), F32),
            ],
            [pltpu.VMEM((Q + 8, maps), F32), pltpu.VMEM((Q + 8, maps), F32)],
            "shared_back",
            rows * 2000,
            (scal, back_bc, from_core(back_bc), small, small, small_halo[:, :maps], shared_taps),
        )
        low_shared = joined(scal, low_shared, first_rows, last_rows, shared_taps, next_y, rows)
        low_rate = sum(low_rates[1:], low_rates[0])
        shared_own = lax.dynamic_slice(low_shared, (own_start, 0), (own_rows, maps))
        grad_shared = dot(normed_own, shared_own, TN)
        grad_rate_all = dot(normed, low_rate, TN)

        lefts = [low_rate] + low_gates + low_values
        rights = [all_rates.T] + gates + values
        sent = many_dots(ahead, lefts, rights, [NT] * len(lefts), own_rows, BF16, "back_other")
        lefts = [low_shared] + lefts
        rights = [w_shared] + rights
        kept = many_dots(own_start, lefts, rights, [NT] * len(lefts), own_rows, F32, "back_own")
        back_normed = kept + from_core(sent).astype(F32)
        grad_norm = jnp.sum(back_normed * residual * inverse_in, axis=0)
        scaled = back_normed * norm_gain
        tokens_grad = (
            cotangent.astype(F32)
            + scaled * inverse_in
            - residual
            * (inverse_in * inverse_in * inverse_in)
            * jnp.sum(scaled * residual, axis=1, keepdims=True)
            / width
        )

        rate_blocks = [grad_rate_all[:, j * heads : (j + 1) * heads].T for j in blocks]
        grad_rate = rate_blocks[0]
        for j in range(1, ny):
            grad_rate = grad_rate + from_y(rate_blocks[j], ny - j)
        grad_rate = lax.dynamic_slice(
            sum_rows(grad_rate), (0, dp * (width // copies)), (heads, width // copies)
        ).T
        head_out = sum(head_sums_[1:], head_sums_[0])
        smalls = []
        for j in blocks:
            skip = gate_sums[j][1].reshape(heads, HEAD).sum(axis=1)
            own_heads = head_out[:2, j * heads : (j + 1) * heads].reshape(2 * heads)
            line = jnp.concatenate([skip, own_heads, jnp.zeros((channels - 3 * heads,), F32)])
            smalls.append(
                jnp.concatenate(
                    [conv_sums[j][:5], gate_sums[j][:1], line[None], jnp.zeros((1, channels), F32)]
                )
            )
        own = smalls[0]
        for j in range(1, ny):
            own = own + from_y(smalls[j], ny - j)
        own = sum_rows(own)
        shared_sums = jnp.where(core == 0, shared_sums, 0.0)
        alls = jnp.concatenate([shared_sums, grad_norm.reshape(-1, maps)], axis=0)
        alls = sum_all(alls)
        grad_shared = lax.psum(grad_shared, ("dp", "tensor"))
        return (
            block_out,
            tokens_grad,
            alls[8:].reshape(width),
            grad_gate,
            grad_value,
            grad_shared,
            grad_rate,
            own[:4].T,
            own[4],
            alls[:4].T,
            alls[4],
            own[6, heads : 2 * heads],
            own[6, 2 * heads : 3 * heads],
            own[6, :heads],
            own[5],
            grad_out,
        )

    def joined(scal, low, first_rows, last_rows, taps, next_y, rows):
        later = next_y(first_rows, -1)
        last = scal[4] + rows - 1
        out = last_rows
        for back in range(1, 4):
            at = last + 1 - back
            extra = jnp.zeros_like(last_rows[0])
            for j in range(back, 4):
                same = same_segment(scal, at, at + j)
                extra = extra + same * taps[3 - j] * later[j - back]
            out = out.at[8 - back].add(extra)
        return lax.dynamic_update_slice(low, out.astype(BF16), (rows - 8, 0))

    in_specs = (
        P(("dp", "tensor"), None),
        P("dp", None),
        P(),
        P(None, "tensor"),
        P(None, "tensor"),
        P(),
        P(None, "tensor"),
        P("tensor", None),
        P("tensor"),
        P(),
        P(),
        P("tensor"),
        P("tensor"),
        P("tensor"),
        P("tensor"),
        P("tensor", None),
        P(("dp", "tensor"), None),
    )
    out_specs = (
        P(("dp", "tensor"), None),
        P(("dp", "tensor"), None),
        P(),
        P("dp", "tensor"),
        P("dp", "tensor"),
        P(),
        P("dp", "tensor"),
        P("tensor", None),
        P("tensor"),
        P(),
        P(),
        P("tensor"),
        P("tensor"),
        P("tensor"),
        P("tensor"),
        P("tensor", "dp"),
    )
    return jax.shard_map(shards, mesh=mesh, in_specs=in_specs, out_specs=out_specs, check_vma=False)
```

```python
from functools import partial

import jax
import jax.numpy as jnp
import numpy as np
from jax import lax
from jax.experimental import pallas as pl
from jax.experimental.pallas import tpu as pltpu
from jax.sharding import PartitionSpec as P

Q = 128
STATE = 128
HEAD = 64
EPS = 1e-05
LOG2E = 1.4426950408889634
NEVER = -1e30
F32 = jnp.float32
BF16 = jnp.bfloat16
HIGH = lax.Precision.HIGHEST
VMEM_LIMIT = 56 * 1024 * 1024
STEP_ROWS = 512

NN = (((1,), (0,)), ((), ()))
NT = (((1,), (1,)), ((), ()))
TN = (((0,), (0,)), ((), ()))


def dot(a, b, dims=NN, precision=None):
    return lax.dot_general(a, b, dims, precision=precision, preferred_element_type=F32)


STEP, LOG, MARK, RISE = 0, 32, 64, 96
CARRIES, ENDING, VALID, SEGMENT = MARK, MARK + 1, MARK + 2, MARK + 3
EARLIER, LATER = MARK + 3, MARK + 6


def loop(count, body):
    def step(k, carry):
        body(k)
        return carry

    lax.fori_loop(0, count, step, 0, unroll=True)


def group_of(ref, k):
    return ref.at[pl.ds(pl.multiple_of(k * Q, Q), Q), :]


def lane_group_of(ref, k):
    return ref.at[:, pl.ds(pl.multiple_of(k * Q, Q), Q)]


def segment_of(scal, position):
    end = scal[0]
    count = (position >= end).astype(jnp.int32)
    for k in range(1, 4):
        end = end + scal[k]
        count = count + (position >= end).astype(jnp.int32)
    return count


def same_segment(scal, position, other):
    return (segment_of(scal, position) == segment_of(scal, other)).astype(F32)


def kept(scal, group):
    first = scal[4] + group * Q
    return same_segment(scal, first - 1, first + Q - 1)


def reaches(scal, group):
    return same_segment(scal, scal[4] + group * Q - 1, scal[4] - 1)


def triangle(cols, rows, flipped):
    first = lax.broadcasted_iota(jnp.int32, (Q, Q), 0)
    second = lax.broadcasted_iota(jnp.int32, (Q, Q), 1)
    ordered = (first <= second) if flipped else (first >= second)
    allowed = ordered & (cols[:, SEGMENT : SEGMENT + 1] == rows[LOG : LOG + 1, :])
    return jnp.where(allowed, 0.0, NEVER)


def in_first(rows):
    return lax.broadcasted_iota(jnp.int32, (rows, 2 * HEAD), 1) < HEAD


def pair_of(columns, lane):
    rows = columns.shape[0]
    first = jnp.broadcast_to(columns[:, lane : lane + 1], (rows, 2 * HEAD))
    second = jnp.broadcast_to(columns[:, lane + 1 : lane + 2], (rows, 2 * HEAD))
    return jnp.where(in_first(rows), first, second)


def spread_heads(columns, lane, channels):
    return jnp.concatenate(
        [pair_of(columns, lane + 2 * p) for p in range(channels // (2 * HEAD))], axis=1
    )


def stacked_heads(member):
    first = in_first(member.shape[0])
    none = jnp.zeros_like(member)
    return jnp.concatenate([jnp.where(first, member, none), jnp.where(first, none, member)], axis=0)


def split_sum(member, picks):
    high = member.astype(BF16)
    rest = (member - high.astype(F32)).astype(BF16)
    return dot(high, picks) + dot(rest, picks)


def in_order(member, ordered):
    first = member.astype(BF16).astype(F32)
    rest = member - first
    second = rest.astype(BF16).astype(F32)
    parts = first + pltpu.roll(second, 32, 1) + pltpu.roll(rest - second, 64, 1)
    total = dot(ordered.astype(BF16), parts.astype(BF16))
    return total + pltpu.roll(total, 96, 1) + pltpu.roll(total, 64, 1)


def sigmoid(v):
    return 0.5 * jnp.tanh(0.5 * v) + 0.5


def conv_before_act(ext, taps, cols):
    total = ext[8 : 8 + Q, :] * taps[3:4, :] + taps[4:5, :]
    for j in range(1, 4):
        same = cols[:, EARLIER + j : EARLIER + j + 1]
        total = total + (ext[8 - j : 8 - j + Q, :] * same) * taps[3 - j : 4 - j, :]
    return total


def follow(group, ext, halo, current):
    @pl.when(group == 0)
    def _():
        ext[0:8, :] = halo[8:16, :].astype(F32)

    @pl.when(group > 0)
    def _():
        ext[0:8, :] = ext[Q : Q + 8, :]

    ext[8 : 8 + Q, :] = current.astype(F32)


def prepare_kernel(
    subs, scal, shared, rates, halo, taps, head_rows, bc_out, bct_out, cols_out, rows_out, total_out,
    ext, running,
):
    @pl.when(pl.program_id(0) == 0)
    def _():
        running[...] = jnp.zeros_like(running)

    def body(k):
        group = pl.program_id(0) * subs + k
        bc, cols = group_of(bc_out, k), group_of(cols_out, k)
        bct, rows = lane_group_of(bct_out, k), rows_out.at[k]
        width = bc.shape[1]
        raw = group_of(rates, k)[...] + head_rows[0:1, :]
        step = jnp.maximum(raw, 0.0) + jnp.log1p(jnp.exp(-jnp.abs(raw)))
        scaled = step * (head_rows[1:2, :] * LOG2E)
        at = lax.broadcasted_iota(jnp.int32, (Q, Q), 0)
        lane = lax.broadcasted_iota(jnp.int32, (Q, Q), 1)
        summed = in_order(jnp.where(lane < 32, scaled, 0.0), (at >= lane).astype(F32))
        first = scal[4] + group * Q
        position = first + at[:, 0:1]
        segment = segment_of(scal, position)
        marks = {
            CARRIES: segment == segment_of(scal, first - 1),
            ENDING: segment == segment_of(scal, first + Q - 1),
            VALID: position < scal[0] + scal[1] + scal[2] + scal[3],
        }
        for j in range(1, 4):
            marks[EARLIER + j] = segment == segment_of(scal, position - j)
            marks[LATER + j] = segment == segment_of(scal, position + j)
        member = jnp.where(lane == SEGMENT, segment.astype(F32), 0.0)
        for mark, found in marks.items():
            member = jnp.where(lane == mark, found.astype(F32), member)
        member = jnp.where(lane < LOG, step, member)
        member = jnp.where((lane >= LOG) & (lane < MARK), pltpu.roll(summed, LOG, 1), member)
        member = jnp.where(lane >= RISE, pltpu.roll(sigmoid(raw), RISE, 1), member)
        cols[...] = member
        across = member.T
        rows[0:LOG, :] = across[LOG:MARK]
        rows[LOG : LOG + 8, :] = across[SEGMENT : SEGMENT + 8]
        total_out[pl.ds(pl.multiple_of(k * 8, 8), 8), :] = running[...]
        running[...] = running[...] + summed[Q - 1 : Q, :]

        follow(group, ext, halo, group_of(shared, k)[...])
        pre = conv_before_act(ext, taps, cols)
        act = pre * sigmoid(pre)
        bc[...] = act.astype(BF16)
        bct[...] = jnp.concatenate(
            [act[:, m * STATE : (m + 1) * STATE].T for m in range(width // STATE)], axis=0
        ).astype(BF16)

    loop(subs, body)


def states_kernel(
    subs, head, scal, raw, halo, taps, cols_in, bct_in, total, act_out, slope_out, states, final,
    through, ext, state,
):
    channels = raw.shape[1]

    @pl.when(pl.program_id(0) == 0)
    def _():
        state[...] = jnp.zeros_like(state)

    def body(k):
        group = pl.program_id(0) * subs + k
        cols, bct = group_of(cols_in, k), lane_group_of(bct_in, k)
        follow(group, ext, halo, group_of(raw, k)[...])
        pre = conv_before_act(ext, taps, cols)
        gate = sigmoid(pre)
        act = (pre * gate).astype(BF16)
        group_of(act_out, k)[...] = act
        group_of(slope_out, k)[...] = (gate * (1.0 + pre * (1.0 - gate))).astype(BF16)
        summed = spread_heads(cols[...], LOG + head, channels)
        last = summed[Q - 1 : Q, :]
        tails = jnp.exp2(last - summed) * cols[:, ENDING : ENDING + 1]
        scaled = (act.astype(F32) * spread_heads(cols[...], STEP + head, channels)).astype(BF16)
        fresh = dot(bct[:STATE, :], (scaled.astype(F32) * tails).astype(BF16))
        states[k] = state[...].astype(BF16)
        state[...] = state[...] * (jnp.exp2(last) * kept(scal, group)) + fresh

    loop(subs, body)

    @pl.when(pl.program_id(0) == pl.num_programs(0) - 1)
    def _():
        final[...] = state[...]
        at = (subs - 1) * 8
        ended = total[at : at + 8, :] + pltpu.roll(cols_in[subs * Q - 8 : subs * Q, :], 128 - LOG, 1)[7:8]
        through[...] = jnp.exp2(spread_heads(ended, head, channels)) * reaches(
            scal, pl.num_programs(0) * subs
        )


def total_share(scal, group, head, total, k, channels):
    here = total[pl.ds(pl.multiple_of(k * 8, 8), 8), :]
    return jnp.exp2(spread_heads(here, head, channels))[0:1] * reaches(scal, group)


def scan_kernel(
    subs, head, scal, act_in, bc_in, cols_in, rows_in, total, gate_in, back_in, states, start, taps,
    scanned_out, stats_out,
):
    channels = act_in.shape[1]

    def body(k):
        group = pl.program_id(0) * subs + k
        act, bc, cols = group_of(act_in, k), group_of(bc_in, k), group_of(cols_in, k)
        gate, back, rows = group_of(gate_in, k), group_of(back_in, k), rows_in.at[k]
        scanned = group_of(scanned_out, k)
        b_map, c_map = bc[:, :STATE], bc[:, STATE:]
        scores = dot(c_map, b_map, NT)
        allowed = triangle(cols, rows, False)
        carries = cols[:, CARRIES : CARRIES + 1]
        share = total_share(scal, group, head, total, k, channels)
        state = (states[k].astype(F32) + share * start[...]).astype(BF16)
        outside = dot(c_map, state)
        squares = jnp.zeros((Q, 2 * HEAD), F32)
        inner = jnp.zeros((Q, 2 * HEAD), F32)
        for p in range(channels // (2 * HEAD)):
            part = slice(2 * HEAD * p, 2 * HEAD * (p + 1))
            weights = []
            columns = []
            for h in (head + 2 * p, head + 2 * p + 1):
                column = jnp.broadcast_to(cols[:, LOG + h : LOG + h + 1], (Q, Q))
                columns.append(column)
                decay = jnp.exp2(column + (allowed - rows[h : h + 1, :]))
                weights.append((decay * scores).astype(BF16))
            summed = jnp.where(in_first(Q), columns[0], columns[1])
            member = act[:, part].astype(F32)
            scaled = (member * pair_of(cols[...], STEP + head + 2 * p)).astype(BF16)
            result = dot(jnp.concatenate(weights, axis=1), stacked_heads(scaled))
            result = result + outside[:, part] * (jnp.exp2(summed) * carries)
            scanned[:, part] = result
            mixed_heads = result + taps[6:7, part] * member
            raw = gate[:, part].astype(F32)
            gated = mixed_heads * (raw * sigmoid(raw))
            squares = squares + gated * gated
            inner = inner + back[:, part].astype(F32) * taps[5:6, part] * gated
        squares = jnp.sum(squares, axis=1, keepdims=True)
        inner = jnp.sum(inner, axis=1, keepdims=True) * cols[:, VALID : VALID + 1]
        lane = lax.broadcasted_iota(jnp.int32, (Q, Q), 1)
        both = jnp.where(lane == 0, squares, jnp.where(lane == 1, inner, 0.0))
        lane_group_of(stats_out, k)[...] = both.T[:8]

    loop(subs, body)


def gate_back_kernel(
    subs, head, inner_channels, scal, scanned_in, act_in, gate_in, back_in, stats_in, bct_in, cols_in,
    total, taps, mixed_out, low_gate_out, back_heads_out, reach, sums,
):
    channels = act_in.shape[1]

    @pl.when(pl.program_id(0) == 0)
    def _():
        reach[...] = jnp.zeros_like(reach)
        sums[...] = jnp.zeros_like(sums)

    def body(k):
        group = pl.program_id(0) * subs + k
        scanned, act, gate = group_of(scanned_in, k), group_of(act_in, k), group_of(gate_in, k)
        back, cols, stats = group_of(back_in, k), group_of(cols_in, k), lane_group_of(stats_in, k)
        mixed, low_gate = group_of(mixed_out, k), group_of(low_gate_out, k)
        back_heads, bct = group_of(back_heads_out, k), lane_group_of(bct_in, k)
        row = lax.broadcasted_iota(jnp.int32, (8, Q), 0)
        inverse_row = lax.rsqrt(stats[...] / inner_channels + EPS)
        both = jnp.concatenate(
            [jnp.where(row == 0, inverse_row, stats[...]), jnp.zeros((Q - 8, Q), F32)], axis=0
        ).T
        inverse, inner = both[:, 0:1], both[:, 1:2]
        valid, carries = cols[:, VALID : VALID + 1], cols[:, CARRIES : CARRIES + 1]
        slope = inverse * inverse * inverse * inner * valid / inner_channels
        inverse_valid = inverse * valid
        gradients = []
        for p in range(channels // (2 * HEAD)):
            part = slice(2 * HEAD * p, 2 * HEAD * (p + 1))
            member = act[:, part].astype(F32)
            mixed_heads = scanned[:, part] + taps[6:7, part] * member
            raw = gate[:, part].astype(F32)
            share = sigmoid(raw)
            opened = raw * share
            gated = mixed_heads * opened
            gain = taps[5:6, part]
            mixed[:, part] = (gated * inverse_valid * gain).astype(BF16)
            scaled_back = back[:, part].astype(F32) * inverse_valid
            gradient = scaled_back * gain - gated * slope
            low_gate[:, part] = (gradient * mixed_heads * (share + opened * (1.0 - share))).astype(BF16)
            low = (gradient * opened).astype(BF16)
            back_heads[:, part] = low
            wide = low.astype(F32)
            sums[0:1, part] = sums[0:1, part] + jnp.sum(scaled_back * gated, axis=0, keepdims=True)
            sums[1:2, part] = sums[1:2, part] + jnp.sum(wide * member, axis=0, keepdims=True)
            entered = jnp.exp2(pair_of(cols[...], LOG + head + 2 * p)) * carries
            gradients.append((wide * entered).astype(BF16))
        share = total_share(scal, group, head, total, k, channels)
        reach[...] = reach[...] + share * dot(bct[STATE:, :], jnp.concatenate(gradients, axis=1))

    loop(subs, body)


def first_sent_back(scal, later, taps):
    row = lax.broadcasted_iota(jnp.int32, (16, 1), 0)
    out = jnp.zeros((16, later.shape[1]), F32)
    for back in range(1, 4):
        at = scal[4] - back
        extra = jnp.zeros((1, later.shape[1]), F32)
        for j in range(back, 4):
            same = same_segment(scal, at, at + j)
            extra = extra + same * taps[3 - j : 4 - j, :] * later[j - back : j - back + 1, :]
        out = jnp.where(row == 16 - back, extra, out)
    return out


def scan_back_kernel(
    subs, head, scal, act_in, slope_in, heads_in, scanned_in, raw, before, halo, taps, picks, bc_in,
    bct_in, cols_in, rows_in, total, head_rows, states, start, leaving, low_out, back_bc_out,
    low_rate_out, sums, head_out, first_rows, last_rows, ext, back_ext, back_state, difference,
):
    turn = pl.program_id(0)
    turns = pl.num_programs(0) - 1
    channels = act_in.shape[1]

    @pl.when(turn == 0)
    def _():
        back_state[...] = leaving[...]
        back_ext[Q : Q + 8, :] = jnp.zeros_like(back_ext[Q : Q + 8, :])
        sums[...] = jnp.zeros_like(sums)
        head_out[...] = jnp.zeros_like(head_out)

    def body(count):
        k = subs - 1 - count
        group = (turns - 1 - turn) * subs + k
        act, slope, back_heads = group_of(act_in, k), group_of(slope_in, k), group_of(heads_in, k)
        scanned, bc, cols = group_of(scanned_in, k), group_of(bc_in, k), group_of(cols_in, k)
        bct, rows, back_bc = lane_group_of(bct_in, k), rows_in.at[k], group_of(back_bc_out, k)
        b_map, c_map = bc[:, :STATE], bc[:, STATE:]
        scores = dot(b_map, c_map, NT)
        allowed = triangle(cols, rows, True)
        carries, ending = cols[:, CARRIES : CARRIES + 1], cols[:, ENDING : ENDING + 1]
        share = total_share(scal, group, head, total, k, channels)
        state = states[k].astype(F32) + share * start[...]
        state_low = state.astype(BF16)
        leaving_low = back_state[...].astype(BF16)
        from_state = dot(b_map, leaving_low)
        back_scores = jnp.zeros((Q, Q), F32)
        into_state, out_of_state, passed, products = [], [], [], []
        for p in range(channels // (2 * HEAD)):
            part = slice(2 * HEAD * p, 2 * HEAD * (p + 1))
            low = back_heads[:, part]
            wide = low.astype(F32)
            member = act[:, part].astype(F32)
            step = pair_of(cols[...], STEP + head + 2 * p)
            scaled = (member * step).astype(BF16)
            back_weights = dot(stacked_heads(scaled), low, NT)
            weights, columns = [], []
            for m, h in enumerate((head + 2 * p, head + 2 * p + 1)):
                column = jnp.broadcast_to(cols[:, LOG + h : LOG + h + 1], (Q, Q))
                columns.append(column)
                decay = jnp.exp2((rows[h : h + 1, :] + allowed) - column)
                weights.append((decay * scores).astype(BF16))
                back_scores = back_scores + decay * back_weights[m * Q : (m + 1) * Q]
            summed = jnp.where(in_first(Q), columns[0], columns[1])
            last = summed[Q - 1 : Q, :]
            tails = jnp.exp2(last - summed) * ending
            back_scaled = dot(jnp.concatenate(weights, axis=1), stacked_heads(low))
            scaled_wide = scaled.astype(F32)
            from_end = tails * from_state[:, part]
            difference[:, part] = wide * scanned[:, part] - scaled_wide * back_scaled
            passed.append((scaled_wide * from_end).astype(BF16))
            back_scaled = back_scaled + from_end
            into_state.append((scaled_wide * tails).astype(BF16))
            out_of_state.append((wide * (jnp.exp2(summed) * carries)).astype(BF16))
            products.append((back_scaled * member).astype(BF16))
            back_act = back_scaled * step + taps[6:7, part] * wide
            back_ext[0:Q, part] = back_act * slope[:, part].astype(F32)
        into_state = jnp.concatenate(into_state, axis=1)
        out_of_state = jnp.concatenate(out_of_state, axis=1)
        back_b = dot(back_scores.astype(BF16), c_map) + dot(into_state, leaving_low, NT)
        back_c = dot(back_scores.T.astype(BF16), b_map) + dot(out_of_state, state_low, NT)
        back_bc[:, :STATE] = back_b
        back_bc[:, STATE:] = back_c

        whole_group = spread_heads(cols[Q - 1 : Q, :], LOG + head, channels)
        kept_state = back_state[...] * (jnp.exp2(whole_group) * kept(scal, group))
        back_state[...] = kept_state + dot(bct[STATE:, :], out_of_state)
        crossing = jnp.sum(kept_state * state, axis=0, keepdims=True)
        difference[Q - 1 : Q, :] = difference[Q - 1 : Q, :] + crossing

        product = dot(jnp.concatenate(products, axis=1), picks[...])
        at = lax.broadcasted_iota(jnp.int32, (Q, Q), 0)
        lane = lax.broadcasted_iota(jnp.int32, (Q, Q), 1)
        before_it = dot(jnp.concatenate(passed, axis=1), picks[...])
        back_logs = in_order(split_sum(difference[...], picks[...]), at <= lane) + dot(
            (at > lane).astype(BF16), before_it.astype(BF16)
        )
        decays = jnp.where(lane < LOG, back_logs * head_rows[1:2, :], 0.0)
        back_rate = (product + decays) * pltpu.roll(cols[...], 128 - RISE, 1)
        back_rate = jnp.where(lane < LOG, back_rate, 0.0)
        group_of(low_rate_out, k)[...] = back_rate.astype(BF16)
        head_out[0:1, :] = head_out[0:1, :] + jnp.sum(back_rate, axis=0, keepdims=True)
        head_out[1:2, :] = head_out[1:2, :] + jnp.sum(decays * cols[...], axis=0, keepdims=True)

        conv_back(turn, k, ext, back_ext, raw, before, halo, taps, cols, group_of(low_out, k), sums,
                  first_rows, last_rows, group)

    @pl.when(turn < turns)
    def _():
        loop(subs, body)

    @pl.when(turn == turns)
    def _():
        low_rate_out[...] = jnp.zeros_like(low_rate_out)
        low_out[...] = jnp.zeros_like(low_out)
        low_out[0:16, :] = first_sent_back(scal, first_rows, taps).astype(BF16)


def conv_back(
    turn, k, ext, back_ext, raw, before, halo, taps, cols, low, sums, first_rows, last_rows, group
):
    start = pl.multiple_of(jnp.maximum(k * Q - 16, 0), 16)
    earlier = jnp.where(group == 0, halo[...], before[...])
    earlier = jnp.where(k == 0, earlier, raw[pl.ds(start, 16), :])
    ext[0:8, :] = earlier[8:16].astype(F32)
    ext[8 : 8 + Q, :] = group_of(raw, k)[...].astype(F32)
    now = back_ext[0:Q, :]
    sums[3:4, :] = sums[3:4, :] + jnp.sum(now * ext[8 : 8 + Q, :], axis=0, keepdims=True)
    sums[4:5, :] = sums[4:5, :] + jnp.sum(now, axis=0, keepdims=True)
    total = now * taps[3:4, :]
    for j in range(1, 4):
        tap = slice(3 - j, 4 - j)
        earlier = ext[8 - j : 8 - j + Q, :] * cols[:, EARLIER + j : EARLIER + j + 1]
        sums[tap, :] = sums[tap, :] + jnp.sum(now * earlier, axis=0, keepdims=True)
        later = back_ext[j : j + Q, :] * cols[:, LATER + j : LATER + j + 1]
        total = total + later * taps[tap, :]
    low[...] = total.astype(BF16)

    @pl.when((turn == 0) & (k == raw.shape[0] // Q - 1))
    def _():
        last_rows[...] = total[Q - 8 : Q, :]

    back_ext[Q : Q + 8, :] = back_ext[0:8, :]
    first_rows[...] = back_ext[0:8, :]


def shared_back_kernel(
    subs, scal, back_bc, back_more, raw, before, halo, taps, cols_in, low_out, sums, first_rows,
    last_rows, ext, back_ext,
):
    turn = pl.program_id(0)
    turns = pl.num_programs(0) - 1

    @pl.when(turn == 0)
    def _():
        back_ext[Q : Q + 8, :] = jnp.zeros_like(back_ext[Q : Q + 8, :])
        sums[...] = jnp.zeros_like(sums)

    def body(count):
        k = subs - 1 - count
        group = (turns - 1 - turn) * subs + k
        cols = group_of(cols_in, k)
        start = pl.multiple_of(jnp.maximum(k * Q - 16, 0), 16)
        earlier = jnp.where(group == 0, halo[...], before[...])
        earlier = jnp.where(k == 0, earlier, raw[pl.ds(start, 16), :])
        ext[0:8, :] = earlier[8:16].astype(F32)
        ext[8 : 8 + Q, :] = group_of(raw, k)[...].astype(F32)
        pre = conv_before_act(ext, taps, cols)
        gate = sigmoid(pre)
        back = group_of(back_bc, k)[...] + group_of(back_more, k)[...]
        back_ext[0:Q, :] = back * (gate * (1.0 + pre * (1.0 - gate)))
        conv_back(turn, k, ext, back_ext, raw, before, halo, taps, cols, group_of(low_out, k), sums,
                  first_rows, last_rows, group)

    @pl.when(turn < turns)
    def _():
        loop(subs, body)

    @pl.when(turn == turns)
    def _():
        low_out[...] = jnp.zeros_like(low_out)
        low_out[0:16, :] = first_sent_back(scal, first_rows, taps).astype(BF16)


def joined(scal, low, later, last_rows, taps, rows):
    sent = []
    for back in range(3, 0, -1):
        at = scal[4] + rows - back
        extra = jnp.zeros_like(later[0])
        for j in range(back, 4):
            extra = extra + same_segment(scal, at, at + j) * taps[3 - j] * later[j - back]
        sent.append(extra)
    out = last_rows + jnp.concatenate([jnp.zeros((5, later.shape[1]), F32), jnp.stack(sent)])
    return lax.dynamic_update_slice(low, out.astype(BF16), (rows - 8, 0))


def split_blocks(member, count):
    return jnp.split(member, count, axis=0)


def chip_rows_kernel(tiles, scal, own, other, out):
    mine = pl.program_id(0) // tiles == scal[0]
    out[...] = jnp.where(mine, own[...], other[...])


def normed_rows_kernel(tiles, scal, own, other, halo, gain, out):
    def normed(member):
        wide = member.astype(F32)
        inverse = lax.rsqrt(jnp.mean(wide * wide, axis=1, keepdims=True) + EPS)
        return (wide * inverse * gain[...]).astype(BF16)

    step = pl.program_id(0)

    @pl.when(step < 2 * tiles)
    def _():
        out[...] = normed(jnp.where(step // tiles == scal[0], own[...], other[...]))

    @pl.when(step == 2 * tiles)
    def _():
        out[...] = jnp.zeros_like(out)
        out[0:16, :] = normed(halo[...])


def chip_rows(core, own, other, halo=None, gain=None):
    rows, width = own.shape
    tile = min(512, rows)
    tiles = rows // tile

    def at(first):
        return pl.BlockSpec((tile, width), lambda i, s: (jnp.clip(i - first(s) * tiles, 0, tiles - 1), 0))

    specs = [at(lambda s: s[0]), at(lambda s: 1 - s[0])]
    args = [core.reshape(1).astype(jnp.int32), own, other]
    body, extra = partial(chip_rows_kernel, tiles), 0
    if gain is not None:
        body, extra = partial(normed_rows_kernel, tiles), 1
        specs += [whole(halo.shape), whole((1, width))]
        args += [halo, gain.reshape(1, width)]
    return call(
        body,
        2 * tiles + extra,
        specs,
        [pl.BlockSpec((tile, width), lambda i, s: (i, 0))],
        [shape_of((2 * rows + extra * Q, width), BF16)],
        [],
        "chip_rows",
        rows * width * 8,
        tuple(args),
    )[0]


def many_dots_kernel(dims, scal, *refs):
    count = len(dims)
    out = refs[2 * count]
    total = dot(refs[0][...], refs[count][...], dims[0])
    for k in range(1, count):
        total = total + dot(refs[k][...], refs[count + k][...], dims[k])
    out[...] = total.astype(out.dtype)


def call(body, grid, in_specs, out_specs, out_shape, scratch, name, flops, args):
    moved = sum(a.size * a.dtype.itemsize for a in args) + sum(
        int(np.prod(o.shape)) * np.dtype(o.dtype).itemsize for o in out_shape
    )
    return pl.pallas_call(
        body,
        grid_spec=pltpu.PrefetchScalarGridSpec(
            num_scalar_prefetch=1,
            grid=(grid,),
            in_specs=in_specs,
            out_specs=out_specs,
            scratch_shapes=scratch,
        ),
        out_shape=out_shape,
        compiler_params=pltpu.CompilerParams(vmem_limit_bytes=VMEM_LIMIT),
        cost_estimate=pl.CostEstimate(flops=10**6, bytes_accessed=10**5, transcendentals=0),
        name=name,
    )(*args)


def whole(shape):
    return pl.BlockSpec(shape, lambda i, s: tuple(0 for _ in shape))


def after(member, *deps):
    return lax.optimization_barrier((member, *deps))[0]


class Order:
    def __init__(self):
        self.last = None

    def hold(self, member):
        return member if self.last is None else after(member, self.last)

    def holds(self, members):
        members = [self.hold(m) for m in members]
        self.last = after(self.last, *members)
        return members

    def done(self, member):
        self.last = member
        return member


def shape_of(shape, dtype):
    return jax.ShapeDtypeStruct(shape, dtype)


def many_dots(offset_rows, lefts, rights, dims, rows, dtype, name):
    tile = min(256, rows)
    columns = rights[0].shape[0 if dims[0] == NT else 1]
    scal = (offset_rows // tile).reshape(1).astype(jnp.int32)
    flops = 2 * rows * columns * sum(a.shape[1] for a in lefts)
    return call(
        partial(many_dots_kernel, tuple(dims)),
        rows // tile,
        [pl.BlockSpec((tile, a.shape[1]), lambda i, s: (s[0] + i, 0)) for a in lefts]
        + [whole(b.shape) for b in rights],
        [pl.BlockSpec((tile, columns), lambda i, s: (i, 0))],
        [shape_of((rows, columns), dtype)],
        [],
        name,
        flops,
        (scal, *lefts, *rights),
    )[0]


def solution(mesh):
    tensor = mesh.shape["tensor"]
    copies = mesh.shape["dp"]
    ny = tensor // 2
    nx = ny if copies % ny == 0 else 1
    nz = copies // nx

    def from_y(member, shift):
        pairs = [((((y + shift) % ny) * 2 + c), y * 2 + c) for y in range(ny) for c in range(2)]
        return lax.ppermute(member, "tensor", pairs)

    def next_y(member, step):
        pairs = [
            ((y - step) * 2 + c, y * 2 + c)
            for y in range(ny)
            for c in range(2)
            if 0 <= y - step < ny
        ]
        return lax.ppermute(member, "tensor", pairs)

    def from_core(member):
        return lax.ppermute(member, "tensor", [(t ^ 1, t) for t in range(tensor)])

    def from_x(member, shift):
        pairs = [(z * nx + (x + shift) % nx, z * nx + x) for z in range(nz) for x in range(nx)]
        return lax.ppermute(member, "dp", pairs)

    def from_z(member, shift):
        pairs = [(((z + shift) % nz) * nx + x, z * nx + x) for z in range(nz) for x in range(nx)]
        return lax.ppermute(member, "dp", pairs)

    def sum_rows(member):
        bit = 1
        while bit < copies:
            member = member + lax.ppermute(member, "dp", [(d ^ bit, d) for d in range(copies)])
            bit *= 2
        return member

    def sum_row_group(member):
        bit = 1
        while bit < tensor:
            member = member + lax.ppermute(member, "tensor", [(t ^ bit, t) for t in range(tensor)])
            bit *= 2
        return member

    def ways_x(member, x):
        kept = lax.dynamic_index_in_dim(member, x, 1, keepdims=False)
        got = []
        for k in range(1, nx):
            sent = lax.dynamic_index_in_dim(member, (x + k) % nx, 1, keepdims=False)
            got.append(from_x(sent.astype(BF16), nx - k))
        return [kept] + got

    def ways_z(member, z, bit):
        parts = member.reshape(-1, 2, *member.shape[-2:])
        own = (z // bit) % 2
        kept = lax.dynamic_index_in_dim(parts, own, 1, keepdims=False)
        sent = lax.dynamic_index_in_dim(parts, 1 - own, 1, keepdims=False)
        pairs = [((p ^ bit) * nx + x, p * nx + x) for p in range(nz) for x in range(nx)]
        return [kept, lax.ppermute(sent.astype(BF16), "dp", pairs)]

    def summed(parts):
        total = parts[0].astype(F32)
        for part in parts[1:]:
            total = total + part.astype(F32)
        return total

    def gather_rows(member, x, z):
        member = member[None]
        bit = nz // 2
        while bit >= 1:
            pairs = [((p ^ bit) * nx + q, p * nx + q) for p in range(nz) for q in range(nx)]
            other = lax.ppermute(member, "dp", pairs)
            high = (z // bit) % 2 == 1
            member = jnp.stack([jnp.where(high, other, member), jnp.where(high, member, other)], axis=1)
            member = member.reshape(-1, *member.shape[2:])
            bit //= 2
        parts = jnp.stack([member] + [from_x(member, k) for k in range(1, nx)])
        parts = [lax.dynamic_index_in_dim(parts, (k - x) % nx, 0, False) for k in range(nx)]
        return jnp.stack(parts, axis=1).reshape(-1, member.shape[-1])

    def shards(
        tokens, lengths, norm_gain, w_gate, w_value, w_shared, w_rate, conv_value, value_bias,
        conv_shared, shared_bias, rate_bias, decay_log, skip_gain, mix_gain, w_out, cotangent,
    ):
        index = lax.axis_index("tensor")
        y, core = index // 2, index % 2
        dp = lax.axis_index("dp")
        z, x = dp // nx, dp % nx
        own_rows, width = tokens.shape
        rows = 2 * own_rows
        groups = rows // Q
        channels = w_gate.shape[1]
        heads = w_rate.shape[1]
        inner = channels * tensor
        own_start = core * own_rows
        lanes = 128
        maps = w_shared.shape[1]
        blocks = range(ny)

        halo_one = next_y(tokens[own_rows - 16 :], 1)
        tokens_other = from_core(tokens)
        halo = jnp.where(core == 1, halo_one, from_core(halo_one))
        packed = jnp.concatenate(
            [
                conv_value.T,
                value_bias[None],
                mix_gain[None],
                jnp.repeat(skip_gain, HEAD)[None],
                jnp.concatenate([rate_bias, decay_log, jnp.zeros((channels - 2 * heads,), F32)])[None],
                w_rate.T.astype(F32).reshape(-1, channels),
            ],
            axis=0,
        )
        packed = after(packed, halo_one)
        packs = [packed] + [from_y(packed, j) for j in range(1, ny)]

        order = Order()

        def own_part(weight):
            part = weight.shape[0] // nx
            return lax.dynamic_slice(weight, (x * part, 0), (part, weight.shape[1]))

        def fetched(member, dep):
            member = after(member, dep)
            return [from_y(member, j) for j in range(1, ny)]

        def from_parts(weight, pieces):
            part = weight.shape[0] // nx
            found = [weight]
            for piece in pieces:
                full = lax.dynamic_update_slice(weight, piece, (x * part, 0))
                for k in range(1, nx):
                    got = from_x(piece, k)
                    full = lax.dynamic_update_slice(full, got, ((x + k) % nx * part, 0))
                found.append(full)
            return found

        back_other = from_core(after(cotangent, tokens_other))
        value_parts = fetched(own_part(w_value), packs[-1])
        rates = [p[8:].reshape(heads, width).astype(BF16) for p in packs]
        packs = [p[:8] for p in packs]
        all_rates = jnp.concatenate(rates + [jnp.zeros((lanes - ny * heads, width), BF16)], axis=0)
        w_small = jnp.concatenate([w_shared, all_rates.T], axis=1)
        fill = jnp.zeros((lanes - ny * heads,), F32)
        head_rows = jnp.concatenate(
            [
                jnp.concatenate([p[7, :heads] for p in packs] + [fill])[None],
                jnp.concatenate([-jnp.exp(p[7, heads : 2 * heads]) for p in packs] + [fill])[None],
                jnp.zeros((6, lanes), F32),
            ],
            axis=0,
        )
        shared_taps = jnp.concatenate(
            [conv_shared.T, shared_bias[None], jnp.zeros((3, maps), F32)], axis=0
        )
        scal = jnp.concatenate([lengths[0], (y * rows).reshape(1)]).astype(jnp.int32)

        residual = tokens.astype(F32)
        inverse_in = lax.rsqrt(jnp.mean(residual * residual, axis=1, keepdims=True) + EPS)
        normed = order.done(chip_rows(core, tokens, tokens_other, halo, norm_gain))
        step_rows = min(STEP_ROWS, rows)
        subs = step_rows // Q
        turns = rows // step_rows

        def up(columns):
            return pl.BlockSpec((step_rows, columns), lambda i, s: (i, 0))

        def up_lanes(depth):
            return pl.BlockSpec((depth, step_rows), lambda i, s: (0, i))

        def up_groups(*shape):
            return pl.BlockSpec((subs, *shape), lambda i, s: (i, 0, 0))

        def downward(i):
            return jnp.maximum(turns - 1 - i, 0)

        def down(columns):
            return pl.BlockSpec((step_rows, columns), lambda i, s: (downward(i), 0))

        def down_extended(columns):
            return pl.BlockSpec(
                (step_rows, columns), lambda i, s: (jnp.where(i == turns, turns, downward(i)), 0)
            )

        def down_lanes(depth):
            return pl.BlockSpec((depth, step_rows), lambda i, s: (0, downward(i)))

        def down_groups(*shape):
            return pl.BlockSpec((subs, *shape), lambda i, s: (downward(i), 0, 0))

        def down_before(columns):
            return pl.BlockSpec(
                (16, columns), lambda i, s: (jnp.maximum(downward(i) * (step_rows // 16) - 1, 0), 0)
            )

        def behind_rows(columns):
            return pl.BlockSpec((16, columns), lambda i, s: (rows // 16, 0))

        up_total = pl.BlockSpec((subs * 8, lanes), lambda i, s: (i, 0))
        down_total = pl.BlockSpec((subs * 8, lanes), lambda i, s: (downward(i), 0))
        row_depth = LOG + 8
        extended = rows + Q

        raw_values = [order.done(dot(order.hold(normed), w_value).astype(BF16))]
        small = order.done(dot(order.hold(normed), w_small))
        value_parts = order.holds(value_parts)
        values = from_parts(w_value, value_parts)
        gate_parts = fetched(own_part(w_gate), value_parts[-1])
        raw_shared = small[:, :maps].astype(BF16)
        bc, bct, cols, across, total = call(
            partial(prepare_kernel, subs),
            turns,
            [up(maps), up(lanes), behind_rows(maps), whole((8, maps)), whole((8, lanes))],
            [up(maps), up_lanes(maps), up(lanes), up_groups(row_depth, Q), up_total],
            [
                shape_of((rows, maps), BF16),
                shape_of((maps, rows), BF16),
                shape_of((rows, lanes), F32),
                shape_of((groups, row_depth, Q), F32),
                shape_of((groups * 8, lanes), F32),
            ],
            [pltpu.VMEM((Q + 8, maps), F32), pltpu.VMEM((8, lanes), F32)],
            "prepare",
            rows * 2000,
            (scal, raw_shared, small[:, maps:], raw_shared, shared_taps, head_rows),
        )
        order.done(total)

        flops_scan = rows * channels * 2 * 600
        acts, slopes, states, finals, throughs = [], [], [], [], []
        for j in blocks:
            if j == 1:
                gate_parts = order.holds(gate_parts)
                gates = from_parts(w_gate, gate_parts)
                out_parts = fetched(own_part(w_out), gate_parts[-1])
                values = [w_value] + [order.hold(v) for v in values[1:]]
            if j > 0:
                raw_values.append(order.done(dot(order.hold(normed), values[j]).astype(BF16)))
            if j == 1:
                raw_gates = [order.done(dot(order.hold(normed), w_gate).astype(BF16))]
            raw = raw_values[j]
            act, slope, state, final, through = call(
                partial(states_kernel, subs, j * heads),
                turns,
                [
                    up(channels),
                    behind_rows(channels),
                    whole((8, channels)),
                    up(lanes),
                    up_lanes(maps),
                    up_total,
                ],
                [
                    up(channels),
                    up(channels),
                    up_groups(STATE, channels),
                    whole((STATE, channels)),
                    whole((8, channels)),
                ],
                [
                    shape_of((rows, channels), BF16),
                    shape_of((rows, channels), BF16),
                    shape_of((groups, STATE, channels), BF16),
                    shape_of((STATE, channels), F32),
                    shape_of((8, channels), F32),
                ],
                [pltpu.VMEM((Q + 8, channels), F32), pltpu.VMEM((STATE, channels), F32)],
                "states",
                flops_scan // 2,
                (scal, order.hold(raw), raw, packs[j], cols, bct, total),
            )
            order.done(final)
            if j == 0:
                back_rows = order.done(chip_rows(core, cotangent, order.hold(back_other)))
            acts.append(act)
            slopes.append(slope)
            states.append(state)
            finals.append(final)
            throughs.append(through)

        before = [(j + 1) % ny for j in blocks]
        behind = [(j - 1) % ny for j in blocks]
        starts = split_blocks(next_y(jnp.concatenate([finals[k] for k in before]), 1), ny)
        for _ in range(ny - 2):
            sent = [finals[k] + throughs[k][0:1] * starts[k] for k in before]
            starts = split_blocks(next_y(jnp.concatenate(sent), 1), ny)

        out_parts = order.holds(out_parts)
        outs = from_parts(w_out, out_parts)
        backs = [order.done(dot(order.hold(back_rows), w_out, NT).astype(BF16))]
        scans, stats = [], []
        for j in blocks:
            if j == 1:
                gates = [w_gate] + [order.hold(w) for w in gates[1:]]
                outs = [w_out] + [order.hold(w) for w in outs[1:]]
            if j > 0:
                raw_gates.append(order.done(dot(order.hold(normed), gates[j]).astype(BF16)))
                backs.append(order.done(dot(order.hold(back_rows), outs[j], NT).astype(BF16)))
            raw_gate, back = raw_gates[j], backs[j]
            scanned, stat = call(
                partial(scan_kernel, subs, j * heads),
                turns,
                [
                    up(channels),
                    up(maps),
                    up(lanes),
                    up_groups(row_depth, Q),
                    up_total,
                    up(channels),
                    up(channels),
                    up_groups(STATE, channels),
                    whole((STATE, channels)),
                    whole((8, channels)),
                ],
                [up(channels), up_lanes(8)],
                [shape_of((rows, channels), F32), shape_of((8, rows), F32)],
                [],
                "scan",
                flops_scan,
                (scal, order.hold(acts[j]), bc, cols, across, total, raw_gate, back, states[j], starts[j],
                 packs[j]),
            )
            scans.append(order.done(scanned))
            stats.append(stat)

        stat = sum(stats[1:], stats[0])
        stat = stat + from_core(stat)

        mixeds, low_gates, back_heads, reaching, gate_sums = ([None] * ny for _ in range(5))
        for j in blocks:
            mixed, low_gate, back_head, reach, sums = call(
                partial(gate_back_kernel, subs, j * heads, inner),
                turns,
                [
                    up(channels),
                    up(channels),
                    up(channels),
                    up(channels),
                    up_lanes(8),
                    up_lanes(maps),
                    up(lanes),
                    up_total,
                    whole((8, channels)),
                ],
                [up(channels)] * 3 + [whole((STATE, channels)), whole((8, channels))],
                [shape_of((rows, channels), BF16)] * 3
                + [shape_of((STATE, channels), F32), shape_of((8, channels), F32)],
                [],
                "gate_back",
                flops_scan // 2,
                (scal, scans[j], order.hold(acts[j]), raw_gates[j], backs[j], stat, bct, cols, total, packs[j]),
            )
            mixeds[j], low_gates[j], back_heads[j] = mixed, low_gate, back_head
            reaching[j], gate_sums[j] = order.done(reach), sums

        leavings = [next_y(reaching[k], -1) for k in behind]
        for _ in range(ny - 2):
            leavings = [next_y(reaching[k] + throughs[k][0:1] * leavings[k], -1) for k in behind]

        def scattered(member):
            return member.reshape(nz, nx, width // copies, member.shape[1])

        out_blocks, gate_blocks = [None] * ny, [None] * ny
        for j in range(1, ny):
            out_blocks[j] = order.done(dot(order.hold(back_rows), mixeds[j], TN).astype(BF16))
            out_blocks[j] = after(out_blocks[j], leavings[-1])
        out_got = [from_y(out_blocks[j], ny - j) for j in range(1, ny)]
        for j in reversed(blocks):
            gate_blocks[j] = order.done(dot(order.hold(normed[:rows]), low_gates[j], TN).astype(BF16))
        gate_ways = [ways_x(scattered(b), x) for b in gate_blocks]
        out_blocks[0] = order.done(dot(order.hold(back_rows), mixeds[0], TN).astype(BF16))
        ahead = (1 - core) * own_rows

        channel = np.arange(channels)
        low_values, back_bcs, low_rates, conv_sums, head_sums_ = [None] * ny, [], [], [None] * ny, []
        value_blocks = [None] * ny
        for j in reversed(blocks):
            picks = jnp.asarray(
                (np.arange(lanes)[None, :] == (j * heads + channel // HEAD)[:, None]), BF16
            )
            low, back_bc, low_rate, sums, head_out, first_rows, last_rows = call(
                partial(scan_back_kernel, subs, j * heads),
                turns + 1,
                [
                    down(channels),
                    down(channels),
                    down(channels),
                    down(channels),
                    down(channels),
                    down_before(channels),
                    behind_rows(channels),
                    whole((8, channels)),
                    whole((channels, lanes)),
                    down(maps),
                    down_lanes(maps),
                    down(lanes),
                    down_groups(row_depth, Q),
                    down_total,
                    whole((8, lanes)),
                    down_groups(STATE, channels),
                    whole((STATE, channels)),
                    whole((STATE, channels)),
                ],
                [
                    down_extended(channels),
                    down(maps),
                    down_extended(lanes),
                    whole((8, channels)),
                    whole((8, lanes)),
                    whole((8, channels)),
                    whole((8, channels)),
                ],
                [
                    shape_of((extended, channels), BF16),
                    shape_of((rows, maps), F32),
                    shape_of((extended, lanes), BF16),
                    shape_of((8, channels), F32),
                    shape_of((8, lanes), F32),
                    shape_of((8, channels), F32),
                    shape_of((8, channels), F32),
                ],
                [
                    pltpu.VMEM((Q + 8, channels), F32),
                    pltpu.VMEM((Q + 8, channels), F32),
                    pltpu.VMEM((STATE, channels), F32),
                    pltpu.VMEM((Q, channels), F32),
                ],
                "scan_back",
                flops_scan * 3,
                (scal, order.hold(acts[j]), slopes[j], back_heads[j], scans[j], raw_values[j], raw_values[j],
                 raw_values[j], packs[j], picks, bc, bct, cols, across, total, head_rows, states[j],
                 starts[j], leavings[j]),
            )
            low_values[j] = (order.done(low), first_rows, last_rows)
            if j == ny - 1:
                gate_rows = [summed([w[0]] + order.holds(w[1:])) for w in gate_ways]
                gate_got = [from_y(gate_rows[k].astype(BF16), ny - k) for k in range(1, ny)]
                order.done(gate_rows[0])
            if j > 0:
                value_blocks[j] = order.done(dot(order.hold(normed), low, TN).astype(BF16))
            if j == 1:
                value_got = [from_y(value_blocks[k], ny - k) for k in range(1, ny)]
                out_sum = summed([out_blocks[0]] + order.holds(out_got))
                out_ways = ways_x(scattered(out_sum), x)
                order.done(out_sum)
                out_sent = order.done(
                    many_dots(
                        ahead, [order.hold(m) for m in mixeds], outs, [NN] * ny, own_rows, BF16, "out_other"
                    )
                )
                out_other = from_core(out_sent)
            back_bcs.append(back_bc)
            low_rates.append(low_rate)
            conv_sums[j] = sums
            head_sums_.append(head_out)

        later = [member[1] for member in low_values]
        later = next_y(jnp.concatenate([later[k] for k in behind], axis=1), -1)
        back_bc = sum(back_bcs[1:], back_bcs[0])
        back_bc_other = from_core(back_bc)
        out_sum = summed([out_ways[0]] + order.holds(out_ways[1:]))
        out_ways = ways_z(out_sum, z, 1)
        order.done(out_sum)
        out_kept = order.done(
            many_dots(
                own_start, [order.hold(m) for m in mixeds], outs, [NN] * ny, own_rows, F32, "out_own"
            )
        )

        back_bc = order.hold(back_bc)
        low_shared, shared_sums, first_rows, last_rows = call(
            partial(shared_back_kernel, subs),
            turns + 1,
            [
                down(maps),
                down(maps),
                down(maps),
                down_before(maps),
                behind_rows(maps),
                whole((8, maps)),
                down(lanes),
            ],
            [down_extended(maps), whole((8, maps)), whole((8, maps)), whole((8, maps))],
            [
                shape_of((extended, maps), BF16),
                shape_of((8, maps), F32),
                shape_of((8, maps), F32),
                shape_of((8, maps), F32),
            ],
            [pltpu.VMEM((Q + 8, maps), F32), pltpu.VMEM((Q + 8, maps), F32)],
            "shared_back",
            rows * 2000,
            (scal, back_bc, back_bc_other, raw_shared, raw_shared, raw_shared, shared_taps, cols),
        )
        order.done(low_shared)
        later_shared = next_y(first_rows, -1)
        low_rate = sum(low_rates[1:], low_rates[0])
        half = maps // 2
        cut = lax.dynamic_slice(low_shared, (0, core * half), (extended, half))
        small_block = jnp.concatenate([cut, low_rate], axis=1)
        value_got = order.holds(value_got)
        value_sum = order.done(summed([dot(order.hold(normed), low_values[0][0], TN)] + value_got))
        late_ways = ways_x(scattered(value_sum), x)
        gate_sum = summed([gate_rows[0]] + order.holds(gate_got))
        gate_ways = ways_z(gate_sum, z, 1)
        out_ways = out_ways[:1] + order.holds(out_ways[1:])
        bit = 2
        while bit < nz:
            out_ways = ways_z(summed(out_ways), z, bit)
            bit *= 2
        order.done(gate_sum)
        small_block = order.done(dot(order.hold(normed), small_block, TN).astype(BF16))
        small_got = [from_y(small_block, ny - j) for j in range(1, ny)]

        later = order.holds([later])[0]
        low_values = [
            joined(scal, m[0], later[:, j * channels : (j + 1) * channels], m[2], packs[j], rows)
            for j, m in enumerate(low_values)
        ]
        low_shared = joined(scal, low_shared, later_shared, last_rows, shared_taps, rows)

        lefts = [low_rate] + low_gates + low_values
        rights = [all_rates] + gates + values
        sent = order.done(
            many_dots(
                ahead, [order.hold(m) for m in lefts], rights, [NN] + [NT] * (2 * ny), own_rows, BF16,
                "back_other",
            )
        )
        back_normed_other = from_core(sent)
        small_sum = small_block[:, :half].astype(F32)
        rate_sum = small_block[:, half : half + heads].astype(F32)
        late = summed(late_ways[:1] + order.holds(late_ways[1:]))
        late_ways = ways_z(late, z, 1)
        for j, got in enumerate(order.holds(small_got)):
            got = got.astype(F32)
            at = half + (ny - 1 - j) * heads
            small_sum = small_sum + got[:, :half]
            rate_sum = rate_sum + got[:, at : at + heads]
        fill = jnp.zeros((width, lanes - heads), F32)
        least = scattered(jnp.concatenate([small_sum, rate_sum, fill], axis=1))
        least_ways = ways_x(least, x)
        gate_ways = gate_ways[:1] + order.holds(gate_ways[1:])
        bit = 2
        while bit < nz:
            gate_ways = ways_z(summed(gate_ways), z, bit)
            bit *= 2
        order.done(late)
        lefts = [order.hold(low_shared)] + lefts
        rights = [w_shared] + rights
        kept = order.done(
            many_dots(
                own_start, [order.hold(m) for m in lefts], rights, [NT, NN] + [NT] * (2 * ny), own_rows, F32,
                "back_own",
            )
        )
        late_ways = late_ways[:1] + order.holds(late_ways[1:])
        least = summed(least_ways[:1] + order.holds(least_ways[1:]))
        least_ways = ways_z(least, z, 1)
        bit = 2
        while bit < nz:
            late_ways = ways_z(summed(late_ways), z, bit)
            bit *= 2
        order.done(least)
        block_out = (residual + out_kept + out_other.astype(F32)).astype(BF16)
        back_normed = order.hold(kept) + back_normed_other.astype(F32)
        grad_norm = jnp.sum(back_normed * residual * inverse_in, axis=0)
        scaled = back_normed * norm_gain
        tokens_grad = (
            cotangent.astype(F32)
            + scaled * inverse_in
            - residual
            * (inverse_in * inverse_in * inverse_in)
            * jnp.sum(scaled * residual, axis=1, keepdims=True)
            / width
        )

        order.done(tokens_grad)

        bit = 2
        while bit < nz:
            least_ways = ways_z(summed(least_ways[:1] + order.holds(least_ways[1:])), z, bit)
            bit *= 2
        grad_out = summed(out_ways).reshape(width // copies, channels).T
        grad_gate = summed(gate_ways).reshape(width // copies, channels)
        grad_value = summed(late_ways).reshape(width // copies, channels)
        least = summed(least_ways).reshape(width // copies, half + lanes)
        grad_rate = least[:, half : half + heads]
        part = gather_rows(least[:, :half].astype(BF16), x, z)
        other = from_core(part)
        grad_shared = jnp.where(
            core == 0, jnp.concatenate([part, other], axis=1), jnp.concatenate([other, part], axis=1)
        ).astype(F32)

        head_out = sum(head_sums_[1:], head_sums_[0])
        smalls = []
        for j in blocks:
            skip = gate_sums[j][1].reshape(heads, HEAD).sum(axis=1)
            own_heads = head_out[:2, j * heads : (j + 1) * heads].reshape(2 * heads)
            line = jnp.concatenate([skip, own_heads, jnp.zeros((channels - 3 * heads,), F32)])
            smalls.append(
                jnp.concatenate(
                    [conv_sums[j][:5], gate_sums[j][:1], line[None], jnp.zeros((1, channels), F32)]
                )
            )
        shared_sums = jnp.where(core == 0, shared_sums, 0.0)
        alls = jnp.concatenate([shared_sums, grad_norm.reshape(-1, maps)], axis=0)
        alls = sum_row_group(alls)
        own = smalls[0]
        for j in range(1, ny):
            own = own + order.hold(from_y(smalls[j], ny - j))
        both = jnp.concatenate([own.reshape(-1, lanes), alls.reshape(-1, lanes)], axis=0)
        both = sum_rows(both)
        own = both[: own.size // lanes].reshape(own.shape)
        alls = both[own.size // lanes :].reshape(alls.shape)
        return (
            block_out,
            tokens_grad,
            alls[8:].reshape(width),
            grad_gate,
            grad_value,
            grad_shared,
            grad_rate,
            own[:4].T,
            own[4],
            alls[:4].T,
            alls[4],
            own[6, heads : 2 * heads],
            own[6, 2 * heads : 3 * heads],
            own[6, :heads],
            own[5],
            grad_out,
        )

    in_specs = (
        P(("dp", "tensor"), None),
        P("dp", None),
        P(),
        P(None, "tensor"),
        P(None, "tensor"),
        P(),
        P(None, "tensor"),
        P("tensor", None),
        P("tensor"),
        P(),
        P(),
        P("tensor"),
        P("tensor"),
        P("tensor"),
        P("tensor"),
        P("tensor", None),
        P(("dp", "tensor"), None),
    )
    out_specs = (
        P(("dp", "tensor"), None),
        P(("dp", "tensor"), None),
        P(),
        P("dp", "tensor"),
        P("dp", "tensor"),
        P(),
        P("dp", "tensor"),
        P("tensor", None),
        P("tensor"),
        P(),
        P(),
        P("tensor"),
        P("tensor"),
        P("tensor"),
        P("tensor"),
        P("tensor", "dp"),
    )
    return jax.shard_map(shards, mesh=mesh, in_specs=in_specs, out_specs=out_specs, check_vma=False)
```

```python
from functools import partial

import jax
import jax.numpy as jnp
import numpy as np
from jax import lax
from jax.experimental import pallas as pl
from jax.experimental.pallas import tpu as pltpu
from jax.sharding import PartitionSpec as P

Q = 128
STATE = 128
HEAD = 64
EPS = 1e-05
LOG2E = 1.4426950408889634
NEVER = -1e30
F32 = jnp.float32
BF16 = jnp.bfloat16
HIGH = lax.Precision.HIGHEST
VMEM_LIMIT = 56 * 1024 * 1024
STEP_ROWS = 512
PACE = 1.15e9 * 1.0
TIMES = dict(
    chip_rows=7, prepare=10, states=13, scan=15, gate_back=16, scan_back=33, out_other=9, out_own=11,
    back_other=17, back_own=22, shared_back=10,
)
SCAN_LANES = False

NN = (((1,), (0,)), ((), ()))
NT = (((1,), (1,)), ((), ()))
TN = (((0,), (0,)), ((), ()))


def dot(a, b, dims=NN, precision=None):
    return lax.dot_general(a, b, dims, precision=precision, preferred_element_type=F32)


STEP, MARK, RISE = 0, 64, 96
CARRIES, ENDING, VALID, SEGMENT = MARK, MARK + 1, MARK + 2, MARK + 3
EARLIER, LATER = MARK + 3, MARK + 6
LOG = 32


def loop(count, body):
    def step(k, carry):
        body(k)
        return carry

    lax.fori_loop(0, count, step, 0, unroll=True)


def group_of(ref, k):
    return ref.at[pl.ds(pl.multiple_of(k * Q, Q), Q), :]


def lane_group_of(ref, k):
    return ref.at[:, pl.ds(pl.multiple_of(k * Q, Q), Q)]


def segment_of(scal, position):
    end = scal[0]
    count = (position >= end).astype(jnp.int32)
    for k in range(1, 4):
        end = end + scal[k]
        count = count + (position >= end).astype(jnp.int32)
    return count


def same_segment(scal, position, other):
    return (segment_of(scal, position) == segment_of(scal, other)).astype(F32)


def kept(scal, group):
    first = scal[4] + group * Q
    return same_segment(scal, first - 1, first + Q - 1)


def reaches(scal, group):
    return same_segment(scal, scal[4] + group * Q - 1, scal[4] - 1)


def triangle(cols, rows, flipped):
    first = lax.broadcasted_iota(jnp.int32, (Q, Q), 0)
    second = lax.broadcasted_iota(jnp.int32, (Q, Q), 1)
    ordered = (first <= second) if flipped else (first >= second)
    allowed = ordered & (cols[:, SEGMENT : SEGMENT + 1] == rows[0:1, :])
    return jnp.where(allowed, 0.0, NEVER)


def in_first(rows):
    return lax.broadcasted_iota(jnp.int32, (rows, 2 * HEAD), 1) < HEAD


def pair_of(columns, lane):
    rows = columns.shape[0]
    first = jnp.broadcast_to(columns[:, lane : lane + 1], (rows, 2 * HEAD))
    second = jnp.broadcast_to(columns[:, lane + 1 : lane + 2], (rows, 2 * HEAD))
    return jnp.where(in_first(rows), first, second)


def spread_heads(columns, lane, channels):
    return jnp.concatenate(
        [pair_of(columns, lane + 2 * p) for p in range(channels // (2 * HEAD))], axis=1
    )


def stacked_heads(member):
    first = in_first(member.shape[0])
    none = jnp.zeros_like(member)
    return jnp.concatenate([jnp.where(first, member, none), jnp.where(first, none, member)], axis=0)


def split_sum(member, picks):
    high = member.astype(BF16)
    rest = (member - high.astype(F32)).astype(BF16)
    return dot(high, picks) + dot(rest, picks)


def in_parts(member):
    lane = lax.broadcasted_iota(jnp.int32, member.shape, 1)
    member = jnp.where(lane < 32, member, 0.0)
    first = member.astype(BF16).astype(F32)
    rest = member - first
    second = rest.astype(BF16).astype(F32)
    return first + pltpu.roll(second, 32, 1) + pltpu.roll(rest - second, 64, 1)


def in_order(member, ordered):
    total = dot(ordered.astype(BF16), in_parts(member).astype(BF16))
    return total + pltpu.roll(total, 96, 1) + pltpu.roll(total, 64, 1)


def sigmoid(v):
    return 0.5 * jnp.tanh(0.5 * v) + 0.5


def shifts(marks, later):
    row = lax.broadcasted_iota(jnp.int32, (Q, Q), 0)
    column = lax.broadcasted_iota(jnp.int32, (Q, Q), 1)
    parts = []
    for j in range(1, 4):
        if later:
            parts.append(jnp.where(column == row + j, marks[j : j + 1, :], 0.0))
        else:
            parts.append(jnp.where(column == row - j, marks[3 + j : 4 + j, :], 0.0))
    return jnp.concatenate(parts, axis=0).astype(BF16)


def edge_shifts(scal, edge, later):
    row = lax.broadcasted_iota(jnp.int32, (16, 16), 0)
    column = lax.broadcasted_iota(jnp.int32, (16, 16), 1)
    at = edge + row - (16 if later else 0)
    other = edge + column - (0 if later else 16)
    same = segment_of(scal, at) == segment_of(scal, other)
    parts = [
        jnp.where(same & (other == (at + j if later else at - j)), 1.0, 0.0) for j in range(1, 4)
    ]
    return jnp.concatenate(parts, axis=0).astype(BF16)


def conv_before_act(scal, group, raw, halo, tail, taps, marks):
    current = raw[...]
    before = jnp.where(group == 0, halo[...], tail[...])
    moved = dot(shifts(marks, False), current)
    edge = dot(edge_shifts(scal, scal[4] + group * Q, False), before)
    total = current.astype(F32) * taps[3:4, :] + taps[4:5, :]
    first = jnp.zeros((16, current.shape[1]), F32)
    for j in range(1, 4):
        tap = taps[3 - j : 4 - j, :]
        total = total + moved[(j - 1) * Q : j * Q] * tap
        first = first + edge[(j - 1) * 16 : j * 16] * tap
    tail[...] = current[Q - 16 : Q]
    return jnp.concatenate([total[:16] + first, total[16:]], axis=0)


def prepare_kernel(
    subs, scal, shared, rates, halo, taps, head_rows, bc_out, bct_out, cols_out, logs_out, steps_out,
    marks_out, across_out, total_out, tail, running,
):
    @pl.when(pl.program_id(0) == 0)
    def _():
        running[...] = jnp.zeros_like(running)

    def body(k):
        group = pl.program_id(0) * subs + k
        bc, cols = group_of(bc_out, k), group_of(cols_out, k)
        bct, marks, across = lane_group_of(bct_out, k), marks_out.at[k], across_out.at[k]
        width = bc.shape[1]
        raw = group_of(rates, k)[...] + head_rows[0:1, :]
        step = jnp.maximum(raw, 0.0) + jnp.log1p(jnp.exp(-jnp.abs(raw)))
        scaled = step * (head_rows[1:2, :] * LOG2E)
        at = lax.broadcasted_iota(jnp.int32, (Q, Q), 0)
        lane = lax.broadcasted_iota(jnp.int32, (Q, Q), 1)
        summed = in_order(scaled, (at >= lane).astype(F32))
        parts = in_parts(summed)
        ones = (lane >= 96) & (lane < 99)
        group_of(logs_out, k)[...] = jnp.where(ones, 1.0, parts).astype(BF16)
        group_of(steps_out, k)[...] = in_parts(step).astype(BF16)
        turned = parts.T
        row = lax.broadcasted_iota(jnp.int32, (16, Q), 0)
        for h in range(across.shape[1] // Q):
            found = jnp.zeros((16, Q), F32)
            for m in range(3):
                found = jnp.where(row == m, -turned[32 * m + h : 32 * m + h + 1, :], found)
            across[:, h * Q : (h + 1) * Q] = found.astype(BF16)

        first = scal[4] + group * Q
        position = first + at[:, 0:1]
        segment = segment_of(scal, position)
        marked = {
            CARRIES: segment == segment_of(scal, first - 1),
            ENDING: segment == segment_of(scal, first + Q - 1),
            VALID: position < scal[0] + scal[1] + scal[2] + scal[3],
        }
        member = jnp.where(lane == SEGMENT, segment.astype(F32), 0.0)
        for mark, found in marked.items():
            member = jnp.where(lane == mark, found.astype(F32), member)
        member = jnp.where(lane < LOG, step, member)
        member = jnp.where((lane >= LOG) & (lane < MARK), pltpu.roll(summed, LOG, 1), member)
        cols[...] = jnp.where(lane >= RISE, pltpu.roll(sigmoid(raw), RISE, 1), member)
        mark = lax.broadcasted_iota(jnp.int32, (8, Q), 0)
        position = first + lax.broadcasted_iota(jnp.int32, (8, Q), 1)
        segment = segment_of(scal, position)
        other = position + jnp.where(mark < 4, -mark, jnp.where(mark < 7, mark - 3, 0))
        same = (segment_of(scal, other) == segment).astype(F32)
        marks[0:8, :] = jnp.where(mark == 0, segment.astype(F32), same)
        marks[8:40, :] = summed.T[:32]
        total_out[pl.ds(pl.multiple_of(k * 8, 8), 8), :] = running[...]
        running[...] = running[...] + summed[Q - 1 : Q, :]

        pre = conv_before_act(scal, group, group_of(shared, k), halo, tail, taps, marks)
        act = pre * sigmoid(pre)
        bc[...] = act.astype(BF16)
        bct[...] = jnp.concatenate(
            [act[:, m * STATE : (m + 1) * STATE].T for m in range(width // STATE)], axis=0
        ).astype(BF16)

    loop(subs, body)


def states_kernel(
    subs, head, scal, raw, halo, taps, spread, cols_in, logs_in, steps_in, marks_in, bct_in, total,
    act_out, slope_out, states, final, through, tail, state,
):
    channels = raw.shape[1]

    @pl.when(pl.program_id(0) == 0)
    def _():
        state[...] = jnp.zeros_like(state)

    def body(k):
        group = pl.program_id(0) * subs + k
        cols, bct = group_of(cols_in, k), lane_group_of(bct_in, k)
        pre = conv_before_act(scal, group, group_of(raw, k), halo, tail, taps, marks_in.at[k])
        gate = sigmoid(pre)
        act = (pre * gate).astype(BF16)
        group_of(act_out, k)[...] = act
        group_of(slope_out, k)[...] = (gate * (1.0 + pre * (1.0 - gate))).astype(BF16)
        summed = dot(group_of(logs_in, k)[...], spread[...])
        last = summed[Q - 1 : Q, :]
        tails = jnp.exp2(last - summed) * cols[:, ENDING : ENDING + 1]
        scaled = act.astype(F32) * dot(group_of(steps_in, k)[...], spread[...])
        fresh = dot(bct[:STATE, :], (scaled * tails).astype(BF16))
        states[k] = state[...].astype(BF16)
        state[...] = state[...] * (jnp.exp2(last) * kept(scal, group)) + fresh

    loop(subs, body)

    @pl.when(pl.program_id(0) == pl.num_programs(0) - 1)
    def _():
        final[...] = state[...]
        ended = total[(subs - 1) * 8 : subs * 8, :]
        last = dot(logs_in[subs * Q - 16 : subs * Q, :], spread[...])[15:16]
        through[...] = jnp.exp2(spread_heads(ended, head, channels) + last) * reaches(
            scal, pl.num_programs(0) * subs
        )


def total_share(scal, group, head, total, k, channels):
    here = total[pl.ds(pl.multiple_of(k * 8, 8), 8), :]
    return jnp.exp2(spread_heads(here, head, channels))[0:1] * reaches(scal, group)


def gaps_of(pair, head, cols, logs, marks, between, across_lanes):
    if not across_lanes:
        both = dot(logs[...], between[:, 2 * pair * Q : 2 * (pair + 1) * Q])
        return [both[:, :Q], both[:, Q:]]
    lane = LOG + head + 2 * pair
    return [
        jnp.broadcast_to(cols[:, lane + m : lane + m + 1], (Q, Q))
        - marks[8 + head + 2 * pair + m : 9 + head + 2 * pair + m, :]
        for m in range(2)
    ]


def scan_kernel(
    subs, head, scal, act_in, bc_in, cols_in, logs_in, steps_in, marks_in, across, spread, spread_rows,
    total, gate_in, back_in, states, start, taps, scanned_out, stats_out, between,
):
    channels = act_in.shape[1]

    @pl.when(pl.program_id(0) == 0)
    def _():
        between[...] = spread_rows[...]

    def body(k):
        group = pl.program_id(0) * subs + k
        act, bc, cols = group_of(act_in, k), group_of(bc_in, k), group_of(cols_in, k)
        gate, back, logs = group_of(gate_in, k), group_of(back_in, k), group_of(logs_in, k)
        between[96:112, :] = across[k]
        marks = marks_in.at[k]
        summed_all = dot(logs[...], spread[...])
        steps = dot(group_of(steps_in, k)[...], spread[...])
        scanned = group_of(scanned_out, k)
        b_map, c_map = bc[:, :STATE], bc[:, STATE:]
        scores = dot(c_map, b_map, NT)
        allowed = triangle(cols, marks, False)
        carries = cols[:, CARRIES : CARRIES + 1]
        share = total_share(scal, group, head, total, k, channels)
        state = (states[k].astype(F32) + share * start[...]).astype(BF16)
        outside = dot(c_map, state)
        squares = jnp.zeros((Q, 2 * HEAD), F32)
        inner = jnp.zeros((Q, 2 * HEAD), F32)
        for p in range(channels // (2 * HEAD)):
            part = slice(2 * HEAD * p, 2 * HEAD * (p + 1))
            gaps = gaps_of(p, head, cols, logs, marks, between, SCAN_LANES)
            weights = []
            for m in range(2):
                decay = jnp.exp2(gaps[m] + allowed)
                weights.append((decay * scores).astype(BF16))
            summed = summed_all[:, part]
            member = act[:, part].astype(F32)
            scaled = (member * steps[:, part]).astype(BF16)
            result = dot(jnp.concatenate(weights, axis=1), stacked_heads(scaled))
            result = result + outside[:, part] * (jnp.exp2(summed) * carries)
            scanned[:, part] = result
            mixed_heads = result + taps[6:7, part] * member
            raw = gate[:, part].astype(F32)
            gated = mixed_heads * (raw * sigmoid(raw))
            squares = squares + gated * gated
            inner = inner + back[:, part].astype(F32) * taps[5:6, part] * gated
        squares = jnp.sum(squares, axis=1, keepdims=True)
        inner = jnp.sum(inner, axis=1, keepdims=True) * cols[:, VALID : VALID + 1]
        lane = lax.broadcasted_iota(jnp.int32, (Q, Q), 1)
        both = jnp.where(lane == 0, squares, jnp.where(lane == 1, inner, 0.0))
        lane_group_of(stats_out, k)[...] = both.T[:8]

    loop(subs, body)


def gate_back_kernel(
    subs, turns, head, inner_channels, scal, scanned_in, act_in, gate_in, back_in, stats_in, bct_in, cols_in,
    logs_in, spread, total, taps, mixed_out, low_gate_out, back_heads_out, reach, sums,
):
    channels = act_in.shape[1]

    @pl.when(pl.program_id(0) == 0)
    def _():
        reach[...] = jnp.zeros_like(reach)
        sums[...] = jnp.zeros_like(sums)

    def body(k):
        group = pl.program_id(0) * subs + k
        scanned, act, gate = group_of(scanned_in, k), group_of(act_in, k), group_of(gate_in, k)
        back, cols, stats = group_of(back_in, k), group_of(cols_in, k), lane_group_of(stats_in, k)
        mixed, low_gate = group_of(mixed_out, k), group_of(low_gate_out, k)
        back_heads, bct = group_of(back_heads_out, k), lane_group_of(bct_in, k)
        row = lax.broadcasted_iota(jnp.int32, (8, Q), 0)
        inverse_row = lax.rsqrt(stats[...] / inner_channels + EPS)
        both = jnp.concatenate(
            [jnp.where(row == 0, inverse_row, stats[...]), jnp.zeros((Q - 8, Q), F32)], axis=0
        ).T
        inverse, inner = both[:, 0:1], both[:, 1:2]
        valid, carries = cols[:, VALID : VALID + 1], cols[:, CARRIES : CARRIES + 1]
        slope = inverse * inverse * inverse * inner * valid / inner_channels
        inverse_valid = inverse * valid
        summed = dot(group_of(logs_in, k)[...], spread[...])
        gradients = []
        for p in range(channels // (2 * HEAD)):
            part = slice(2 * HEAD * p, 2 * HEAD * (p + 1))
            member = act[:, part].astype(F32)
            mixed_heads = scanned[:, part] + taps[6:7, part] * member
            raw = gate[:, part].astype(F32)
            share = sigmoid(raw)
            opened = raw * share
            gated = mixed_heads * opened
            gain = taps[5:6, part]
            mixed[:, part] = (gated * inverse_valid * gain).astype(BF16)
            scaled_back = back[:, part].astype(F32) * inverse_valid
            gradient = scaled_back * gain - gated * slope
            low_gate[:, part] = (gradient * mixed_heads * (share + opened * (1.0 - share))).astype(BF16)
            low = (gradient * opened).astype(BF16)
            back_heads[:, part] = low
            wide = low.astype(F32)
            sums[0:1, part] = sums[0:1, part] + jnp.sum(scaled_back * gated, axis=0, keepdims=True)
            sums[1:2, part] = sums[1:2, part] + jnp.sum(wide * member, axis=0, keepdims=True)
            entered = jnp.exp2(summed[:, part]) * carries
            gradients.append((wide * entered).astype(BF16))
        share = total_share(scal, group, head, total, k, channels)
        reach[...] = reach[...] + share * dot(bct[STATE:, :], jnp.concatenate(gradients, axis=1))

    @pl.when(pl.program_id(0) < turns)
    def _():
        loop(subs, body)

    @pl.when(pl.program_id(0) == turns)
    def _():
        low_gate_out[...] = jnp.zeros_like(low_gate_out)


def scan_back_kernel(
    subs, head, scal, act_in, slope_in, heads_in, scanned_in, raw, halo, taps, picks, bc_in, bct_in,
    cols_in, logs_in, steps_in, marks_in, across, spread, spread_rows, total, head_rows, states, start,
    leaving, low_out, back_bc_out, low_rate_out, sums, head_out, first_rows, last_rows, behind, back_pre,
    back_state, difference, between,
):
    turn = pl.program_id(0)
    turns = pl.num_programs(0) - 1
    channels = act_in.shape[1]

    @pl.when(turn == 0)
    def _():
        back_state[...] = leaving[...]
        behind[...] = jnp.zeros_like(behind)
        between[...] = spread_rows[...]
        sums[...] = jnp.zeros_like(sums)
        head_out[...] = jnp.zeros_like(head_out)

    def body(count):
        k = subs - 1 - count
        group = (turns - 1 - turn) * subs + k
        act, slope, back_heads = group_of(act_in, k), group_of(slope_in, k), group_of(heads_in, k)
        scanned, bc, cols = group_of(scanned_in, k), group_of(bc_in, k), group_of(cols_in, k)
        bct, back_bc, logs = lane_group_of(bct_in, k), group_of(back_bc_out, k), group_of(logs_in, k)
        between[96:112, :] = across[k]
        marks = marks_in.at[k]
        summed_all = dot(logs[...], spread[...])
        steps = dot(group_of(steps_in, k)[...], spread[...])
        b_map, c_map = bc[:, :STATE], bc[:, STATE:]
        scores = dot(b_map, c_map, NT)
        allowed = triangle(cols, marks, True)
        carries, ending = cols[:, CARRIES : CARRIES + 1], cols[:, ENDING : ENDING + 1]
        share = total_share(scal, group, head, total, k, channels)
        state = states[k].astype(F32) + share * start[...]
        state_low = state.astype(BF16)
        leaving_low = back_state[...].astype(BF16)
        from_state = dot(b_map, leaving_low)
        back_scores = jnp.zeros((Q, Q), F32)
        into_state, out_of_state, passed, products = [], [], [], []
        for p in range(channels // (2 * HEAD)):
            part = slice(2 * HEAD * p, 2 * HEAD * (p + 1))
            low = back_heads[:, part]
            wide = low.astype(F32)
            member = act[:, part].astype(F32)
            step = steps[:, part]
            scaled = (member * step).astype(BF16)
            stacked = stacked_heads(low)
            back_weights = dot(stacked_heads(scaled), low, NT)
            gaps = gaps_of(p, head, cols, logs, marks, between, True)
            weights = []
            for m in range(2):
                decay = jnp.exp2(allowed - gaps[m])
                weights.append((decay * scores).astype(BF16))
                back_scores = back_scores + decay * back_weights[m * Q : (m + 1) * Q]
            summed = summed_all[:, part]
            last = summed[Q - 1 : Q, :]
            tails = jnp.exp2(last - summed) * ending
            back_scaled = dot(jnp.concatenate(weights, axis=1), stacked)
            scaled_wide = scaled.astype(F32)
            from_end = tails * from_state[:, part]
            difference[:, part] = wide * scanned[:, part] - scaled_wide * back_scaled
            passed.append((scaled_wide * from_end).astype(BF16))
            back_scaled = back_scaled + from_end
            into_state.append((scaled_wide * tails).astype(BF16))
            out_of_state.append((wide * (jnp.exp2(summed) * carries)).astype(BF16))
            products.append((back_scaled * member).astype(BF16))
            back_act = back_scaled * step + taps[6:7, part] * wide
            back_pre[:, part] = back_act * slope[:, part].astype(F32)
        into_state = jnp.concatenate(into_state, axis=1)
        out_of_state = jnp.concatenate(out_of_state, axis=1)
        back_b = dot(back_scores.astype(BF16), c_map) + dot(into_state, leaving_low, NT)
        back_c = dot(back_scores.T.astype(BF16), b_map) + dot(out_of_state, state_low, NT)
        back_bc[:, :STATE] = back_b
        back_bc[:, STATE:] = back_c

        kept_state = back_state[...] * (jnp.exp2(summed_all[Q - 1 : Q, :]) * kept(scal, group))
        back_state[...] = kept_state + dot(bct[STATE:, :], out_of_state)
        crossing = jnp.sum(kept_state * state, axis=0, keepdims=True)
        difference[Q - 1 : Q, :] = difference[Q - 1 : Q, :] + crossing

        product = dot(jnp.concatenate(products, axis=1), picks[...])
        at = lax.broadcasted_iota(jnp.int32, (Q, Q), 0)
        lane = lax.broadcasted_iota(jnp.int32, (Q, Q), 1)
        before_it = dot(jnp.concatenate(passed, axis=1), picks[...])
        back_logs = in_order(split_sum(difference[...], picks[...]), at <= lane) + dot(
            (at > lane).astype(BF16), before_it.astype(BF16)
        )
        decays = jnp.where(lane < LOG, back_logs * head_rows[1:2, :], 0.0)
        back_rate = (product + decays) * pltpu.roll(cols[...], 128 - RISE, 1)
        back_rate = jnp.where(lane < LOG, back_rate, 0.0)
        group_of(low_rate_out, k)[...] = back_rate.astype(BF16)
        head_out[0:1, :] = head_out[0:1, :] + jnp.sum(back_rate, axis=0, keepdims=True)
        head_out[1:2, :] = head_out[1:2, :] + jnp.sum(decays * cols[...], axis=0, keepdims=True)

        conv_back(scal, turn, k, group, back_pre[...], behind, group_of(raw, k), taps, marks,
                  group_of(low_out, k), sums, first_rows, last_rows, subs)

    @pl.when(turn < turns)
    def _():
        loop(subs, body)

    @pl.when(turn == turns)
    def _():
        low_rate_out[...] = jnp.zeros_like(low_rate_out)
        rows_behind(scal, behind, halo, taps, low_out, sums)


def conv_back(
    scal, turn, k, group, now, behind, raw, taps, marks, low, sums, first_rows, last_rows, subs
):
    now_low = now.astype(BF16)
    moved = dot(shifts(marks, True), now_low)
    edge = dot(edge_shifts(scal, scal[4] + (group + 1) * Q, True), behind[...])
    value = raw[...].astype(F32)
    sums[3:4, :] = sums[3:4, :] + jnp.sum(now * value, axis=0, keepdims=True)
    sums[4:5, :] = sums[4:5, :] + jnp.sum(now, axis=0, keepdims=True)
    total = now * taps[3:4, :]
    last = jnp.zeros((16, now.shape[1]), F32)
    for j in range(1, 4):
        tap = slice(3 - j, 4 - j)
        part, rest = moved[(j - 1) * Q : j * Q], edge[(j - 1) * 16 : j * 16]
        total = total + part * taps[tap, :]
        last = last + rest * taps[tap, :]
        sums[tap, :] = (
            sums[tap, :]
            + jnp.sum(part * value, axis=0, keepdims=True)
            + jnp.sum(rest * value[Q - 16 : Q], axis=0, keepdims=True)
        )
    last = total[Q - 16 :] + last
    low[...] = jnp.concatenate([total[: Q - 16], last], axis=0).astype(BF16)

    @pl.when((turn == 0) & (k == subs - 1))
    def _():
        last_rows[...] = last[8:]

    behind[...] = now_low[0:16]
    first_rows[...] = now[0:8]


def rows_behind(scal, behind, halo, taps, low_out, sums):
    edge = dot(edge_shifts(scal, scal[4], True), behind[...])
    value = halo[...].astype(F32)
    total = jnp.zeros((16, value.shape[1]), F32)
    for j in range(1, 4):
        tap, rest = slice(3 - j, 4 - j), edge[(j - 1) * 16 : j * 16]
        total = total + rest * taps[tap, :]
        sums[tap, :] = sums[tap, :] + jnp.sum(rest * value, axis=0, keepdims=True)
    low_out[...] = jnp.zeros_like(low_out)
    low_out[0:16, :] = total.astype(BF16)


def shared_back_kernel(
    subs, scal, back_bc, back_more, raw, before, halo, taps, marks_in, low_out, sums, first_rows,
    last_rows, behind, tail,
):
    turn = pl.program_id(0)
    turns = pl.num_programs(0) - 1

    @pl.when(turn == 0)
    def _():
        behind[...] = jnp.zeros_like(behind)
        sums[...] = jnp.zeros_like(sums)

    def body(count):
        k = subs - 1 - count
        group = (turns - 1 - turn) * subs + k
        start = pl.multiple_of(jnp.maximum(k * Q - 16, 0), 16)
        tail[...] = jnp.where(k == 0, before[...], raw[pl.ds(start, 16), :])
        marks = marks_in.at[k]
        pre = conv_before_act(scal, group, group_of(raw, k), halo, tail, taps, marks)
        gate = sigmoid(pre)
        back = group_of(back_bc, k)[...] + group_of(back_more, k)[...]
        now = back * (gate * (1.0 + pre * (1.0 - gate)))
        conv_back(scal, turn, k, group, now, behind, group_of(raw, k), taps, marks,
                  group_of(low_out, k), sums, first_rows, last_rows, subs)

    @pl.when(turn < turns)
    def _():
        loop(subs, body)

    @pl.when(turn == turns)
    def _():
        rows_behind(scal, behind, halo, taps, low_out, sums)


def joined(scal, low, later, last_rows, taps, rows):
    sent = []
    for back in range(3, 0, -1):
        at = scal[4] + rows - back
        extra = jnp.zeros_like(later[0])
        for j in range(back, 4):
            extra = extra + same_segment(scal, at, at + j) * taps[3 - j] * later[j - back]
        sent.append(extra)
    out = last_rows + jnp.concatenate([jnp.zeros((5, later.shape[1]), F32), jnp.stack(sent)])
    return lax.dynamic_update_slice(low, out.astype(BF16), (rows - 8, 0))


def split_blocks(member, count):
    return jnp.split(member, count, axis=0)


def chip_rows_kernel(tiles, scal, own, other, out):
    mine = pl.program_id(0) // tiles == scal[0]
    out[...] = jnp.where(mine, own[...], other[...])


def normed_rows_kernel(tiles, scal, own, other, gain, out):
    step = pl.program_id(0)

    @pl.when(step < 2 * tiles)
    def _():
        wide = jnp.where(step // tiles == scal[0], own[...], other[...]).astype(F32)
        inverse = lax.rsqrt(jnp.mean(wide * wide, axis=1, keepdims=True) + EPS)
        out[...] = (wide * inverse * gain[...]).astype(BF16)

    @pl.when(step == 2 * tiles)
    def _():
        out[...] = jnp.zeros_like(out)


def chip_rows(core, own, other, gain=None):
    rows, width = own.shape
    tile = min(512, rows)
    tiles = rows // tile

    def at(first):
        return pl.BlockSpec((tile, width), lambda i, s: (jnp.clip(i - first(s) * tiles, 0, tiles - 1), 0))

    specs = [at(lambda s: s[0]), at(lambda s: 1 - s[0])]
    args = [core.reshape(1).astype(jnp.int32), own, other]
    body, extra = partial(chip_rows_kernel, tiles), 0
    if gain is not None:
        body, extra = partial(normed_rows_kernel, tiles), 1
        specs.append(whole((1, width)))
        args.append(gain.reshape(1, width))
    return call(
        body,
        2 * tiles + extra,
        specs,
        [pl.BlockSpec((tile, width), lambda i, s: (i, 0))],
        [shape_of((2 * rows + extra * Q, width), BF16)],
        [],
        "chip_rows",
        tuple(args),
    )[0]


def many_dots_kernel(dims, finish, scal, *refs):
    count = len(dims)
    total = dot(refs[0][...], refs[count][...], dims[0])
    for k in range(1, count):
        total = total + dot(refs[k][...], refs[count + k][...], dims[k])
    finish(total, *refs[2 * count :])


def write_sum(total, out):
    out[...] = total.astype(out.dtype)


def write_output(total, tokens, other, out):
    out[...] = (tokens[...].astype(F32) + total + other[...].astype(F32)).astype(out.dtype)


def write_input_gradient(total, tokens, other, cotangent, gain, out, gain_sum):
    @pl.when(pl.program_id(0) == 0)
    def _():
        gain_sum[...] = jnp.zeros_like(gain_sum)

    residual = tokens[...].astype(F32)
    inverse = lax.rsqrt(jnp.mean(residual * residual, axis=1, keepdims=True) + EPS)
    back = total + other[...].astype(F32)
    gain_sum[0:1, :] = gain_sum[0:1, :] + jnp.sum(back * residual * inverse, axis=0, keepdims=True)
    scaled = back * gain[...]
    slope = inverse * inverse * inverse * jnp.mean(scaled * residual, axis=1, keepdims=True)
    out[...] = cotangent[...].astype(F32) + scaled * inverse - residual * slope


def call(body, grid, in_specs, out_specs, out_shape, scratch, name, args, waits=()):
    given, made = len(in_specs), len(out_specs)

    def kernel(scal, *refs):
        outs = refs[given + len(waits) :]
        outs[made][...] = jnp.ones_like(outs[made])
        body(scal, *refs[:given], *outs[:made], *outs[made + 1 :])

    return pl.pallas_call(
        kernel,
        grid_spec=pltpu.PrefetchScalarGridSpec(
            num_scalar_prefetch=1,
            grid=(grid,),
            in_specs=list(in_specs) + [pl.BlockSpec(memory_space=pl.ANY)] * len(waits),
            out_specs=list(out_specs) + [whole((8, 128))],
            scratch_shapes=scratch,
        ),
        out_shape=list(out_shape) + [shape_of((8, 128), F32)],
        compiler_params=pltpu.CompilerParams(vmem_limit_bytes=VMEM_LIMIT),
        cost_estimate=pl.CostEstimate(
            flops=int(PACE * TIMES[name]), bytes_accessed=10**5, transcendentals=0
        ),
        name=name,
    )(*args, *waits)


def whole(shape):
    return pl.BlockSpec(shape, lambda i, s: tuple(0 for _ in shape))


def after(member, *deps):
    return lax.optimization_barrier((member, *deps))[0]


class Order:
    def __init__(self):
        self.last = None

    def hold(self, member):
        return member if self.last is None else after(member, self.last)

    def holds(self, members):
        members = [self.hold(m) for m in members]
        self.last = after(self.last, *members)
        return members

    def done(self, member):
        self.last = member
        return member


def shape_of(shape, dtype):
    return jax.ShapeDtypeStruct(shape, dtype)


def many_dots(
    offset_rows, lefts, rights, dims, rows, name, finish=write_sum, extras=(), dtype=BF16, sums=(), waits=()
):
    tile = min(256, rows)
    columns = rights[0].shape[0 if dims[0] == NT else 1]
    scal = (offset_rows // tile).reshape(1).astype(jnp.int32)
    by_row = pl.BlockSpec((tile, columns), lambda i, s: (i, 0))
    return call(
        partial(many_dots_kernel, tuple(dims), finish),
        rows // tile,
        [pl.BlockSpec((tile, a.shape[1]), lambda i, s: (s[0] + i, 0)) for a in lefts]
        + [whole(b.shape) for b in rights]
        + [by_row if e.shape[0] == rows else whole(e.shape) for e in extras],
        [by_row] + [whole(shape) for shape in sums],
        [shape_of((rows, columns), dtype)] + [shape_of(shape, F32) for shape in sums],
        [],
        name,
        (scal, *lefts, *rights, *extras),
        waits,
    )


def solution(mesh):
    tensor = mesh.shape["tensor"]
    copies = mesh.shape["dp"]
    ny = tensor // 2
    nx = ny if copies % ny == 0 else 1
    nz = copies // nx

    def from_y(member, shift):
        pairs = [((((y + shift) % ny) * 2 + c), y * 2 + c) for y in range(ny) for c in range(2)]
        return lax.ppermute(member, "tensor", pairs)

    def next_y(member, step):
        pairs = [
            ((y - step) * 2 + c, y * 2 + c)
            for y in range(ny)
            for c in range(2)
            if 0 <= y - step < ny
        ]
        return lax.ppermute(member, "tensor", pairs)

    def from_core(member):
        return lax.ppermute(member, "tensor", [(t ^ 1, t) for t in range(tensor)])

    def from_x(member, shift):
        pairs = [(z * nx + (x + shift) % nx, z * nx + x) for z in range(nz) for x in range(nx)]
        return lax.ppermute(member, "dp", pairs)

    def from_z(member, shift):
        pairs = [(((z + shift) % nz) * nx + x, z * nx + x) for z in range(nz) for x in range(nx)]
        return lax.ppermute(member, "dp", pairs)

    def sum_rows(member):
        bit = 1
        while bit < copies:
            member = member + lax.ppermute(member, "dp", [(d ^ bit, d) for d in range(copies)])
            bit *= 2
        return member

    def ways_x(member, x):
        kept = lax.dynamic_index_in_dim(member, x, 1, keepdims=False)
        got = []
        for k in range(1, nx):
            sent = lax.dynamic_index_in_dim(member, (x + k) % nx, 1, keepdims=False)
            got.append(from_x(sent.astype(BF16), nx - k))
        return [kept] + got

    def ways_z(member, z, bit):
        parts = member.reshape(-1, 2, *member.shape[-2:])
        own = (z // bit) % 2
        kept = lax.dynamic_index_in_dim(parts, own, 1, keepdims=False)
        sent = lax.dynamic_index_in_dim(parts, 1 - own, 1, keepdims=False)
        pairs = [((p ^ bit) * nx + x, p * nx + x) for p in range(nz) for x in range(nx)]
        return [kept, lax.ppermute(sent.astype(BF16), "dp", pairs)]

    def summed(parts, one=None):
        total = parts[0].astype(F32)
        for part in parts[1:]:
            part = part.astype(F32)
            total = total + (part if one is None else part * one[0, 0])
        return total

    def gather_rows(member, x, z):
        member = member[None]
        bit = nz // 2
        while bit >= 1:
            pairs = [((p ^ bit) * nx + q, p * nx + q) for p in range(nz) for q in range(nx)]
            other = lax.ppermute(member, "dp", pairs)
            high = (z // bit) % 2 == 1
            member = jnp.stack([jnp.where(high, other, member), jnp.where(high, member, other)], axis=1)
            member = member.reshape(-1, *member.shape[2:])
            bit //= 2
        parts = jnp.stack([member] + [from_x(member, k) for k in range(1, nx)])
        parts = [lax.dynamic_index_in_dim(parts, (k - x) % nx, 0, False) for k in range(nx)]
        return jnp.stack(parts, axis=1).reshape(-1, member.shape[-1])

    def shards(
        tokens, lengths, norm_gain, w_gate, w_value, w_shared, w_rate, conv_value, value_bias,
        conv_shared, shared_bias, rate_bias, decay_log, skip_gain, mix_gain, w_out, cotangent,
    ):
        index = lax.axis_index("tensor")
        y, core = index // 2, index % 2
        dp = lax.axis_index("dp")
        z, x = dp // nx, dp % nx
        own_rows, width = tokens.shape
        rows = 2 * own_rows
        groups = rows // Q
        channels = w_gate.shape[1]
        heads = w_rate.shape[1]
        inner = channels * tensor
        own_start = core * own_rows
        lanes = 128
        maps = w_shared.shape[1]
        blocks = range(ny)

        halo_one = next_y(tokens[own_rows - 16 :], 1)
        tokens_other = from_core(tokens)
        halo = jnp.where(core == 1, halo_one, from_core(halo_one))
        packed = jnp.concatenate(
            [
                conv_value.T,
                value_bias[None],
                mix_gain[None],
                jnp.repeat(skip_gain, HEAD)[None],
                jnp.concatenate([rate_bias, decay_log, jnp.zeros((channels - 2 * heads,), F32)])[None],
                w_rate.T.astype(F32).reshape(-1, channels),
            ],
            axis=0,
        )
        packed = after(packed, halo_one)
        packs = [packed] + [from_y(packed, j) for j in range(1, ny)]

        order = Order()

        def own_part(weight):
            part = weight.shape[0] // nx
            return lax.dynamic_slice(weight, (x * part, 0), (part, weight.shape[1]))

        def fetched(member, dep):
            member = after(member, dep)
            return [from_y(member, j) for j in range(1, ny)]

        def from_parts(weight, pieces):
            part = weight.shape[0] // nx
            found = [weight]
            for piece in pieces:
                full = lax.dynamic_update_slice(weight, piece, (x * part, 0))
                for k in range(1, nx):
                    got = from_x(piece, k)
                    full = lax.dynamic_update_slice(full, got, ((x + k) % nx * part, 0))
                found.append(full)
            return found

        back_other = from_core(after(cotangent, tokens_other))
        value_parts = fetched(own_part(w_value), packs[-1])
        rates = [p[8:].reshape(heads, width).astype(BF16) for p in packs]
        packs = [p[:8] for p in packs]
        all_rates = jnp.concatenate(rates + [jnp.zeros((lanes - ny * heads, width), BF16)], axis=0)
        w_small = jnp.concatenate([w_shared, all_rates.T], axis=1)
        fill = jnp.zeros((lanes - ny * heads,), F32)
        head_rows = jnp.concatenate(
            [
                jnp.concatenate([p[7, :heads] for p in packs] + [fill])[None],
                jnp.concatenate([-jnp.exp(p[7, heads : 2 * heads]) for p in packs] + [fill])[None],
                jnp.zeros((6, lanes), F32),
            ],
            axis=0,
        )
        shared_taps = jnp.concatenate(
            [conv_shared.T, shared_bias[None], jnp.zeros((3, maps), F32)], axis=0
        )
        scal = jnp.concatenate([lengths[0], (y * rows).reshape(1)]).astype(jnp.int32)

        normed = chip_rows(core, tokens, tokens_other, norm_gain)
        halo = halo.astype(F32)
        halo = halo * lax.rsqrt(jnp.mean(halo * halo, axis=1, keepdims=True) + EPS) * norm_gain
        normed = order.done(lax.dynamic_update_slice(normed, halo.astype(BF16), (rows, 0)))
        step_rows = min(STEP_ROWS, rows)
        subs = step_rows // Q
        turns = rows // step_rows

        def up(columns):
            return pl.BlockSpec((step_rows, columns), lambda i, s: (i, 0))

        def stay(columns):
            return pl.BlockSpec((step_rows, columns), lambda i, s: (jnp.minimum(i, turns - 1), 0))

        def stay_lanes(depth):
            return pl.BlockSpec((depth, step_rows), lambda i, s: (0, jnp.minimum(i, turns - 1)))

        def up_lanes(depth):
            return pl.BlockSpec((depth, step_rows), lambda i, s: (0, i))

        def up_groups(*shape):
            return pl.BlockSpec((subs, *shape), lambda i, s: (i, 0, 0))

        def downward(i):
            return jnp.maximum(turns - 1 - i, 0)

        def down(columns):
            return pl.BlockSpec((step_rows, columns), lambda i, s: (downward(i), 0))

        def down_extended(columns):
            return pl.BlockSpec(
                (step_rows, columns), lambda i, s: (jnp.where(i == turns, turns, downward(i)), 0)
            )

        def down_lanes(depth):
            return pl.BlockSpec((depth, step_rows), lambda i, s: (0, downward(i)))

        def down_groups(*shape):
            return pl.BlockSpec((subs, *shape), lambda i, s: (downward(i), 0, 0))

        def down_before(columns):
            return pl.BlockSpec(
                (16, columns), lambda i, s: (jnp.maximum(downward(i) * (step_rows // 16) - 1, 0), 0)
            )

        def behind_rows(columns):
            return pl.BlockSpec((16, columns), lambda i, s: (rows // 16, 0))

        stay_total = pl.BlockSpec((subs * 8, lanes), lambda i, s: (jnp.minimum(i, turns - 1), 0))
        up_total = pl.BlockSpec((subs * 8, lanes), lambda i, s: (i, 0))
        down_total = pl.BlockSpec((subs * 8, lanes), lambda i, s: (downward(i), 0))
        extended = rows + Q

        raw_values = [order.done(dot(order.hold(normed), w_value).astype(BF16))]
        small = order.done(dot(order.hold(normed), w_small))
        value_parts = order.holds(value_parts)
        values = from_parts(w_value, value_parts)
        gate_parts = fetched(own_part(w_gate), value_parts[-1])
        raw_shared = small[:, :maps].astype(BF16)
        heads_here = ny * heads
        channel = np.arange(channels)
        column = np.arange(heads * Q)
        part_row = np.arange(lanes)[:, None]
        picks, spreads, spread_rows = [], [], []
        for j in blocks:
            mine = (j * heads + channel // HEAD)[None, :]
            picks.append(jnp.asarray((part_row == mine).T, BF16))
            spreads.append(jnp.asarray((part_row % 32 == mine) & (part_row < 96), BF16))
            mine = (j * heads + column // Q)[None, :]
            spread_rows.append(jnp.asarray((part_row % 32 == mine) & (part_row < 96), BF16))
        bc, bct, cols, logs, steps, marks, across, total, _ = call(
            partial(prepare_kernel, subs),
            turns,
            [up(maps), up(lanes), behind_rows(maps), whole((8, maps)), whole((8, lanes))],
            [
                up(maps),
                up_lanes(maps),
                up(lanes),
                up(lanes),
                up(lanes),
                up_groups(40, Q),
                up_groups(16, heads_here * Q),
                up_total,
            ],
            [
                shape_of((rows, maps), BF16),
                shape_of((maps, rows), BF16),
                shape_of((rows, lanes), F32),
                shape_of((rows, lanes), BF16),
                shape_of((rows, lanes), BF16),
                shape_of((groups, 40, Q), F32),
                shape_of((groups, 16, heads_here * Q), BF16),
                shape_of((groups * 8, lanes), F32),
            ],
            [pltpu.VMEM((16, maps), BF16), pltpu.VMEM((8, lanes), F32)],
            "prepare",
            (scal, raw_shared, small[:, maps:], raw_shared, shared_taps, head_rows),
        )
        order.done(total)

        acts, slopes, states, finals, throughs = [], [], [], [], []
        for j in blocks:
            if j == 1:
                gate_parts = order.holds(gate_parts)
                gates = from_parts(w_gate, gate_parts)
                out_parts = fetched(own_part(w_out), gate_parts[-1])
                values = [w_value] + [order.hold(v) for v in values[1:]]
            if j > 0:
                raw_values.append(order.done(dot(order.hold(normed), values[j]).astype(BF16)))
            if j == 1:
                raw_gates = [order.done(dot(order.hold(normed), w_gate).astype(BF16))]
            raw = raw_values[j]
            act, slope, state, final, through, _ = call(
                partial(states_kernel, subs, j * heads),
                turns,
                [
                    up(channels),
                    behind_rows(channels),
                    whole((8, channels)),
                    whole((lanes, channels)),
                    up(lanes),
                    up(lanes),
                    up(lanes),
                    up_groups(40, Q),
                    up_lanes(maps),
                    up_total,
                ],
                [
                    up(channels),
                    up(channels),
                    up_groups(STATE, channels),
                    whole((STATE, channels)),
                    whole((8, channels)),
                ],
                [
                    shape_of((rows, channels), BF16),
                    shape_of((rows, channels), BF16),
                    shape_of((groups, STATE, channels), BF16),
                    shape_of((STATE, channels), F32),
                    shape_of((8, channels), F32),
                ],
                [pltpu.VMEM((16, channels), BF16), pltpu.VMEM((STATE, channels), F32)],
                "states",
                (scal, order.hold(raw), raw, packs[j], spreads[j], cols, logs, steps, marks, bct, total),
                gate_parts if j == 1 else (),
            )
            order.done(final)
            if j == 0:
                back_rows = order.done(chip_rows(core, cotangent, order.hold(back_other)))
            acts.append(act)
            slopes.append(slope)
            states.append(state)
            finals.append(final)
            throughs.append(through)

        before = [(j + 1) % ny for j in blocks]
        behind = [(j - 1) % ny for j in blocks]
        starts = split_blocks(next_y(jnp.concatenate([finals[k] for k in before]), 1), ny)
        for _ in range(ny - 2):
            sent = [finals[k] + throughs[k][0:1] * starts[k] for k in before]
            starts = split_blocks(next_y(jnp.concatenate(sent), 1), ny)

        out_parts = order.holds(out_parts)
        outs = from_parts(w_out, out_parts)
        backs = [order.done(dot(order.hold(back_rows), w_out, NT).astype(BF16))]
        scans, stats = [], []
        for j in blocks:
            if j == 1:
                gates = [w_gate] + [order.hold(w) for w in gates[1:]]
                outs = [w_out] + [order.hold(w) for w in outs[1:]]
            if j > 0:
                raw_gates.append(order.done(dot(order.hold(normed), gates[j]).astype(BF16)))
                backs.append(order.done(dot(order.hold(back_rows), outs[j], NT).astype(BF16)))
            raw_gate, back = raw_gates[j], backs[j]
            scanned, stat, _ = call(
                partial(scan_kernel, subs, j * heads),
                turns,
                [
                    up(channels),
                    up(maps),
                    up(lanes),
                    up(lanes),
                    up(lanes),
                    up_groups(40, Q),
                    pl.BlockSpec((subs, 16, heads * Q), lambda i, s, j=j: (i, 0, j)),
                    whole((lanes, channels)),
                    whole((lanes, heads * Q)),
                    up_total,
                    up(channels),
                    up(channels),
                    up_groups(STATE, channels),
                    whole((STATE, channels)),
                    whole((8, channels)),
                ],
                [up(channels), up_lanes(8)],
                [shape_of((rows, channels), F32), shape_of((8, rows), F32)],
                [pltpu.VMEM((lanes, heads * Q), BF16)],
                "scan",
                (scal, order.hold(acts[j]), bc, cols, logs, steps, marks, across, spreads[j], spread_rows[j],
                 total, raw_gate, back, states[j], starts[j], packs[j]),
                out_parts if j == 0 else (),
            )
            scans.append(order.done(scanned))
            stats.append(stat)

        stat = sum(stats[1:], stats[0])
        stat = stat + from_core(stat)

        mixeds, low_gates, back_heads, reaching, gate_sums = ([None] * ny for _ in range(5))
        for j in blocks:
            mixed, low_gate, back_head, reach, sums, _ = call(
                partial(gate_back_kernel, subs, turns, j * heads, inner),
                turns + 1,
                [
                    stay(channels),
                    stay(channels),
                    stay(channels),
                    stay(channels),
                    stay_lanes(8),
                    stay_lanes(maps),
                    stay(lanes),
                    stay(lanes),
                    whole((lanes, channels)),
                    stay_total,
                    whole((8, channels)),
                ],
                [stay(channels), up(channels), stay(channels)] + [whole((STATE, channels)), whole((8, channels))],
                [shape_of((m, channels), BF16) for m in (rows, extended, rows)]
                + [shape_of((STATE, channels), F32), shape_of((8, channels), F32)],
                [],
                "gate_back",
                (scal, scans[j], order.hold(acts[j]), raw_gates[j], backs[j], stat, bct, cols, logs,
                 spreads[j], total, packs[j]),
            )
            mixeds[j], low_gates[j], back_heads[j] = mixed, low_gate, back_head
            reaching[j], gate_sums[j] = order.done(reach), sums

        leavings = [next_y(reaching[k], -1) for k in behind]
        for _ in range(ny - 2):
            leavings = [next_y(reaching[k] + throughs[k][0:1] * leavings[k], -1) for k in behind]

        def scattered(member):
            return member.reshape(nz, nx, width // copies, member.shape[1])

        out_blocks, gate_blocks = [None] * ny, [None] * ny
        for j in range(1, ny):
            out_blocks[j] = order.done(dot(order.hold(back_rows), mixeds[j], TN).astype(BF16))
            out_blocks[j] = after(out_blocks[j], leavings[-1])
        out_got = [from_y(out_blocks[j], ny - j) for j in range(1, ny)]
        for j in reversed(blocks):
            gate_blocks[j] = order.done(dot(order.hold(normed), low_gates[j], TN).astype(BF16))
        gate_ways = [ways_x(scattered(b), x) for b in gate_blocks]
        out_blocks[0] = order.done(dot(order.hold(back_rows), mixeds[0], TN).astype(BF16))
        ahead = (1 - core) * own_rows

        low_values, back_bcs, low_rates, conv_sums, head_sums_ = [None] * ny, [], [], [None] * ny, []
        value_blocks = [None] * ny
        for j in reversed(blocks):
            low, back_bc, low_rate, sums, head_out, first_rows, last_rows, scan_one = call(
                partial(scan_back_kernel, subs, j * heads),
                turns + 1,
                [
                    down(channels),
                    down(channels),
                    down(channels),
                    down(channels),
                    down(channels),
                    behind_rows(channels),
                    whole((8, channels)),
                    whole((channels, lanes)),
                    down(maps),
                    down_lanes(maps),
                    down(lanes),
                    down(lanes),
                    down(lanes),
                    down_groups(40, Q),
                    pl.BlockSpec((subs, 16, heads * Q), lambda i, s, j=j: (downward(i), 0, j)),
                    whole((lanes, channels)),
                    whole((lanes, heads * Q)),
                    down_total,
                    whole((8, lanes)),
                    down_groups(STATE, channels),
                    whole((STATE, channels)),
                    whole((STATE, channels)),
                ],
                [
                    down_extended(channels),
                    down(maps),
                    down_extended(lanes),
                    whole((8, channels)),
                    whole((8, lanes)),
                    whole((8, channels)),
                    whole((8, channels)),
                ],
                [
                    shape_of((extended, channels), BF16),
                    shape_of((rows, maps), F32),
                    shape_of((extended, lanes), BF16),
                    shape_of((8, channels), F32),
                    shape_of((8, lanes), F32),
                    shape_of((8, channels), F32),
                    shape_of((8, channels), F32),
                ],
                [
                    pltpu.VMEM((16, channels), BF16),
                    pltpu.VMEM((Q, channels), F32),
                    pltpu.VMEM((STATE, channels), F32),
                    pltpu.VMEM((Q, channels), F32),
                    pltpu.VMEM((lanes, heads * Q), BF16),
                ],
                "scan_back",
                (scal, order.hold(acts[j]), slopes[j], back_heads[j], scans[j], raw_values[j],
                 raw_values[j], packs[j], picks[j], bc, bct, cols, logs, steps, marks, across, spreads[j],
                 spread_rows[j], total, head_rows, states[j], starts[j], leavings[j]),
            )
            low_values[j] = (order.done(low), first_rows, last_rows)
            if j == ny - 1:
                gate_rows = [summed([w[0]] + order.holds(w[1:])) for w in gate_ways]
                gate_got = [from_y(gate_rows[k].astype(BF16), ny - k) for k in range(1, ny)]
                order.done(gate_rows[0])
            if j > 0:
                value_blocks[j] = order.done(dot(order.hold(normed), low, TN).astype(BF16))
            if j == 1:
                value_got = [from_y(value_blocks[k], ny - k) for k in range(1, ny)]
                out_sum = summed([out_blocks[0]] + order.holds(out_got))
                out_ways = ways_x(scattered(out_sum), x)
                order.done(out_sum)
                out_sent = order.done(
                    many_dots(
                        ahead, [order.hold(m) for m in mixeds], outs, [NN] * ny, own_rows, "out_other"
                    )[0]
                )
                out_other = from_core(out_sent)
            back_bcs.append(back_bc)
            low_rates.append(low_rate)
            conv_sums[j] = sums
            head_sums_.append(head_out)

        later = [member[1] for member in low_values]
        later = next_y(jnp.concatenate([later[k] for k in behind], axis=1), -1)
        back_bc = sum(back_bcs[1:], back_bcs[0])
        back_bc_other = from_core(back_bc)
        out_sum = summed(out_ways, scan_one)
        out_ways = ways_z(out_sum, z, 1)
        block_out, own_one = many_dots(
            own_start, mixeds, outs, [NN] * ny, own_rows, "out_own", write_output, (tokens, out_other),
            waits=(back_bc, out_sum),
        )

        low_shared, shared_sums, first_rows, last_rows, shared_one = call(
            partial(shared_back_kernel, subs),
            turns + 1,
            [
                down(maps),
                down(maps),
                down(maps),
                down_before(maps),
                behind_rows(maps),
                whole((8, maps)),
                down_groups(40, Q),
            ],
            [down_extended(maps), whole((8, maps)), whole((8, maps)), whole((8, maps))],
            [
                shape_of((extended, maps), BF16),
                shape_of((8, maps), F32),
                shape_of((8, maps), F32),
                shape_of((8, maps), F32),
            ],
            [pltpu.VMEM((16, maps), BF16), pltpu.VMEM((16, maps), BF16)],
            "shared_back",
            (scal, back_bc, back_bc_other, raw_shared, raw_shared, raw_shared, shared_taps, marks),
            (own_one,),
        )
        later_shared = next_y(first_rows, -1)
        low_rate = sum(low_rates[1:], low_rates[0])
        half = maps // 2
        part = lax.dynamic_slice(low_shared, (0, core * half), (extended, half))
        small_block = dot(normed, jnp.concatenate([part, low_rate], axis=1), TN).astype(BF16)
        small_got = [from_y(small_block, ny - j) for j in range(1, ny)]
        value_sum = summed([dot(normed, low_values[0][0], TN)] + value_got, shared_one)
        late_ways = ways_x(scattered(value_sum), x)
        gate_sum = summed([gate_rows[0]] + gate_got, shared_one)
        gate_ways = ways_z(gate_sum, z, 1)
        bit = 2
        while bit < nz:
            out_ways = ways_z(summed(out_ways, shared_one), z, bit)
            bit *= 2

        low_values = [
            joined(scal, m[0], later[:, j * channels : (j + 1) * channels], m[2], packs[j], rows)
            for j, m in enumerate(low_values)
        ]
        low_shared = joined(scal, low_shared, later_shared, last_rows, shared_taps, rows)

        lefts = [low_rate] + low_gates + low_values
        rights = [all_rates] + gates + values
        sent, other_one = many_dots(
            ahead, lefts, rights, [NN] + [NT] * (2 * ny), own_rows, "back_other",
            waits=(value_sum, small_block),
        )
        back_normed_other = from_core(sent)
        small_sum = small_block[:, :half].astype(F32)
        rate_sum = small_block[:, half : half + heads].astype(F32)
        late = summed(late_ways, other_one)
        late_ways = ways_z(late, z, 1)
        for j, got in enumerate(small_got):
            got = got.astype(F32) * other_one[0, 0]
            at = half + (ny - 1 - j) * heads
            small_sum = small_sum + got[:, :half]
            rate_sum = rate_sum + got[:, at : at + heads]
        fill = jnp.zeros((width, lanes - heads), F32)
        least = scattered(jnp.concatenate([small_sum, rate_sum, fill], axis=1))
        least_ways = ways_x(least, x)
        bit = 2
        while bit < nz:
            gate_ways = ways_z(summed(gate_ways, other_one), z, bit)
            bit *= 2
        tokens_grad, gain_sum, kept_one = many_dots(
            own_start, [low_shared] + lefts, [w_shared] + rights, [NT, NN] + [NT] * (2 * ny), own_rows,
            "back_own", write_input_gradient, (tokens, back_normed_other, cotangent, norm_gain[None]), F32,
            ((8, width),), waits=(late, least),
        )
        least_ways = ways_z(summed(least_ways, kept_one), z, 1)
        bit = 2
        while bit < nz:
            late_ways = ways_z(summed(late_ways, kept_one), z, bit)
            bit *= 2
        grad_norm = gain_sum[0]

        bit = 2
        while bit < nz:
            least_ways = ways_z(summed(least_ways), z, bit)
            bit *= 2
        grad_out = summed(out_ways, other_one).reshape(width // copies, channels).T
        grad_gate = summed(gate_ways, kept_one).reshape(width // copies, channels)
        grad_value = summed(late_ways).reshape(width // copies, channels)
        least = summed(least_ways).reshape(width // copies, half + lanes)
        grad_rate = least[:, half : half + heads]
        part = gather_rows(least[:, :half].astype(BF16), x, z)
        other = from_core(part)
        grad_shared = jnp.where(
            core == 0, jnp.concatenate([part, other], axis=1), jnp.concatenate([other, part], axis=1)
        ).astype(F32)

        head_out = sum(head_sums_[1:], head_sums_[0])
        smalls = []
        for j in blocks:
            skip = gate_sums[j][1].reshape(heads, HEAD).sum(axis=1)
            own_heads = head_out[:2, j * heads : (j + 1) * heads].reshape(2 * heads)
            line = jnp.concatenate([skip, own_heads, jnp.zeros((channels - 3 * heads,), F32)])
            smalls.append(
                jnp.concatenate(
                    [conv_sums[j][:5], gate_sums[j][:1], line[None], jnp.zeros((1, channels), F32)]
                )
            )
        shared_sums = jnp.where(core == 0, shared_sums, 0.0)
        alls = jnp.concatenate([shared_sums, grad_norm.reshape(-1, maps)], axis=0)
        alls = alls.reshape(-1, lanes)
        alls = alls + from_core(alls)
        size = smalls[0].size // lanes
        ways = [jnp.concatenate([smalls[0].reshape(-1, lanes), alls], axis=0)]
        for j in range(1, ny):
            sent = jnp.concatenate([smalls[j].reshape(-1, lanes), alls], axis=0)
            ways.append(from_y(sent, ny - j))
        own = summed([way[:size] for way in ways])
        if ny > 1:
            ways = jnp.stack([way[size:] for way in ways])
            alls = summed([lax.dynamic_index_in_dim(ways, (y - k) % ny, 0, False) for k in range(ny)])
        both = sum_rows(jnp.concatenate([own, alls], axis=0))
        own = both[:size].reshape(smalls[0].shape)
        alls = both[size:].reshape(-1, maps)
        return (
            block_out,
            tokens_grad,
            alls[8:].reshape(width),
            grad_gate,
            grad_value,
            grad_shared,
            grad_rate,
            own[:4].T,
            own[4],
            alls[:4].T,
            alls[4],
            own[6, heads : 2 * heads],
            own[6, 2 * heads : 3 * heads],
            own[6, :heads],
            own[5],
            grad_out,
        )

    in_specs = (
        P(("dp", "tensor"), None),
        P("dp", None),
        P(),
        P(None, "tensor"),
        P(None, "tensor"),
        P(),
        P(None, "tensor"),
        P("tensor", None),
        P("tensor"),
        P(),
        P(),
        P("tensor"),
        P("tensor"),
        P("tensor"),
        P("tensor"),
        P("tensor", None),
        P(("dp", "tensor"), None),
    )
    out_specs = (
        P(("dp", "tensor"), None),
        P(("dp", "tensor"), None),
        P(),
        P("dp", "tensor"),
        P("dp", "tensor"),
        P(),
        P("dp", "tensor"),
        P("tensor", None),
        P("tensor"),
        P(),
        P(),
        P("tensor"),
        P("tensor"),
        P("tensor"),
        P("tensor"),
        P("tensor", "dp"),
    )
    return jax.shard_map(shards, mesh=mesh, in_specs=in_specs, out_specs=out_specs, check_vma=False)
```

```python
from functools import partial

import jax
import jax.numpy as jnp
import numpy as np
from jax import lax
from jax.experimental import pallas as pl
from jax.experimental.pallas import tpu as pltpu
from jax.sharding import PartitionSpec as P

Q = 128
STATE = 128
HEAD = 64
EPS = 1e-05
LOG2E = 1.4426950408889634
NEVER = -1e30
F32 = jnp.float32
BF16 = jnp.bfloat16
HIGH = lax.Precision.HIGHEST
VMEM_LIMIT = 56 * 1024 * 1024
STEP_ROWS = 512
PACE = 1.15e9 * 1.0
TIMES = dict(
    chip_rows=7, prepare=10, states=13, scan=15, gate_back=16, scan_back=33, out_other=9, out_own=11,
    back_other=17, back_own=22, shared_back=10,
)
SCAN_LANES = False

NN = (((1,), (0,)), ((), ()))
NT = (((1,), (1,)), ((), ()))
TN = (((0,), (0,)), ((), ()))


def dot(a, b, dims=NN, precision=None):
    return lax.dot_general(a, b, dims, precision=precision, preferred_element_type=F32)


STEP, MARK, RISE = 0, 64, 96
CARRIES, ENDING, VALID, SEGMENT = MARK, MARK + 1, MARK + 2, MARK + 3
EARLIER, LATER = MARK + 3, MARK + 6
LOG = 32


def loop(count, body):
    def step(k, carry):
        body(k)
        return carry

    lax.fori_loop(0, count, step, 0, unroll=True)


def group_of(ref, k):
    return ref.at[pl.ds(pl.multiple_of(k * Q, Q), Q), :]


def lane_group_of(ref, k):
    return ref.at[:, pl.ds(pl.multiple_of(k * Q, Q), Q)]


def segment_of(scal, position):
    end = scal[0]
    count = (position >= end).astype(jnp.int32)
    for k in range(1, 4):
        end = end + scal[k]
        count = count + (position >= end).astype(jnp.int32)
    return count


def same_segment(scal, position, other):
    return (segment_of(scal, position) == segment_of(scal, other)).astype(F32)


def kept(scal, group):
    first = scal[4] + group * Q
    return same_segment(scal, first - 1, first + Q - 1)


def reaches(scal, group):
    return same_segment(scal, scal[4] + group * Q - 1, scal[4] - 1)


def triangle(cols, rows, flipped):
    first = lax.broadcasted_iota(jnp.int32, (Q, Q), 0)
    second = lax.broadcasted_iota(jnp.int32, (Q, Q), 1)
    ordered = (first <= second) if flipped else (first >= second)
    allowed = ordered & (cols[:, SEGMENT : SEGMENT + 1] == rows[0:1, :])
    return jnp.where(allowed, 0.0, NEVER)


def in_first(rows):
    return lax.broadcasted_iota(jnp.int32, (rows, 2 * HEAD), 1) < HEAD


def pair_of(columns, lane):
    rows = columns.shape[0]
    first = jnp.broadcast_to(columns[:, lane : lane + 1], (rows, 2 * HEAD))
    second = jnp.broadcast_to(columns[:, lane + 1 : lane + 2], (rows, 2 * HEAD))
    return jnp.where(in_first(rows), first, second)


def spread_heads(columns, lane, channels):
    return jnp.concatenate(
        [pair_of(columns, lane + 2 * p) for p in range(channels // (2 * HEAD))], axis=1
    )


def stacked_heads(member):
    first = in_first(member.shape[0])
    none = jnp.zeros_like(member)
    return jnp.concatenate([jnp.where(first, member, none), jnp.where(first, none, member)], axis=0)


def split_sum(member, picks):
    high = member.astype(BF16)
    rest = (member - high.astype(F32)).astype(BF16)
    return dot(high, picks) + dot(rest, picks)


def in_parts(member):
    lane = lax.broadcasted_iota(jnp.int32, member.shape, 1)
    member = jnp.where(lane < 32, member, 0.0)
    first = member.astype(BF16).astype(F32)
    rest = member - first
    second = rest.astype(BF16).astype(F32)
    return first + pltpu.roll(second, 32, 1) + pltpu.roll(rest - second, 64, 1)


def in_order(member, ordered):
    total = dot(ordered.astype(BF16), in_parts(member).astype(BF16))
    return total + pltpu.roll(total, 96, 1) + pltpu.roll(total, 64, 1)


def sigmoid(v):
    return 0.5 * jnp.tanh(0.5 * v) + 0.5


def shifts(marks, later):
    row = lax.broadcasted_iota(jnp.int32, (Q, Q), 0)
    column = lax.broadcasted_iota(jnp.int32, (Q, Q), 1)
    parts = []
    for j in range(1, 4):
        if later:
            parts.append(jnp.where(column == row + j, marks[j : j + 1, :], 0.0))
        else:
            parts.append(jnp.where(column == row - j, marks[3 + j : 4 + j, :], 0.0))
    return jnp.concatenate(parts, axis=0).astype(BF16)


def edge_shifts(scal, edge, later):
    row = lax.broadcasted_iota(jnp.int32, (16, 16), 0)
    column = lax.broadcasted_iota(jnp.int32, (16, 16), 1)
    at = edge + row - (16 if later else 0)
    other = edge + column - (0 if later else 16)
    same = segment_of(scal, at) == segment_of(scal, other)
    parts = [
        jnp.where(same & (other == (at + j if later else at - j)), 1.0, 0.0) for j in range(1, 4)
    ]
    return jnp.concatenate(parts, axis=0).astype(BF16)


def conv_before_act(scal, group, raw, halo, tail, taps, marks):
    current = raw[...]
    before = jnp.where(group == 0, halo[...], tail[...])
    moved = dot(shifts(marks, False), current)
    edge = dot(edge_shifts(scal, scal[4] + group * Q, False), before)
    total = current.astype(F32) * taps[3:4, :] + taps[4:5, :]
    first = jnp.zeros((16, current.shape[1]), F32)
    for j in range(1, 4):
        tap = taps[3 - j : 4 - j, :]
        total = total + moved[(j - 1) * Q : j * Q] * tap
        first = first + edge[(j - 1) * 16 : j * 16] * tap
    tail[...] = current[Q - 16 : Q]
    return jnp.concatenate([total[:16] + first, total[16:]], axis=0)


def prepare_kernel(
    subs, scal, shared, rates, halo, taps, head_rows, bc_out, bct_out, cols_out, logs_out, steps_out,
    marks_out, across_out, total_out, tail, running,
):
    @pl.when(pl.program_id(0) == 0)
    def _():
        running[...] = jnp.zeros_like(running)

    def body(k):
        group = pl.program_id(0) * subs + k
        bc, cols = group_of(bc_out, k), group_of(cols_out, k)
        bct, marks, across = lane_group_of(bct_out, k), marks_out.at[k], across_out.at[k]
        width = bc.shape[1]
        raw = group_of(rates, k)[...] + head_rows[0:1, :]
        step = jnp.maximum(raw, 0.0) + jnp.log1p(jnp.exp(-jnp.abs(raw)))
        scaled = step * (head_rows[1:2, :] * LOG2E)
        at = lax.broadcasted_iota(jnp.int32, (Q, Q), 0)
        lane = lax.broadcasted_iota(jnp.int32, (Q, Q), 1)
        summed = in_order(scaled, (at >= lane).astype(F32))
        parts = in_parts(summed)
        ones = (lane >= 96) & (lane < 99)
        group_of(logs_out, k)[...] = jnp.where(ones, 1.0, parts).astype(BF16)
        group_of(steps_out, k)[...] = in_parts(step).astype(BF16)
        turned = parts.T
        row = lax.broadcasted_iota(jnp.int32, (16, Q), 0)
        for h in range(across.shape[1] // Q):
            found = jnp.zeros((16, Q), F32)
            for m in range(3):
                found = jnp.where(row == m, -turned[32 * m + h : 32 * m + h + 1, :], found)
            across[:, h * Q : (h + 1) * Q] = found.astype(BF16)

        first = scal[4] + group * Q
        position = first + at[:, 0:1]
        segment = segment_of(scal, position)
        marked = {
            CARRIES: segment == segment_of(scal, first - 1),
            ENDING: segment == segment_of(scal, first + Q - 1),
            VALID: position < scal[0] + scal[1] + scal[2] + scal[3],
        }
        member = jnp.where(lane == SEGMENT, segment.astype(F32), 0.0)
        for mark, found in marked.items():
            member = jnp.where(lane == mark, found.astype(F32), member)
        member = jnp.where(lane < LOG, step, member)
        member = jnp.where((lane >= LOG) & (lane < MARK), pltpu.roll(summed, LOG, 1), member)
        cols[...] = jnp.where(lane >= RISE, pltpu.roll(sigmoid(raw), RISE, 1), member)
        mark = lax.broadcasted_iota(jnp.int32, (8, Q), 0)
        position = first + lax.broadcasted_iota(jnp.int32, (8, Q), 1)
        segment = segment_of(scal, position)
        other = position + jnp.where(mark < 4, -mark, jnp.where(mark < 7, mark - 3, 0))
        same = (segment_of(scal, other) == segment).astype(F32)
        marks[0:8, :] = jnp.where(mark == 0, segment.astype(F32), same)
        marks[8:40, :] = summed.T[:32]
        total_out[pl.ds(pl.multiple_of(k * 8, 8), 8), :] = running[...]
        running[...] = running[...] + summed[Q - 1 : Q, :]

        pre = conv_before_act(scal, group, group_of(shared, k), halo, tail, taps, marks)
        act = pre * sigmoid(pre)
        bc[...] = act.astype(BF16)
        bct[...] = jnp.concatenate(
            [act[:, m * STATE : (m + 1) * STATE].T for m in range(width // STATE)], axis=0
        ).astype(BF16)

    loop(subs, body)


def states_kernel(
    subs, head, scal, raw, halo, taps, spread, cols_in, logs_in, steps_in, marks_in, bct_in, total,
    act_out, slope_out, states, final, through, tail, state,
):
    channels = raw.shape[1]

    @pl.when(pl.program_id(0) == 0)
    def _():
        state[...] = jnp.zeros_like(state)

    def body(k):
        group = pl.program_id(0) * subs + k
        cols, bct = group_of(cols_in, k), lane_group_of(bct_in, k)
        pre = conv_before_act(scal, group, group_of(raw, k), halo, tail, taps, marks_in.at[k])
        gate = sigmoid(pre)
        act = (pre * gate).astype(BF16)
        group_of(act_out, k)[...] = act
        group_of(slope_out, k)[...] = (gate * (1.0 + pre * (1.0 - gate))).astype(BF16)
        summed = dot(group_of(logs_in, k)[...], spread[...])
        last = summed[Q - 1 : Q, :]
        tails = jnp.exp2(last - summed) * cols[:, ENDING : ENDING + 1]
        scaled = act.astype(F32) * dot(group_of(steps_in, k)[...], spread[...])
        fresh = dot(bct[:STATE, :], (scaled * tails).astype(BF16))
        states[k] = state[...].astype(BF16)
        state[...] = state[...] * (jnp.exp2(last) * kept(scal, group)) + fresh

    loop(subs, body)

    @pl.when(pl.program_id(0) == pl.num_programs(0) - 1)
    def _():
        final[...] = state[...]
        ended = total[(subs - 1) * 8 : subs * 8, :]
        last = dot(logs_in[subs * Q - 16 : subs * Q, :], spread[...])[15:16]
        through[...] = jnp.exp2(spread_heads(ended, head, channels) + last) * reaches(
            scal, pl.num_programs(0) * subs
        )


def total_share(scal, group, head, total, k, channels):
    here = total[pl.ds(pl.multiple_of(k * 8, 8), 8), :]
    return jnp.exp2(spread_heads(here, head, channels))[0:1] * reaches(scal, group)


def gaps_of(pair, head, cols, logs, marks, between, across_lanes):
    if not across_lanes:
        both = dot(logs[...], between[:, 2 * pair * Q : 2 * (pair + 1) * Q])
        return [both[:, :Q], both[:, Q:]]
    lane = LOG + head + 2 * pair
    return [
        jnp.broadcast_to(cols[:, lane + m : lane + m + 1], (Q, Q))
        - marks[8 + head + 2 * pair + m : 9 + head + 2 * pair + m, :]
        for m in range(2)
    ]


def scan_kernel(
    subs, head, scal, act_in, bc_in, cols_in, logs_in, steps_in, marks_in, across, spread, spread_rows,
    total, gate_in, back_in, states, start, taps, scanned_out, stats_out, between,
):
    channels = act_in.shape[1]

    @pl.when(pl.program_id(0) == 0)
    def _():
        between[...] = spread_rows[...]

    def body(k):
        group = pl.program_id(0) * subs + k
        act, bc, cols = group_of(act_in, k), group_of(bc_in, k), group_of(cols_in, k)
        gate, back, logs = group_of(gate_in, k), group_of(back_in, k), group_of(logs_in, k)
        between[96:112, :] = across[k]
        marks = marks_in.at[k]
        summed_all = dot(logs[...], spread[...])
        steps = dot(group_of(steps_in, k)[...], spread[...])
        scanned = group_of(scanned_out, k)
        b_map, c_map = bc[:, :STATE], bc[:, STATE:]
        scores = dot(c_map, b_map, NT)
        allowed = triangle(cols, marks, False)
        carries = cols[:, CARRIES : CARRIES + 1]
        share = total_share(scal, group, head, total, k, channels)
        state = (states[k].astype(F32) + share * start[...]).astype(BF16)
        outside = dot(c_map, state)
        squares = jnp.zeros((Q, 2 * HEAD), F32)
        inner = jnp.zeros((Q, 2 * HEAD), F32)
        for p in range(channels // (2 * HEAD)):
            part = slice(2 * HEAD * p, 2 * HEAD * (p + 1))
            gaps = gaps_of(p, head, cols, logs, marks, between, SCAN_LANES)
            weights = []
            for m in range(2):
                decay = jnp.exp2(gaps[m] + allowed)
                weights.append((decay * scores).astype(BF16))
            summed = summed_all[:, part]
            member = act[:, part].astype(F32)
            scaled = (member * steps[:, part]).astype(BF16)
            result = dot(jnp.concatenate(weights, axis=1), stacked_heads(scaled))
            result = result + outside[:, part] * (jnp.exp2(summed) * carries)
            scanned[:, part] = result
            mixed_heads = result + taps[6:7, part] * member
            raw = gate[:, part].astype(F32)
            gated = mixed_heads * (raw * sigmoid(raw))
            squares = squares + gated * gated
            inner = inner + back[:, part].astype(F32) * taps[5:6, part] * gated
        squares = jnp.sum(squares, axis=1, keepdims=True)
        inner = jnp.sum(inner, axis=1, keepdims=True) * cols[:, VALID : VALID + 1]
        lane = lax.broadcasted_iota(jnp.int32, (Q, Q), 1)
        both = jnp.where(lane == 0, squares, jnp.where(lane == 1, inner, 0.0))
        lane_group_of(stats_out, k)[...] = both.T[:8]

    loop(subs, body)


def gate_back_kernel(
    subs, turns, head, inner_channels, scal, scanned_in, act_in, gate_in, back_in, stats_in, bct_in, cols_in,
    logs_in, spread, total, taps, mixed_out, low_gate_out, back_heads_out, reach, sums,
):
    channels = act_in.shape[1]

    @pl.when(pl.program_id(0) == 0)
    def _():
        reach[...] = jnp.zeros_like(reach)
        sums[...] = jnp.zeros_like(sums)

    def body(k):
        group = pl.program_id(0) * subs + k
        scanned, act, gate = group_of(scanned_in, k), group_of(act_in, k), group_of(gate_in, k)
        back, cols, stats = group_of(back_in, k), group_of(cols_in, k), lane_group_of(stats_in, k)
        mixed, low_gate = group_of(mixed_out, k), group_of(low_gate_out, k)
        back_heads, bct = group_of(back_heads_out, k), lane_group_of(bct_in, k)
        row = lax.broadcasted_iota(jnp.int32, (8, Q), 0)
        inverse_row = lax.rsqrt(stats[...] / inner_channels + EPS)
        both = jnp.concatenate(
            [jnp.where(row == 0, inverse_row, stats[...]), jnp.zeros((Q - 8, Q), F32)], axis=0
        ).T
        inverse, inner = both[:, 0:1], both[:, 1:2]
        valid, carries = cols[:, VALID : VALID + 1], cols[:, CARRIES : CARRIES + 1]
        slope = inverse * inverse * inverse * inner * valid / inner_channels
        inverse_valid = inverse * valid
        summed = dot(group_of(logs_in, k)[...], spread[...])
        gradients = []
        for p in range(channels // (2 * HEAD)):
            part = slice(2 * HEAD * p, 2 * HEAD * (p + 1))
            member = act[:, part].astype(F32)
            mixed_heads = scanned[:, part] + taps[6:7, part] * member
            raw = gate[:, part].astype(F32)
            share = sigmoid(raw)
            opened = raw * share
            gated = mixed_heads * opened
            gain = taps[5:6, part]
            mixed[:, part] = (gated * inverse_valid * gain).astype(BF16)
            scaled_back = back[:, part].astype(F32) * inverse_valid
            gradient = scaled_back * gain - gated * slope
            low_gate[:, part] = (gradient * mixed_heads * (share + opened * (1.0 - share))).astype(BF16)
            low = (gradient * opened).astype(BF16)
            back_heads[:, part] = low
            wide = low.astype(F32)
            sums[0:1, part] = sums[0:1, part] + jnp.sum(scaled_back * gated, axis=0, keepdims=True)
            sums[1:2, part] = sums[1:2, part] + jnp.sum(wide * member, axis=0, keepdims=True)
            entered = jnp.exp2(summed[:, part]) * carries
            gradients.append((wide * entered).astype(BF16))
        share = total_share(scal, group, head, total, k, channels)
        reach[...] = reach[...] + share * dot(bct[STATE:, :], jnp.concatenate(gradients, axis=1))

    @pl.when(pl.program_id(0) < turns)
    def _():
        loop(subs, body)

    @pl.when(pl.program_id(0) == turns)
    def _():
        low_gate_out[...] = jnp.zeros_like(low_gate_out)


def scan_back_kernel(
    subs, head, scal, act_in, slope_in, heads_in, scanned_in, raw, halo, taps, picks, bc_in, bct_in,
    cols_in, logs_in, steps_in, marks_in, across, spread, spread_rows, total, head_rows, states, start,
    leaving, low_out, back_bc_out, low_rate_out, sums, head_out, first_rows, last_rows, behind, back_pre,
    back_state, difference, between,
):
    turn = pl.program_id(0)
    turns = pl.num_programs(0) - 1
    channels = act_in.shape[1]

    @pl.when(turn == 0)
    def _():
        back_state[...] = leaving[...]
        behind[...] = jnp.zeros_like(behind)
        between[...] = spread_rows[...]
        sums[...] = jnp.zeros_like(sums)
        head_out[...] = jnp.zeros_like(head_out)

    def body(count):
        k = subs - 1 - count
        group = (turns - 1 - turn) * subs + k
        act, slope, back_heads = group_of(act_in, k), group_of(slope_in, k), group_of(heads_in, k)
        scanned, bc, cols = group_of(scanned_in, k), group_of(bc_in, k), group_of(cols_in, k)
        bct, back_bc, logs = lane_group_of(bct_in, k), group_of(back_bc_out, k), group_of(logs_in, k)
        between[96:112, :] = across[k]
        marks = marks_in.at[k]
        summed_all = dot(logs[...], spread[...])
        steps = dot(group_of(steps_in, k)[...], spread[...])
        b_map, c_map = bc[:, :STATE], bc[:, STATE:]
        scores = dot(b_map, c_map, NT)
        allowed = triangle(cols, marks, True)
        carries, ending = cols[:, CARRIES : CARRIES + 1], cols[:, ENDING : ENDING + 1]
        share = total_share(scal, group, head, total, k, channels)
        state = states[k].astype(F32) + share * start[...]
        state_low = state.astype(BF16)
        leaving_low = back_state[...].astype(BF16)
        from_state = dot(b_map, leaving_low)
        back_scores = jnp.zeros((Q, Q), F32)
        into_state, out_of_state, passed, products = [], [], [], []
        for p in range(channels // (2 * HEAD)):
            part = slice(2 * HEAD * p, 2 * HEAD * (p + 1))
            low = back_heads[:, part]
            wide = low.astype(F32)
            member = act[:, part].astype(F32)
            step = steps[:, part]
            scaled = (member * step).astype(BF16)
            stacked = stacked_heads(low)
            back_weights = dot(stacked_heads(scaled), low, NT)
            gaps = gaps_of(p, head, cols, logs, marks, between, True)
            weights = []
            for m in range(2):
                decay = jnp.exp2(allowed - gaps[m])
                weights.append((decay * scores).astype(BF16))
                back_scores = back_scores + decay * back_weights[m * Q : (m + 1) * Q]
            summed = summed_all[:, part]
            last = summed[Q - 1 : Q, :]
            tails = jnp.exp2(last - summed) * ending
            back_scaled = dot(jnp.concatenate(weights, axis=1), stacked)
            scaled_wide = scaled.astype(F32)
            from_end = tails * from_state[:, part]
            difference[:, part] = wide * scanned[:, part] - scaled_wide * back_scaled
            passed.append((scaled_wide * from_end).astype(BF16))
            back_scaled = back_scaled + from_end
            into_state.append((scaled_wide * tails).astype(BF16))
            out_of_state.append((wide * (jnp.exp2(summed) * carries)).astype(BF16))
            products.append((back_scaled * member).astype(BF16))
            back_act = back_scaled * step + taps[6:7, part] * wide
            back_pre[:, part] = back_act * slope[:, part].astype(F32)
        into_state = jnp.concatenate(into_state, axis=1)
        out_of_state = jnp.concatenate(out_of_state, axis=1)
        back_b = dot(back_scores.astype(BF16), c_map) + dot(into_state, leaving_low, NT)
        back_c = dot(back_scores.T.astype(BF16), b_map) + dot(out_of_state, state_low, NT)
        back_bc[:, :STATE] = back_b
        back_bc[:, STATE:] = back_c

        kept_state = back_state[...] * (jnp.exp2(summed_all[Q - 1 : Q, :]) * kept(scal, group))
        back_state[...] = kept_state + dot(bct[STATE:, :], out_of_state)
        crossing = jnp.sum(kept_state * state, axis=0, keepdims=True)
        difference[Q - 1 : Q, :] = difference[Q - 1 : Q, :] + crossing

        product = dot(jnp.concatenate(products, axis=1), picks[...])
        at = lax.broadcasted_iota(jnp.int32, (Q, Q), 0)
        lane = lax.broadcasted_iota(jnp.int32, (Q, Q), 1)
        before_it = dot(jnp.concatenate(passed, axis=1), picks[...])
        back_logs = in_order(split_sum(difference[...], picks[...]), at <= lane) + dot(
            (at > lane).astype(BF16), before_it.astype(BF16)
        )
        decays = jnp.where(lane < LOG, back_logs * head_rows[1:2, :], 0.0)
        back_rate = (product + decays) * pltpu.roll(cols[...], 128 - RISE, 1)
        back_rate = jnp.where(lane < LOG, back_rate, 0.0)
        group_of(low_rate_out, k)[...] = back_rate.astype(BF16)
        head_out[0:1, :] = head_out[0:1, :] + jnp.sum(back_rate, axis=0, keepdims=True)
        head_out[1:2, :] = head_out[1:2, :] + jnp.sum(decays * cols[...], axis=0, keepdims=True)

        conv_back(scal, turn, k, group, back_pre[...], behind, group_of(raw, k), taps, marks,
                  group_of(low_out, k), sums, first_rows, last_rows, subs)

    @pl.when(turn < turns)
    def _():
        loop(subs, body)

    @pl.when(turn == turns)
    def _():
        low_rate_out[...] = jnp.zeros_like(low_rate_out)
        rows_behind(scal, behind, halo, taps, low_out, sums)


def conv_back(
    scal, turn, k, group, now, behind, raw, taps, marks, low, sums, first_rows, last_rows, subs
):
    now_low = now.astype(BF16)
    moved = dot(shifts(marks, True), now_low)
    edge = dot(edge_shifts(scal, scal[4] + (group + 1) * Q, True), behind[...])
    value = raw[...].astype(F32)
    sums[3:4, :] = sums[3:4, :] + jnp.sum(now * value, axis=0, keepdims=True)
    sums[4:5, :] = sums[4:5, :] + jnp.sum(now, axis=0, keepdims=True)
    total = now * taps[3:4, :]
    last = jnp.zeros((16, now.shape[1]), F32)
    for j in range(1, 4):
        tap = slice(3 - j, 4 - j)
        part, rest = moved[(j - 1) * Q : j * Q], edge[(j - 1) * 16 : j * 16]
        total = total + part * taps[tap, :]
        last = last + rest * taps[tap, :]
        sums[tap, :] = (
            sums[tap, :]
            + jnp.sum(part * value, axis=0, keepdims=True)
            + jnp.sum(rest * value[Q - 16 : Q], axis=0, keepdims=True)
        )
    last = total[Q - 16 :] + last
    low[...] = jnp.concatenate([total[: Q - 16], last], axis=0).astype(BF16)

    @pl.when((turn == 0) & (k == subs - 1))
    def _():
        last_rows[...] = last[8:]

    behind[...] = now_low[0:16]
    first_rows[...] = now[0:8]


def rows_behind(scal, behind, halo, taps, low_out, sums):
    edge = dot(edge_shifts(scal, scal[4], True), behind[...])
    value = halo[...].astype(F32)
    total = jnp.zeros((16, value.shape[1]), F32)
    for j in range(1, 4):
        tap, rest = slice(3 - j, 4 - j), edge[(j - 1) * 16 : j * 16]
        total = total + rest * taps[tap, :]
        sums[tap, :] = sums[tap, :] + jnp.sum(rest * value, axis=0, keepdims=True)
    low_out[...] = jnp.zeros_like(low_out)
    low_out[0:16, :] = total.astype(BF16)


def shared_back_kernel(
    subs, scal, back_bc, back_more, raw, before, halo, taps, marks_in, low_out, sums, first_rows,
    last_rows, behind, tail,
):
    turn = pl.program_id(0)
    turns = pl.num_programs(0) - 1

    @pl.when(turn == 0)
    def _():
        behind[...] = jnp.zeros_like(behind)
        sums[...] = jnp.zeros_like(sums)

    def body(count):
        k = subs - 1 - count
        group = (turns - 1 - turn) * subs + k
        start = pl.multiple_of(jnp.maximum(k * Q - 16, 0), 16)
        tail[...] = jnp.where(k == 0, before[...], raw[pl.ds(start, 16), :])
        marks = marks_in.at[k]
        pre = conv_before_act(scal, group, group_of(raw, k), halo, tail, taps, marks)
        gate = sigmoid(pre)
        back = group_of(back_bc, k)[...] + group_of(back_more, k)[...]
        now = back * (gate * (1.0 + pre * (1.0 - gate)))
        conv_back(scal, turn, k, group, now, behind, group_of(raw, k), taps, marks,
                  group_of(low_out, k), sums, first_rows, last_rows, subs)

    @pl.when(turn < turns)
    def _():
        loop(subs, body)

    @pl.when(turn == turns)
    def _():
        rows_behind(scal, behind, halo, taps, low_out, sums)


def joined(scal, low, later, last_rows, taps, rows):
    sent = []
    for back in range(3, 0, -1):
        at = scal[4] + rows - back
        extra = jnp.zeros_like(later[0])
        for j in range(back, 4):
            extra = extra + same_segment(scal, at, at + j) * taps[3 - j] * later[j - back]
        sent.append(extra)
    out = last_rows + jnp.concatenate([jnp.zeros((5, later.shape[1]), F32), jnp.stack(sent)])
    return lax.dynamic_update_slice(low, out.astype(BF16), (rows - 8, 0))


def split_blocks(member, count):
    return jnp.split(member, count, axis=0)


def chip_rows_kernel(tiles, scal, own, other, out):
    mine = pl.program_id(0) // tiles == scal[0]
    out[...] = jnp.where(mine, own[...], other[...])


def normed_rows_kernel(tiles, scal, own, other, gain, out):
    step = pl.program_id(0)

    @pl.when(step < 2 * tiles)
    def _():
        wide = jnp.where(step // tiles == scal[0], own[...], other[...]).astype(F32)
        inverse = lax.rsqrt(jnp.mean(wide * wide, axis=1, keepdims=True) + EPS)
        out[...] = (wide * inverse * gain[...]).astype(BF16)

    @pl.when(step == 2 * tiles)
    def _():
        out[...] = jnp.zeros_like(out)


def chip_rows(core, own, other, gain=None):
    rows, width = own.shape
    tile = min(512, rows)
    tiles = rows // tile

    def at(first):
        return pl.BlockSpec((tile, width), lambda i, s: (jnp.clip(i - first(s) * tiles, 0, tiles - 1), 0))

    specs = [at(lambda s: s[0]), at(lambda s: 1 - s[0])]
    args = [core.reshape(1).astype(jnp.int32), own, other]
    body, extra = partial(chip_rows_kernel, tiles), 0
    if gain is not None:
        body, extra = partial(normed_rows_kernel, tiles), 1
        specs.append(whole((1, width)))
        args.append(gain.reshape(1, width))
    return call(
        body,
        2 * tiles + extra,
        specs,
        [pl.BlockSpec((tile, width), lambda i, s: (i, 0))],
        [shape_of((2 * rows + extra * Q, width), BF16)],
        [],
        "chip_rows",
        tuple(args),
    )[0]


def many_dots_kernel(dims, finish, scal, *refs):
    count = len(dims)
    total = dot(refs[0][...], refs[count][...], dims[0])
    for k in range(1, count):
        total = total + dot(refs[k][...], refs[count + k][...], dims[k])
    finish(total, *refs[2 * count :])


def write_sum(total, out):
    out[...] = total.astype(out.dtype)


def write_output(total, tokens, other, out):
    out[...] = (tokens[...].astype(F32) + total + other[...].astype(F32)).astype(out.dtype)


def write_input_gradient(total, tokens, other, cotangent, gain, out, gain_sum):
    @pl.when(pl.program_id(0) == 0)
    def _():
        gain_sum[...] = jnp.zeros_like(gain_sum)

    residual = tokens[...].astype(F32)
    inverse = lax.rsqrt(jnp.mean(residual * residual, axis=1, keepdims=True) + EPS)
    back = total + other[...].astype(F32)
    gain_sum[0:1, :] = gain_sum[0:1, :] + jnp.sum(back * residual * inverse, axis=0, keepdims=True)
    scaled = back * gain[...]
    slope = inverse * inverse * inverse * jnp.mean(scaled * residual, axis=1, keepdims=True)
    out[...] = cotangent[...].astype(F32) + scaled * inverse - residual * slope


def call(body, grid, in_specs, out_specs, out_shape, scratch, name, args, waits=()):
    given, made = len(in_specs), len(out_specs)

    def kernel(scal, *refs):
        outs = refs[given + len(waits) :]
        outs[made][...] = jnp.ones_like(outs[made])
        body(scal, *refs[:given], *outs[:made], *outs[made + 1 :])

    return pl.pallas_call(
        kernel,
        grid_spec=pltpu.PrefetchScalarGridSpec(
            num_scalar_prefetch=1,
            grid=(grid,),
            in_specs=list(in_specs) + [pl.BlockSpec(memory_space=pl.ANY)] * len(waits),
            out_specs=list(out_specs) + [whole((8, 128))],
            scratch_shapes=scratch,
        ),
        out_shape=list(out_shape) + [shape_of((8, 128), F32)],
        compiler_params=pltpu.CompilerParams(vmem_limit_bytes=VMEM_LIMIT),
        cost_estimate=pl.CostEstimate(
            flops=int(PACE * TIMES[name]), bytes_accessed=10**5, transcendentals=0
        ),
        name=name,
    )(*args, *waits)


def whole(shape):
    return pl.BlockSpec(shape, lambda i, s: tuple(0 for _ in shape))


def after(member, *deps):
    return lax.optimization_barrier((member, *deps))[0]


class Order:
    def __init__(self):
        self.last = None

    def hold(self, member):
        return member if self.last is None else after(member, self.last)

    def holds(self, members):
        members = [self.hold(m) for m in members]
        self.last = after(self.last, *members)
        return members

    def done(self, member):
        self.last = member
        return member


def shape_of(shape, dtype):
    return jax.ShapeDtypeStruct(shape, dtype)


def many_dots(
    offset_rows, lefts, rights, dims, rows, name, finish=write_sum, extras=(), dtype=BF16, sums=(), waits=()
):
    tile = min(256, rows)
    columns = rights[0].shape[0 if dims[0] == NT else 1]
    scal = (offset_rows // tile).reshape(1).astype(jnp.int32)
    by_row = pl.BlockSpec((tile, columns), lambda i, s: (i, 0))
    return call(
        partial(many_dots_kernel, tuple(dims), finish),
        rows // tile,
        [pl.BlockSpec((tile, a.shape[1]), lambda i, s: (s[0] + i, 0)) for a in lefts]
        + [whole(b.shape) for b in rights]
        + [by_row if e.shape[0] == rows else whole(e.shape) for e in extras],
        [by_row] + [whole(shape) for shape in sums],
        [shape_of((rows, columns), dtype)] + [shape_of(shape, F32) for shape in sums],
        [],
        name,
        (scal, *lefts, *rights, *extras),
        waits,
    )


def solution(mesh):
    tensor = mesh.shape["tensor"]
    copies = mesh.shape["dp"]
    ny = tensor // 2
    nx = ny if copies % ny == 0 else 1
    nz = copies // nx

    def from_y(member, shift):
        pairs = [((((y + shift) % ny) * 2 + c), y * 2 + c) for y in range(ny) for c in range(2)]
        return lax.ppermute(member, "tensor", pairs)

    def next_y(member, step):
        pairs = [
            ((y - step) * 2 + c, y * 2 + c)
            for y in range(ny)
            for c in range(2)
            if 0 <= y - step < ny
        ]
        return lax.ppermute(member, "tensor", pairs)

    def from_core(member):
        return lax.ppermute(member, "tensor", [(t ^ 1, t) for t in range(tensor)])

    def from_x(member, shift):
        pairs = [(z * nx + (x + shift) % nx, z * nx + x) for z in range(nz) for x in range(nx)]
        return lax.ppermute(member, "dp", pairs)

    def from_z(member, shift):
        pairs = [(((z + shift) % nz) * nx + x, z * nx + x) for z in range(nz) for x in range(nx)]
        return lax.ppermute(member, "dp", pairs)

    def sum_rows(member):
        bit = 1
        while bit < copies:
            member = member + lax.ppermute(member, "dp", [(d ^ bit, d) for d in range(copies)])
            bit *= 2
        return member

    def ways_x(member, x):
        kept = lax.dynamic_index_in_dim(member, x, 1, keepdims=False)
        got = []
        for k in range(1, nx):
            sent = lax.dynamic_index_in_dim(member, (x + k) % nx, 1, keepdims=False)
            got.append(from_x(sent.astype(BF16), nx - k))
        return [kept] + got

    def ways_z(member, z, bit):
        parts = member.reshape(-1, 2, *member.shape[-2:])
        own = (z // bit) % 2
        kept = lax.dynamic_index_in_dim(parts, own, 1, keepdims=False)
        sent = lax.dynamic_index_in_dim(parts, 1 - own, 1, keepdims=False)
        pairs = [((p ^ bit) * nx + x, p * nx + x) for p in range(nz) for x in range(nx)]
        return [kept, lax.ppermute(sent.astype(BF16), "dp", pairs)]

    def summed(parts, one=None):
        total = parts[0].astype(F32)
        for part in parts[1:]:
            part = part.astype(F32)
            total = total + (part if one is None else part * one[0, 0])
        return total

    def gather_rows(member, x, z):
        member = member[None]
        bit = nz // 2
        while bit >= 1:
            pairs = [((p ^ bit) * nx + q, p * nx + q) for p in range(nz) for q in range(nx)]
            other = lax.ppermute(member, "dp", pairs)
            high = (z // bit) % 2 == 1
            member = jnp.stack([jnp.where(high, other, member), jnp.where(high, member, other)], axis=1)
            member = member.reshape(-1, *member.shape[2:])
            bit //= 2
        parts = jnp.stack([member] + [from_x(member, k) for k in range(1, nx)])
        parts = [lax.dynamic_index_in_dim(parts, (k - x) % nx, 0, False) for k in range(nx)]
        return jnp.stack(parts, axis=1).reshape(-1, member.shape[-1])

    def shards(
        tokens, lengths, norm_gain, w_gate, w_value, w_shared, w_rate, conv_value, value_bias,
        conv_shared, shared_bias, rate_bias, decay_log, skip_gain, mix_gain, w_out, cotangent,
    ):
        index = lax.axis_index("tensor")
        y, core = index // 2, index % 2
        dp = lax.axis_index("dp")
        z, x = dp // nx, dp % nx
        own_rows, width = tokens.shape
        rows = 2 * own_rows
        groups = rows // Q
        channels = w_gate.shape[1]
        heads = w_rate.shape[1]
        inner = channels * tensor
        own_start = core * own_rows
        lanes = 128
        maps = w_shared.shape[1]
        blocks = range(ny)

        halo_one = next_y(tokens[own_rows - 16 :], 1)
        tokens_other = from_core(tokens)
        halo = jnp.where(core == 1, halo_one, from_core(halo_one))
        packed = jnp.concatenate(
            [
                conv_value.T,
                value_bias[None],
                mix_gain[None],
                jnp.repeat(skip_gain, HEAD)[None],
                jnp.concatenate([rate_bias, decay_log, jnp.zeros((channels - 2 * heads,), F32)])[None],
                w_rate.T.astype(F32).reshape(-1, channels),
            ],
            axis=0,
        )
        packed = after(packed, halo_one)
        packs = [packed] + [from_y(packed, j) for j in range(1, ny)]

        order = Order()

        def own_part(weight):
            part = weight.shape[0] // nx
            return lax.dynamic_slice(weight, (x * part, 0), (part, weight.shape[1]))

        def fetched(member, dep):
            member = after(member, dep)
            return [from_y(member, j) for j in range(1, ny)]

        def from_parts(weight, pieces):
            part = weight.shape[0] // nx
            found = [weight]
            for piece in pieces:
                full = lax.dynamic_update_slice(weight, piece, (x * part, 0))
                for k in range(1, nx):
                    got = from_x(piece, k)
                    full = lax.dynamic_update_slice(full, got, ((x + k) % nx * part, 0))
                found.append(full)
            return found

        back_other = from_core(after(cotangent, tokens_other))
        value_parts = fetched(own_part(w_value), packs[-1])
        rates = [p[8:].reshape(heads, width).astype(BF16) for p in packs]
        packs = [p[:8] for p in packs]
        all_rates = jnp.concatenate(rates + [jnp.zeros((lanes - ny * heads, width), BF16)], axis=0)
        w_small = jnp.concatenate([w_shared, all_rates.T], axis=1)
        fill = jnp.zeros((lanes - ny * heads,), F32)
        head_rows = jnp.concatenate(
            [
                jnp.concatenate([p[7, :heads] for p in packs] + [fill])[None],
                jnp.concatenate([-jnp.exp(p[7, heads : 2 * heads]) for p in packs] + [fill])[None],
                jnp.zeros((6, lanes), F32),
            ],
            axis=0,
        )
        shared_taps = jnp.concatenate(
            [conv_shared.T, shared_bias[None], jnp.zeros((3, maps), F32)], axis=0
        )
        scal = jnp.concatenate([lengths[0], (y * rows).reshape(1)]).astype(jnp.int32)

        normed = chip_rows(core, tokens, tokens_other, norm_gain)
        halo = halo.astype(F32)
        halo = halo * lax.rsqrt(jnp.mean(halo * halo, axis=1, keepdims=True) + EPS) * norm_gain
        normed = order.done(lax.dynamic_update_slice(normed, halo.astype(BF16), (rows, 0)))
        step_rows = min(STEP_ROWS, rows)
        subs = step_rows // Q
        turns = rows // step_rows

        def up(columns):
            return pl.BlockSpec((step_rows, columns), lambda i, s: (i, 0))

        def stay(columns):
            return pl.BlockSpec((step_rows, columns), lambda i, s: (jnp.minimum(i, turns - 1), 0))

        def stay_lanes(depth):
            return pl.BlockSpec((depth, step_rows), lambda i, s: (0, jnp.minimum(i, turns - 1)))

        def up_lanes(depth):
            return pl.BlockSpec((depth, step_rows), lambda i, s: (0, i))

        def up_groups(*shape):
            return pl.BlockSpec((subs, *shape), lambda i, s: (i, 0, 0))

        def downward(i):
            return jnp.maximum(turns - 1 - i, 0)

        def down(columns):
            return pl.BlockSpec((step_rows, columns), lambda i, s: (downward(i), 0))

        def down_extended(columns):
            return pl.BlockSpec(
                (step_rows, columns), lambda i, s: (jnp.where(i == turns, turns, downward(i)), 0)
            )

        def down_lanes(depth):
            return pl.BlockSpec((depth, step_rows), lambda i, s: (0, downward(i)))

        def down_groups(*shape):
            return pl.BlockSpec((subs, *shape), lambda i, s: (downward(i), 0, 0))

        def down_before(columns):
            return pl.BlockSpec(
                (16, columns), lambda i, s: (jnp.maximum(downward(i) * (step_rows // 16) - 1, 0), 0)
            )

        def behind_rows(columns):
            return pl.BlockSpec((16, columns), lambda i, s: (rows // 16, 0))

        stay_total = pl.BlockSpec((subs * 8, lanes), lambda i, s: (jnp.minimum(i, turns - 1), 0))
        up_total = pl.BlockSpec((subs * 8, lanes), lambda i, s: (i, 0))
        down_total = pl.BlockSpec((subs * 8, lanes), lambda i, s: (downward(i), 0))
        extended = rows + Q

        raw_values = [order.done(dot(order.hold(normed), w_value).astype(BF16))]
        small = order.done(dot(order.hold(normed), w_small))
        value_parts = order.holds(value_parts)
        values = from_parts(w_value, value_parts)
        gate_parts = fetched(own_part(w_gate), value_parts[-1])
        raw_shared = small[:, :maps].astype(BF16)
        heads_here = ny * heads
        channel = np.arange(channels)
        column = np.arange(heads * Q)
        part_row = np.arange(lanes)[:, None]
        picks, spreads, spread_rows = [], [], []
        for j in blocks:
            mine = (j * heads + channel // HEAD)[None, :]
            picks.append(jnp.asarray((part_row == mine).T, BF16))
            spreads.append(jnp.asarray((part_row % 32 == mine) & (part_row < 96), BF16))
            mine = (j * heads + column // Q)[None, :]
            spread_rows.append(jnp.asarray((part_row % 32 == mine) & (part_row < 96), BF16))
        bc, bct, cols, logs, steps, marks, across, total, _ = call(
            partial(prepare_kernel, subs),
            turns,
            [up(maps), up(lanes), behind_rows(maps), whole((8, maps)), whole((8, lanes))],
            [
                up(maps),
                up_lanes(maps),
                up(lanes),
                up(lanes),
                up(lanes),
                up_groups(40, Q),
                up_groups(16, heads_here * Q),
                up_total,
            ],
            [
                shape_of((rows, maps), BF16),
                shape_of((maps, rows), BF16),
                shape_of((rows, lanes), F32),
                shape_of((rows, lanes), BF16),
                shape_of((rows, lanes), BF16),
                shape_of((groups, 40, Q), F32),
                shape_of((groups, 16, heads_here * Q), BF16),
                shape_of((groups * 8, lanes), F32),
            ],
            [pltpu.VMEM((16, maps), BF16), pltpu.VMEM((8, lanes), F32)],
            "prepare",
            (scal, raw_shared, small[:, maps:], raw_shared, shared_taps, head_rows),
        )
        order.done(total)

        acts, slopes, states, finals, throughs = [], [], [], [], []
        for j in blocks:
            if j == 1:
                gate_parts = order.holds(gate_parts)
                gates = from_parts(w_gate, gate_parts)
                out_parts = fetched(own_part(w_out), gate_parts[-1])
                values = [w_value] + [order.hold(v) for v in values[1:]]
            if j > 0:
                raw_values.append(order.done(dot(order.hold(normed), values[j]).astype(BF16)))
            if j == 1:
                raw_gates = [order.done(dot(order.hold(normed), w_gate).astype(BF16))]
            raw = raw_values[j]
            act, slope, state, final, through, _ = call(
                partial(states_kernel, subs, j * heads),
                turns,
                [
                    up(channels),
                    behind_rows(channels),
                    whole((8, channels)),
                    whole((lanes, channels)),
                    up(lanes),
                    up(lanes),
                    up(lanes),
                    up_groups(40, Q),
                    up_lanes(maps),
                    up_total,
                ],
                [
                    up(channels),
                    up(channels),
                    up_groups(STATE, channels),
                    whole((STATE, channels)),
                    whole((8, channels)),
                ],
                [
                    shape_of((rows, channels), BF16),
                    shape_of((rows, channels), BF16),
                    shape_of((groups, STATE, channels), BF16),
                    shape_of((STATE, channels), F32),
                    shape_of((8, channels), F32),
                ],
                [pltpu.VMEM((16, channels), BF16), pltpu.VMEM((STATE, channels), F32)],
                "states",
                (scal, order.hold(raw), raw, packs[j], spreads[j], cols, logs, steps, marks, bct, total),
                gate_parts if j == 1 else (),
            )
            order.done(final)
            if j == 0:
                back_rows = order.done(chip_rows(core, cotangent, order.hold(back_other)))
            acts.append(act)
            slopes.append(slope)
            states.append(state)
            finals.append(final)
            throughs.append(through)

        before = [(j + 1) % ny for j in blocks]
        behind = [(j - 1) % ny for j in blocks]
        starts = split_blocks(next_y(jnp.concatenate([finals[k] for k in before]), 1), ny)
        for _ in range(ny - 2):
            sent = [finals[k] + throughs[k][0:1] * starts[k] for k in before]
            starts = split_blocks(next_y(jnp.concatenate(sent), 1), ny)

        out_parts = order.holds(out_parts)
        outs = from_parts(w_out, out_parts)
        backs = [order.done(dot(order.hold(back_rows), w_out, NT).astype(BF16))]
        scans, stats = [], []
        for j in blocks:
            if j == 1:
                gates = [w_gate] + [order.hold(w) for w in gates[1:]]
                outs = [w_out] + [order.hold(w) for w in outs[1:]]
            if j > 0:
                raw_gates.append(order.done(dot(order.hold(normed), gates[j]).astype(BF16)))
                backs.append(order.done(dot(order.hold(back_rows), outs[j], NT).astype(BF16)))
            raw_gate, back = raw_gates[j], backs[j]
            scanned, stat, _ = call(
                partial(scan_kernel, subs, j * heads),
                turns,
                [
                    up(channels),
                    up(maps),
                    up(lanes),
                    up(lanes),
                    up(lanes),
                    up_groups(40, Q),
                    pl.BlockSpec((subs, 16, heads * Q), lambda i, s, j=j: (i, 0, j)),
                    whole((lanes, channels)),
                    whole((lanes, heads * Q)),
                    up_total,
                    up(channels),
                    up(channels),
                    up_groups(STATE, channels),
                    whole((STATE, channels)),
                    whole((8, channels)),
                ],
                [up(channels), up_lanes(8)],
                [shape_of((rows, channels), F32), shape_of((8, rows), F32)],
                [pltpu.VMEM((lanes, heads * Q), BF16)],
                "scan",
                (scal, order.hold(acts[j]), bc, cols, logs, steps, marks, across, spreads[j], spread_rows[j],
                 total, raw_gate, back, states[j], starts[j], packs[j]),
                out_parts if j == 0 else (),
            )
            scans.append(order.done(scanned))
            stats.append(stat)

        stat = sum(stats[1:], stats[0])
        stat = stat + from_core(stat)

        mixeds, low_gates, back_heads, reaching, gate_sums = ([None] * ny for _ in range(5))
        for j in blocks:
            mixed, low_gate, back_head, reach, sums, _ = call(
                partial(gate_back_kernel, subs, turns, j * heads, inner),
                turns + 1,
                [
                    stay(channels),
                    stay(channels),
                    stay(channels),
                    stay(channels),
                    stay_lanes(8),
                    stay_lanes(maps),
                    stay(lanes),
                    stay(lanes),
                    whole((lanes, channels)),
                    stay_total,
                    whole((8, channels)),
                ],
                [stay(channels), up(channels), stay(channels)] + [whole((STATE, channels)), whole((8, channels))],
                [shape_of((m, channels), BF16) for m in (rows, extended, rows)]
                + [shape_of((STATE, channels), F32), shape_of((8, channels), F32)],
                [],
                "gate_back",
                (scal, scans[j], order.hold(acts[j]), raw_gates[j], backs[j], stat, bct, cols, logs,
                 spreads[j], total, packs[j]),
            )
            mixeds[j], low_gates[j], back_heads[j] = mixed, low_gate, back_head
            reaching[j], gate_sums[j] = order.done(reach), sums

        leavings = [next_y(reaching[k], -1) for k in behind]
        for _ in range(ny - 2):
            leavings = [next_y(reaching[k] + throughs[k][0:1] * leavings[k], -1) for k in behind]

        def scattered(member):
            return member.reshape(nz, nx, width // copies, member.shape[1])

        out_blocks, gate_blocks = [None] * ny, [None] * ny
        for j in range(1, ny):
            out_blocks[j] = order.done(dot(order.hold(back_rows), mixeds[j], TN).astype(BF16))
            out_blocks[j] = after(out_blocks[j], leavings[-1])
        out_got = [from_y(out_blocks[j], ny - j) for j in range(1, ny)]
        for j in reversed(blocks):
            gate_blocks[j] = order.done(dot(order.hold(normed), low_gates[j], TN).astype(BF16))
        gate_ways = [ways_x(scattered(b), x) for b in gate_blocks]
        out_blocks[0] = order.done(dot(order.hold(back_rows), mixeds[0], TN).astype(BF16))
        ahead = (1 - core) * own_rows

        low_values, back_bcs, low_rates, conv_sums, head_sums_ = [None] * ny, [], [], [None] * ny, []
        value_blocks = [None] * ny
        for j in reversed(blocks):
            low, back_bc, low_rate, sums, head_out, first_rows, last_rows, scan_one = call(
                partial(scan_back_kernel, subs, j * heads),
                turns + 1,
                [
                    down(channels),
                    down(channels),
                    down(channels),
                    down(channels),
                    down(channels),
                    behind_rows(channels),
                    whole((8, channels)),
                    whole((channels, lanes)),
                    down(maps),
                    down_lanes(maps),
                    down(lanes),
                    down(lanes),
                    down(lanes),
                    down_groups(40, Q),
                    pl.BlockSpec((subs, 16, heads * Q), lambda i, s, j=j: (downward(i), 0, j)),
                    whole((lanes, channels)),
                    whole((lanes, heads * Q)),
                    down_total,
                    whole((8, lanes)),
                    down_groups(STATE, channels),
                    whole((STATE, channels)),
                    whole((STATE, channels)),
                ],
                [
                    down_extended(channels),
                    down(maps),
                    down_extended(lanes),
                    whole((8, channels)),
                    whole((8, lanes)),
                    whole((8, channels)),
                    whole((8, channels)),
                ],
                [
                    shape_of((extended, channels), BF16),
                    shape_of((rows, maps), F32),
                    shape_of((extended, lanes), BF16),
                    shape_of((8, channels), F32),
                    shape_of((8, lanes), F32),
                    shape_of((8, channels), F32),
                    shape_of((8, channels), F32),
                ],
                [
                    pltpu.VMEM((16, channels), BF16),
                    pltpu.VMEM((Q, channels), F32),
                    pltpu.VMEM((STATE, channels), F32),
                    pltpu.VMEM((Q, channels), F32),
                    pltpu.VMEM((lanes, heads * Q), BF16),
                ],
                "scan_back",
                (scal, order.hold(acts[j]), slopes[j], back_heads[j], scans[j], raw_values[j],
                 raw_values[j], packs[j], picks[j], bc, bct, cols, logs, steps, marks, across, spreads[j],
                 spread_rows[j], total, head_rows, states[j], starts[j], leavings[j]),
            )
            low_values[j] = (order.done(low), first_rows, last_rows)
            if j == ny - 1:
                gate_rows = [summed([w[0]] + order.holds(w[1:])) for w in gate_ways]
                gate_got = [from_y(gate_rows[k].astype(BF16), ny - k) for k in range(1, ny)]
                order.done(gate_rows[0])
            if j > 0:
                value_blocks[j] = order.done(dot(order.hold(normed), low, TN).astype(BF16))
            if j == 1:
                value_got = [from_y(value_blocks[k], ny - k) for k in range(1, ny)]
                out_sum = summed([out_blocks[0]] + order.holds(out_got))
                out_ways = ways_x(scattered(out_sum), x)
                order.done(out_sum)
                out_sent = order.done(
                    many_dots(
                        ahead, [order.hold(m) for m in mixeds], outs, [NN] * ny, own_rows, "out_other"
                    )[0]
                )
                out_other = from_core(out_sent)
            back_bcs.append(back_bc)
            low_rates.append(low_rate)
            conv_sums[j] = sums
            head_sums_.append(head_out)

        later = [member[1] for member in low_values]
        later = next_y(jnp.concatenate([later[k] for k in behind], axis=1), -1)
        back_bc = sum(back_bcs[1:], back_bcs[0])
        back_bc_other = from_core(back_bc)
        out_sum = summed(out_ways, scan_one)
        out_ways = ways_z(out_sum, z, 1)
        block_out, own_one = many_dots(
            own_start, mixeds, outs, [NN] * ny, own_rows, "out_own", write_output, (tokens, out_other),
            waits=(back_bc, out_sum),
        )

        low_shared, shared_sums, first_rows, last_rows, shared_one = call(
            partial(shared_back_kernel, subs),
            turns + 1,
            [
                down(maps),
                down(maps),
                down(maps),
                down_before(maps),
                behind_rows(maps),
                whole((8, maps)),
                down_groups(40, Q),
            ],
            [down_extended(maps), whole((8, maps)), whole((8, maps)), whole((8, maps))],
            [
                shape_of((extended, maps), BF16),
                shape_of((8, maps), F32),
                shape_of((8, maps), F32),
                shape_of((8, maps), F32),
            ],
            [pltpu.VMEM((16, maps), BF16), pltpu.VMEM((16, maps), BF16)],
            "shared_back",
            (scal, back_bc, back_bc_other, raw_shared, raw_shared, raw_shared, shared_taps, marks),
            (own_one,),
        )
        later_shared = next_y(first_rows, -1)
        low_rate = sum(low_rates[1:], low_rates[0])
        half = maps // 2
        part = lax.dynamic_slice(low_shared, (0, core * half), (extended, half))
        small_block = dot(normed, jnp.concatenate([part, low_rate], axis=1), TN).astype(BF16)
        small_got = [from_y(small_block, ny - j) for j in range(1, ny)]
        value_sum = summed([dot(normed, low_values[0][0], TN)] + value_got, shared_one)
        late_ways = ways_x(scattered(value_sum), x)
        gate_sum = summed([gate_rows[0]] + gate_got, shared_one)
        gate_ways = ways_z(gate_sum, z, 1)
        bit = 2
        while bit < nz:
            out_ways = ways_z(summed(out_ways, shared_one), z, bit)
            bit *= 2

        low_values = [
            joined(scal, m[0], later[:, j * channels : (j + 1) * channels], m[2], packs[j], rows)
            for j, m in enumerate(low_values)
        ]
        low_shared = joined(scal, low_shared, later_shared, last_rows, shared_taps, rows)

        lefts = [low_rate] + low_gates + low_values
        rights = [all_rates] + gates + values
        sent, other_one = many_dots(
            ahead, lefts, rights, [NN] + [NT] * (2 * ny), own_rows, "back_other",
            waits=(value_sum, small_block),
        )
        back_normed_other = from_core(sent)
        small_sum = small_block[:, :half].astype(F32)
        rate_sum = small_block[:, half : half + heads].astype(F32)
        late = summed(late_ways, other_one)
        late_ways = ways_z(late, z, 1)
        for j, got in enumerate(small_got):
            got = got.astype(F32) * other_one[0, 0]
            at = half + (ny - 1 - j) * heads
            small_sum = small_sum + got[:, :half]
            rate_sum = rate_sum + got[:, at : at + heads]
        fill = jnp.zeros((width, lanes - heads), F32)
        least = scattered(jnp.concatenate([small_sum, rate_sum, fill], axis=1))
        least_ways = ways_x(least, x)
        bit = 2
        while bit < nz:
            gate_ways = ways_z(summed(gate_ways, other_one), z, bit)
            bit *= 2
        tokens_grad, gain_sum, kept_one = many_dots(
            own_start, [low_shared] + lefts, [w_shared] + rights, [NT, NN] + [NT] * (2 * ny), own_rows,
            "back_own", write_input_gradient, (tokens, back_normed_other, cotangent, norm_gain[None]), F32,
            ((8, width),), waits=(late, least),
        )
        least_ways = ways_z(summed(least_ways, kept_one), z, 1)
        bit = 2
        while bit < nz:
            late_ways = ways_z(summed(late_ways, kept_one), z, bit)
            bit *= 2
        grad_norm = gain_sum[0]

        bit = 2
        while bit < nz:
            least_ways = ways_z(summed(least_ways), z, bit)
            bit *= 2
        grad_out = summed(out_ways, other_one).reshape(width // copies, channels).T
        grad_gate = summed(gate_ways, kept_one).reshape(width // copies, channels)
        grad_value = summed(late_ways).reshape(width // copies, channels)
        least = summed(least_ways).reshape(width // copies, half + lanes)
        grad_rate = least[:, half : half + heads]
        head_out = sum(head_sums_[1:], head_sums_[0])
        smalls = []
        for j in blocks:
            skip = gate_sums[j][1].reshape(heads, HEAD).sum(axis=1)
            own_heads = head_out[:2, j * heads : (j + 1) * heads].reshape(2 * heads)
            line = jnp.concatenate([skip, own_heads, jnp.zeros((channels - 3 * heads,), F32)])
            smalls.append(
                jnp.concatenate(
                    [conv_sums[j][:5], gate_sums[j][:1], line[None], jnp.zeros((1, channels), F32)]
                )
            )
        shared_sums = jnp.where(core == 0, shared_sums, 0.0)
        alls = jnp.concatenate([shared_sums, grad_norm.reshape(-1, maps)], axis=0)
        alls = alls.reshape(-1, lanes)
        size = smalls[0].size // lanes
        ways = [jnp.concatenate([smalls[0].reshape(-1, lanes), alls], axis=0)]
        for j in range(1, ny):
            sent = jnp.concatenate([smalls[j].reshape(-1, lanes), alls], axis=0)
            ways.append(from_y(sent, ny - j))
        own = summed([way[:size] for way in ways])
        if ny > 1:
            ways = jnp.stack([way[size:] for way in ways])
            alls = summed([lax.dynamic_index_in_dim(ways, (y - k) % ny, 0, False) for k in range(ny)])
        both = jnp.concatenate([own, alls], axis=0)

        part = least[:, :half].reshape(-1, lanes)
        each = part.shape[0]
        part = part[None]

        def step(pairs, axis):
            sent = jnp.concatenate([part.reshape(-1, lanes), both], axis=0)
            got = lax.ppermute(sent, axis, pairs)
            return got[: part.size // lanes].reshape(part.shape), got[part.size // lanes :]

        def joined_parts(high, other):
            pair = [jnp.where(high, other, part), jnp.where(high, part, other)]
            return jnp.stack(pair, axis=1).reshape(-1, each, lanes)

        bit = copies // 2
        while bit >= 1:
            got, more = step([(d ^ bit, d) for d in range(copies)], "dp")
            part, both = joined_parts((dp // bit) % 2 == 1, got), both + more
            bit //= 2
        got, more = step([(t ^ 1, t) for t in range(tensor)], "tensor")
        part, got = part.reshape(width, half), got.reshape(width, half)
        grad_shared = jnp.concatenate(
            [jnp.where(core == 0, part, got), jnp.where(core == 0, got, part)], axis=1
        )
        own = both[:size].reshape(smalls[0].shape)
        alls = (both[size:] + more[size:]).reshape(-1, maps)
        return (
            block_out,
            tokens_grad,
            alls[8:].reshape(width),
            grad_gate,
            grad_value,
            grad_shared,
            grad_rate,
            own[:4].T,
            own[4],
            alls[:4].T,
            alls[4],
            own[6, heads : 2 * heads],
            own[6, 2 * heads : 3 * heads],
            own[6, :heads],
            own[5],
            grad_out,
        )

    in_specs = (
        P(("dp", "tensor"), None),
        P("dp", None),
        P(),
        P(None, "tensor"),
        P(None, "tensor"),
        P(),
        P(None, "tensor"),
        P("tensor", None),
        P("tensor"),
        P(),
        P(),
        P("tensor"),
        P("tensor"),
        P("tensor"),
        P("tensor"),
        P("tensor", None),
        P(("dp", "tensor"), None),
    )
    out_specs = (
        P(("dp", "tensor"), None),
        P(("dp", "tensor"), None),
        P(),
        P("dp", "tensor"),
        P("dp", "tensor"),
        P(),
        P("dp", "tensor"),
        P("tensor", None),
        P("tensor"),
        P(),
        P(),
        P("tensor"),
        P("tensor"),
        P("tensor"),
        P("tensor"),
        P("tensor", "dp"),
    )
    return jax.shard_map(shards, mesh=mesh, in_specs=in_specs, out_specs=out_specs, check_vma=False)
```
